256 devices in a mesh: grp: 4 (over x), rcv: 64 (over y, z, core).
Axes of the slice: x: 4, y: 4, z: 8, core: 2. Of those that a mesh axis runs over, the one named last changes fastest.
Arguments:
- recorded: bfloat16 [2, 2, 1024, 8192], P(None, None, ('grp', 'rcv')), may hold values from -6 to 6
- surface: bfloat16 [2, 2, 8192, 8192], P(None, None, None, 'rcv'), as said below
- receiver_map: int32 [8192], replicated, may hold values from 0 to 8191, each once
- live_traces: int32 [1024, 8192], P('grp', 'rcv'), may hold values 0 or 1
Outputs:
- primaries: bfloat16 [2, 2, 1024, 8192], P(None, None, ('grp', 'rcv'))
- gains: float32 [2, 2, 8192], P(None, None, 'rcv')
The draws below stay inside these ranges and needn't reach their ends.
Inputs may be any that keep to these rules, and one draw needn't show every extreme that they name: `surface`: in each frequency slice the real part of the operator has on its diagonal a positive entry of about 0.5 to 2; its entries off the diagonal, and all entries of the imaginary part, have mean zero and deviation 0.7 / sqrt(8192).
All inputs are finite; a program needn't handle non-finite values. No bound on the sum of `live_traces` on one device may be relied on, other than what follows from the above.
Results may differ from the reference program's by a relative error of at most 0.0022.
Values may be sent and summed in bfloat16 or wider, within the bound.
No kernel may reach another device: no remote copies, remote signals or barrier semaphores. Data moves between devices by JAX's collectives and lax.ppermute only.
A program may use at most 192 MiB of HBM per device.

```python
import math
import jax
import jax.numpy as jnp
from jax import lax

NREC = 8192
FREQ = 2
SHOTS = 1024


def draw_surface(key, part):
    key = jax.random.fold_in(key, 11)
    noise_key, scale_key = jax.random.split(key)
    shape = (2, FREQ, NREC, NREC)
    noise = jax.random.normal(noise_key, shape, jnp.float32)
    noise = noise * (0.7 / math.sqrt(NREC))
    diag_scale = jnp.exp(jax.random.uniform(scale_key, (FREQ, 1, NREC), jnp.float32, math.log(0.5), math.log(2.0)))
    identity = (jnp.arange(NREC)[:, None] == jnp.arange(NREC)[None, :]).astype(jnp.float32)
    real_part = noise[0] + identity[None, :, :] * diag_scale
    return jnp.stack([real_part, noise[1]]).astype(jnp.bfloat16)


def set_ends(array, own_key, low, largest):
    shape = array.shape
    place = [jax.random.randint(jax.random.fold_in(own_key, axis), (), 0, shape[axis]) for axis in range(len(shape))]
    array = array.at[tuple(place)].set(low)
    longest = shape.index(max(shape))
    place[longest] = (place[longest] + 1) % shape[longest]
    return array.at[tuple(place)].set(largest)


def level_of(own_key, dims, cuts, smallest, largest):
    loudness = 1.0
    for axis_at, parts in cuts:
        heights = jax.random.uniform(jax.random.fold_in(jax.random.fold_in(own_key, 6), axis_at), (parts,), jnp.float32, smallest / len(cuts), largest / len(cuts))
        loudness = loudness * jnp.repeat(jnp.exp(heights), dims[axis_at] // parts).reshape((-1,) + (1,) * (len(dims) - 1 - axis_at))
    return loudness


def scatter_about(key, dims, scale, bound, shards=(), held_as=jnp.bfloat16):
    level = level_of(key, dims, shards, -0.22, 0.18) if shards else 1.0
    drawn = jax.random.normal(key, dims, jnp.float32) * scale * level
    return jnp.minimum(jnp.maximum(drawn, -bound), bound).astype(held_as)


def setup_inputs(seed: int = 0) -> dict:
    key_list = jax.random.split(jax.random.key(seed), 5)
    recorded = scatter_about(key_list[0], (2, FREQ, SHOTS, NREC), 1.0, 6.0, ((2, 256),))
    surface = draw_surface(jax.random.fold_in(key_list[4], 71), 0)
    receiver_map = jax.random.permutation(key_list[2], NREC).astype(jnp.int32)
    live_traces = set_ends((jax.random.randint(key_list[3], (SHOTS, NREC), 0, 8) < 7).astype(jnp.int32), jax.random.fold_in(key_list[3], 1), 0, 1)
    return dict(recorded=recorded, surface=surface, receiver_map=receiver_map, live_traces=live_traces)


ridge_share = 0.05


def predict(shot_real, shot_imag, surf_real, surf_imag):
    real_part = jnp.dot(shot_real, surf_real, preferred_element_type=jnp.float32) - jnp.dot(shot_imag, surf_imag, preferred_element_type=jnp.float32)
    imag_part = jnp.dot(shot_real, surf_imag, preferred_element_type=jnp.float32) + jnp.dot(shot_imag, surf_real, preferred_element_type=jnp.float32)
    return real_part, imag_part


def reference(recorded, surface, receiver_map, live_traces):
    shuffled = jnp.take(recorded, receiver_map.astype(jnp.int32), axis=3)
    weights = live_traces.astype(jnp.float32)
    total_shots = recorded.shape[2]
    term_real_list, term_imag_list, gain_real_list, gain_imag_list = [], [], [], []
    for which in range(FREQ):
        mult_real, mult_imag = predict(shuffled[0, which], shuffled[1, which], surface[0, which], surface[1, which])
        data_real = recorded[0, which].astype(jnp.float32)
        data_imag = recorded[1, which].astype(jnp.float32)
        numer_real = jnp.sum(weights * (mult_real * data_real + mult_imag * data_imag), axis=0)
        numer_imag = jnp.sum(weights * (mult_real * data_imag - mult_imag * data_real), axis=0)
        energy = jnp.sum(weights * (mult_real * mult_real + mult_imag * mult_imag), axis=0)
        denom = energy + ridge_share * total_shots
        gain_real = numer_real / denom
        gain_imag = numer_imag / denom
        term_real_list.append(weights * (gain_real * mult_real - gain_imag * mult_imag))
        term_imag_list.append(weights * (gain_real * mult_imag + gain_imag * mult_real))
        gain_real_list.append(gain_real)
        gain_imag_list.append(gain_imag)
    term = jnp.stack([jnp.stack(term_real_list), jnp.stack(term_imag_list)]).astype(jnp.bfloat16)
    term = lax.optimization_barrier(term).astype(jnp.float32)
    primaries = (recorded.astype(jnp.float32) - term).astype(jnp.bfloat16)
    gains = jnp.stack([jnp.stack(gain_real_list), jnp.stack(gain_imag_list)])
    return primaries, gains
```

```python
import jax
import jax.numpy as jnp
import numpy as np
from jax import lax
from jax.experimental import pallas as pl
from jax.experimental.pallas import tpu as pltpu
from jax.sharding import Mesh, PartitionSpec as P

ridge_share = 0.05
NY, NZ = 4, 8
CHIPS = NY * NZ
RCV = ("y", "z", "core")

LOW_Z = [(0, 0), (0, -1), (0, 1), (0, -2)]
HIGH_Z = [(0, 2), (0, -3), (0, 3), (0, -4)]
LOW_Y = [(0, 0), (-1, 0), (1, 0), (-2, 0)]


def shift(blocks, dy, dz):
    return [(a + dy, b + dz) for a, b in blocks]


SLOTS = (
    LOW_Z + shift(LOW_Z, -1, 0) + shift(LOW_Z, 1, 0) + shift(HIGH_Z, -1, 0) + shift(HIGH_Z, 1, 0)
    + shift(HIGH_Z, -2, 0) + shift(LOW_Z, 2, 0) + HIGH_Z,
    LOW_Y + shift(LOW_Y, 0, -1) + shift(LOW_Y, 0, 1) + shift(LOW_Y, 0, -2) + shift(LOW_Y, 0, 2)
    + shift(LOW_Y, 0, -3) + shift(LOW_Y, 0, 3) + shift(LOW_Y[:2], 0, -4) + shift(LOW_Y[2:], 0, 4),
)


def send(value, move0, move1):
    pairs = []
    for y in range(NY):
        for z in range(NZ):
            for core, move in enumerate((move0, move1)):
                if move is not None:
                    to = ((y + move[0]) % NY * NZ + (z + move[1]) % NZ) * 2 + core
                    pairs.append(((y * NZ + z) * 2 + core, to))
    return lax.ppermute(value, RCV, pairs)


def swap(value):
    return lax.ppermute(value, "core", [(0, 1), (1, 0)])


def flip4(value):
    rows, cols = value.shape
    return pltpu.roll(value.reshape(rows // 8, 8, cols), 4, 1).reshape(rows, cols)


def signs(rows, cols):
    row = lax.broadcasted_iota(jnp.int32, (rows, cols), 0)
    return jnp.where(row % 8 < 4, -1.0, 1.0).astype(jnp.float32)


def reorder_body(block, steps, info, rmap, own, sib, out, stage, held):
    step = pl.program_id(0)
    first = info[0] == 0

    @pl.when(step < steps)
    def _():
        for part in range(2):
            mine = own[part, 0].astype(jnp.float32)
            other = sib[part, 0].astype(jnp.float32)
            stage[pl.ds(part * 2, block, stride=8), :] = jnp.where(first, mine, other)
            stage[pl.ds(part * 2 + 1, block, stride=8), :] = jnp.where(first, other, mine)
        unroll = 16

        def rows(g, carry):
            for u in range(unroll):
                k = g * unroll + u
                to = rmap[step * block + k]
                held[pl.ds(pl.multiple_of(to * 8, 8), 8), :] = stage[pl.ds(pl.multiple_of(k * 8, 8), 8), :]
            return carry

        lax.fori_loop(0, block // unroll, rows, 0)

    @pl.when(step >= steps)
    def _():
        base = (step - steps) * block * 8
        for plane in range(4):
            got = held[pl.ds(base + plane, block, stride=8), :]
            out[:, plane * 128 : (plane + 1) * 128] = got.astype(jnp.bfloat16)


def reorder(info, receiver_map, surface, sibling):
    order, columns = surface.shape[2:]
    block = 512
    steps = order // block
    spec = pl.BlockSpec((2, 1, block, columns), lambda i, info, rmap: (0, info[0], jnp.minimum(i, steps - 1), 0))

    def body(info, rmap, own, sib, out, stage, held):
        reorder_body(block, steps, info, rmap, own, sib, out, stage, held)

    return pl.pallas_call(
        body,
        out_shape=jax.ShapeDtypeStruct((order, 4 * columns), jnp.bfloat16),
        grid_spec=pltpu.PrefetchScalarGridSpec(
            num_scalar_prefetch=2,
            grid=(2 * steps,),
            in_specs=[spec, spec],
            out_specs=pl.BlockSpec((block, 4 * columns), lambda i, info, rmap: (jnp.maximum(i - steps, 0), 0)),
            scratch_shapes=[
                pltpu.VMEM((block * 8, columns), jnp.float32),
                pltpu.VMEM((order * 8, columns), jnp.float32),
            ],
        ),
        compiler_params=pltpu.CompilerParams(vmem_limit_bytes=50 * 2**20),
        cost_estimate=pl.CostEstimate(flops=20_000_000_000, bytes_accessed=20_000_000, transcendentals=0),
        name="reorder",
    )(info, receiver_map, surface, sibling)


def weights_of(info, slot, own_w, sib_w):
    first = info[0] == 0
    chip = info[4 + slot]
    mine = own_w[chip].astype(jnp.float32)
    other = sib_w[chip].astype(jnp.float32)
    natural = jnp.concatenate([jnp.where(first, mine, other), jnp.where(first, other, mine)], axis=1)
    rolled = pltpu.roll(natural, 4, 0)
    low = lax.broadcasted_iota(jnp.int32, natural.shape, 0) < 4
    core0 = jnp.where(low, natural, rolled)
    core1 = jnp.where(low, rolled, natural)
    return jnp.where(first, core0, core1), jnp.where(first, core1, core0)


def all_weights(info, slot0, slots, own_w, sib_w):
    tiles = []
    for slot in range(slots):
        tiles.extend(weights_of(info, slot0 + slot, own_w, sib_w))
    return jnp.concatenate(tiles, axis=0)


def product(info, slot0, groups, surf, own_w, sib_w, earlier):
    order, width = surf.shape
    half = width // 2
    block = 1024
    steps = order // block
    flat = []
    for group in groups:
        flat.extend(group if isinstance(group, tuple) else (group,))
    count = len(flat)
    total_rows = 64 * len(groups)
    slots = total_rows // 16

    def join(info, refs):
        refs = list(refs)
        parts = []
        for group in groups:
            if isinstance(group, tuple):
                one, low, high = refs.pop(0), refs.pop(0), refs.pop(0)
                parts.append(jnp.where(info[0] == 0, one[...], jnp.concatenate([low[...], high[...]], axis=0)))
            else:
                parts.append(refs.pop(0)[...])
        return jnp.concatenate(parts, axis=0)

    def body(info, *refs):
        rows = refs[:count]
        data = refs[count : 2 * count]
        surf_ref, own_ref, sib_ref, before, mult, sums, total = refs[2 * count :]
        step = pl.program_id(0)

        @pl.when(step == 0)
        def _():
            total[...] = jnp.zeros_like(total)

        total[...] += jnp.dot(join(info, rows), surf_ref[...], preferred_element_type=jnp.float32)

        @pl.when(step == steps - 1)
        def _():
            sign = signs(total_rows, half)
            value = total[:, :half] + sign * flip4(total[:, half:])
            mult[...] = value
            seen = join(info, data).astype(jnp.float32)
            weight = all_weights(info, slot0, slots, own_ref, sib_ref)
            scaled = weight * value

            def add(terms):
                return jnp.sum(terms, axis=0, keepdims=True)

            numer_real = add(scaled * seen)
            numer_imag = add(scaled * (-sign * flip4(seen)))
            energy = add(scaled * value)
            row = lax.broadcasted_iota(jnp.int32, (8, half), 0)
            packed = jnp.where(row == 0, numer_real, jnp.where(row == 1, numer_imag, jnp.where(row == 2, energy, 0.0)))
            sums[...] = packed + before[...]

    row_specs = [pl.BlockSpec((a.shape[0], block), lambda i, info: (0, i)) for a in flat]
    data_specs = [pl.BlockSpec((a.shape[0], half), lambda i, info: (0, info[1])) for a in flat]
    whole = lambda a: pl.BlockSpec(a.shape, lambda i, info: (0,) * a.ndim)
    return pl.pallas_call(
        body,
        out_shape=[
            jax.ShapeDtypeStruct((total_rows, half), jnp.float32),
            jax.ShapeDtypeStruct((8, half), jnp.float32),
        ],
        grid_spec=pltpu.PrefetchScalarGridSpec(
            num_scalar_prefetch=1,
            grid=(steps,),
            in_specs=row_specs + data_specs + [
                pl.BlockSpec((block, width), lambda i, info: (i, 0)), whole(own_w), whole(sib_w), whole(earlier),
            ],
            out_specs=[
                pl.BlockSpec((total_rows, half), lambda i, info: (0, 0)),
                pl.BlockSpec((8, half), lambda i, info: (0, 0)),
            ],
            scratch_shapes=[pltpu.VMEM((total_rows, width), jnp.float32)],
        ),
        compiler_params=pltpu.CompilerParams(vmem_limit_bytes=40 * 2**20),
        cost_estimate=pl.CostEstimate(
            flops=2 * total_rows * order * width, bytes_accessed=2 * order * (width + total_rows), transcendentals=0
        ),
        name="product",
    )(info, *flat, *flat, surf, own_w, sib_w, earlier)


def subtract(info, groups, mults, own_w, sib_w, shares, total_shots):
    half = mults[0].shape[1]
    flat = []
    for group in groups:
        flat.extend(group if isinstance(group, tuple) else (group,))
    count = len(flat)

    def body(info, *refs):
        data = list(refs[:count])
        mult_refs = list(refs[count : count + len(mults)])
        own_ref, sib_ref = refs[count + len(mults) : count + len(mults) + 2]
        share_refs = refs[count + len(mults) + 2 : -3]
        out, gains, kept = refs[-3:]
        for k, share in enumerate(share_refs):
            kept[k] = share[...]
        here = info[2]
        sums = kept[here]
        for place in range(1, 4):
            sums = sums + kept[(here + 4 - place) % 4]
        denom = sums[2:3] + ridge_share * total_shots
        gain_real = sums[0:1] / denom
        gain_imag = sums[1:2] / denom
        row = lax.broadcasted_iota(jnp.int32, (8, half), 0)
        gains[...] = jnp.where(row == 0, gain_real, jnp.where(row == 1, gain_imag, 0.0))
        sign = signs(64, half)
        lines = []
        for ref in mult_refs:
            lines.extend((ref, start) for start in range(0, ref.shape[0], 64))
        for index, group in enumerate(groups):
            if isinstance(group, tuple):
                one, low, high = data.pop(0), data.pop(0), data.pop(0)
                seen = jnp.where(info[0] == 0, one[...], jnp.concatenate([low[...], high[...]], axis=0))
            else:
                seen = data.pop(0)[...]
            ref, start = lines[index]
            value = ref[start : start + 64, :]
            weight = all_weights(info, index * 4, 4, own_ref, sib_ref)
            term = weight * (gain_real * value + sign * gain_imag * flip4(value))
            term = term.astype(jnp.bfloat16).astype(jnp.float32)
            left = (seen.astype(jnp.float32) - term).astype(jnp.bfloat16)
            for slot in range(4):
                out[info[4 + index * 4 + slot]] = left[slot * 16 : (slot + 1) * 16, :]

    whole = lambda a: pl.BlockSpec(a.shape, lambda i, info: (0,) * a.ndim)
    return pl.pallas_call(
        body,
        out_shape=[
            jax.ShapeDtypeStruct((CHIPS, 16, half), jnp.bfloat16),
            jax.ShapeDtypeStruct((8, half), jnp.float32),
        ],
        grid_spec=pltpu.PrefetchScalarGridSpec(
            num_scalar_prefetch=1,
            grid=(1,),
            in_specs=[pl.BlockSpec((a.shape[0], half), lambda i, info: (0, info[1])) for a in flat]
            + [whole(a) for a in (*mults, own_w, sib_w, *shares)],
            out_specs=[
                pl.BlockSpec((CHIPS, 16, half), lambda i, info: (0, 0, 0)),
                pl.BlockSpec((8, half), lambda i, info: (0, 0)),
            ],
            scratch_shapes=[pltpu.VMEM((4, 8, half), jnp.float32)],
        ),
        compiler_params=pltpu.CompilerParams(vmem_limit_bytes=24 * 2**20),
        cost_estimate=pl.CostEstimate(flops=4_000_000, bytes_accessed=2_000_000, transcendentals=0),
        name="subtract",
    )(info, *flat, *mults, own_w, sib_w, *shares)


def per_device(recorded, surface, receiver_map, live_traces):
    x, y, z, core = (lax.axis_index(a) for a in ("grp", "y", "z", "core"))
    nrec = recorded.shape[3]
    columns = surface.shape[3]
    table = jnp.where(core == 0, jnp.asarray(np.array(SLOTS[0], np.int32)), jnp.asarray(np.array(SLOTS[1], np.int32)))
    chips = (y + table[:, 0] + NY) % NY * NZ + (z + table[:, 1] + NZ) % NZ
    zero = jnp.zeros((), jnp.int32)
    info = jnp.concatenate([jnp.stack([core, y * NZ + z, x, zero]), chips]).astype(jnp.int32)

    by_freq = jnp.transpose(recorded, (1, 0, 2, 3)).reshape(2, 8, nrec)
    mine = lax.dynamic_index_in_dim(by_freq, core, 0, keepdims=False)
    other = lax.dynamic_index_in_dim(by_freq, 1 - core, 0, keepdims=False)
    block = jnp.concatenate([mine, swap(other)], axis=0)
    sib_surface = swap(surface)
    sib_live = swap(live_traces)

    up, down, right, left = (0, 1), (0, -1), (1, 0), (-1, 0)
    p1 = send(block, up, right)
    m1 = send(block, down, left)
    p2 = send(p1, up, right)
    m2 = send(m1, down, None)
    low = jnp.concatenate([block, p1, m1, p2], axis=0)
    p5 = send(low, right, up)
    m5 = send(low, left, down)
    p3 = send(p2, up, None)
    m3 = send(m2, down, None)
    p4 = send(p3, up, None)
    high = jnp.concatenate([m2, p3, m3, p4], axis=0)
    p6 = send(jnp.where(core == 0, high, p5), right, up)
    m6 = send(jnp.where(core == 0, high, m5), left, down)
    p7 = send(p6, right, up)
    m7 = send(jnp.where(core == 0, m5, m6), left, down)
    p8 = send(p7[:32], None, up)
    m8 = send(m7[32:], None, down)

    surf = reorder(info, receiver_map, surface, sib_surface)
    shots = live_traces.shape[0]
    own_w = live_traces.reshape(CHIPS, shots // CHIPS, columns)
    sib_w = sib_live.reshape(CHIPS, shots // CHIPS, columns)
    early = [low, p5, m5, p6, m6]
    late = [p7, m7, (high, p8, m8)]
    none = jnp.zeros((8, 2 * columns), jnp.float32)
    mult1, sums1 = product(info, 0, early, surf, own_w, sib_w, none)
    mult2, sums = product(info, 4 * len(early), late, surf, own_w, sib_w, sums1)
    shares = [sums] + [lax.ppermute(sums, "grp", [(i, (i + k) % 4) for i in range(4)]) for k in (1, 2, 3)]
    total_shots = shots * lax.axis_size("grp")
    out, gains = subtract(info, early + late, [mult1, mult2], own_w, sib_w, shares, total_shots)

    back = lax.all_to_all(out, ("y", "z"), split_axis=0, concat_axis=0, tiled=True)
    mine = back[:, :8]
    other = swap(back[:, 8:])
    both = jnp.where(core == 0, jnp.stack([mine, other]), jnp.stack([other, mine]))
    both = both.reshape(2, CHIPS, 2, 4, 2 * columns)
    primaries = jnp.transpose(both, (2, 0, 3, 1, 4)).reshape(2, 2, 4, nrec)

    halves = jnp.transpose(gains[:2].reshape(2, 2, columns), (1, 0, 2))
    kept = lax.dynamic_index_in_dim(halves, core, 0, keepdims=False)
    given = swap(lax.dynamic_index_in_dim(halves, 1 - core, 0, keepdims=False))
    gains = jnp.where(core == 0, jnp.stack([kept, given], 1), jnp.stack([given, kept], 1))
    return (primaries, gains)


def solution(mesh):
    fine = Mesh(mesh.devices.reshape(4, NY, NZ, 2), ("grp", "y", "z", "core"))
    every = ("grp", "y", "z", "core")
    return jax.shard_map(
        per_device,
        mesh=fine,
        in_specs=(P(None, None, every, None), P(None, None, None, RCV), P(), P("grp", RCV)),
        out_specs=(P(None, None, every, None), P(None, None, RCV)),
        check_vma=False,
    )
```

```python
import jax
import jax.numpy as jnp
import numpy as np
from jax import lax
from jax.experimental import pallas as pl
from jax.experimental.pallas import tpu as pltpu
from jax.sharding import Mesh, PartitionSpec as P

ridge_share = 0.05
NY, NZ = 4, 8
CHIPS = NY * NZ
RCV = ("y", "z", "core")

LOW_Z = [(0, 0), (0, -1), (0, 1), (0, 2)]
HIGH_Z = [(0, -2), (0, -3), (0, 3), (0, 4)]
LOW_Y = [(0, 0), (-1, 0), (1, 0), (2, 0)]


def shift(blocks, dy, dz):
    return [(a + dy, b + dz) for a, b in blocks]


SLOTS = (
    LOW_Z + shift(LOW_Z, -1, 0) + shift(LOW_Z, 1, 0) + shift(LOW_Z, -2, 0) + HIGH_Z
    + shift(HIGH_Z, -1, 0) + shift(HIGH_Z, 1, 0) + shift(HIGH_Z[:2], -2, 0) + shift(HIGH_Z[2:], 2, 0),
    LOW_Y + shift(LOW_Y, 0, -1) + shift(LOW_Y, 0, 1) + shift(LOW_Y, 0, -2) + shift(LOW_Y, 0, 2)
    + shift(LOW_Y, 0, -3) + shift(LOW_Y, 0, 3) + shift(LOW_Y[:2], 0, -4) + shift(LOW_Y[2:], 0, 4),
)


def send(value, move0, move1):
    pairs = []
    for y in range(NY):
        for z in range(NZ):
            for core, move in enumerate((move0, move1)):
                if move is None:
                    continue
                to = ((y + move[0]) % NY * NZ + (z + move[1]) % NZ) * 2 + core
                pairs.append(((y * NZ + z) * 2 + core, to))
    return lax.ppermute(value, RCV, pairs)


def swap(value):
    return lax.ppermute(value, "core", [(0, 1), (1, 0)])


def flip4(value):
    rows, cols = value.shape
    return pltpu.roll(value.reshape(rows // 8, 8, cols), 4, 1).reshape(rows, cols)


def signs(rows, cols):
    row = lax.broadcasted_iota(jnp.int32, (rows, cols), 0)
    return jnp.where(row % 8 < 4, -1.0, 1.0).astype(jnp.float32)


def reorder_body(block, steps, info, rmap, own, sib, out, stage, held):
    step = pl.program_id(0)
    first = info[0] == 0

    @pl.when(step < steps)
    def _():
        for part in range(2):
            mine = own[part, 0].astype(jnp.float32)
            other = sib[part, 0].astype(jnp.float32)
            stage[pl.ds(part * 2, block, stride=4), :] = jnp.where(first, mine, other)
            stage[pl.ds(part * 2 + 1, block, stride=4), :] = jnp.where(first, other, mine)
        unroll = 128

        def rows(g, carry):
            start = g * unroll
            to = [rmap[step * block + start + u] for u in range(unroll)]
            for some in range(0, unroll, 32):
                lines = [stage[pl.ds(pl.multiple_of((start + some + u) * 4, 4), 4), :] for u in range(32)]
                for u in range(32):
                    held[pl.ds(pl.multiple_of(to[some + u], 4), 4), :] = lines[u]
            return carry

        lax.fori_loop(0, block // unroll, rows, 0)

    @pl.when(step >= steps)
    def _():
        base = (step - steps) * block * 4
        for plane in range(4):
            got = held[pl.ds(base + plane, block, stride=4), :]
            out[:, plane * 128 : (plane + 1) * 128] = got.astype(jnp.bfloat16)


def reorder(info, receiver_map, surface, sibling):
    order, columns = surface.shape[2:]
    block = 2048
    steps = order // block
    spec = pl.BlockSpec((2, 1, block, columns), lambda i, info, rmap: (0, info[0], jnp.minimum(i, steps - 1), 0))

    def body(info, rmap, own, sib, out, stage, held):
        reorder_body(block, steps, info, rmap, own, sib, out, stage, held)

    return pl.pallas_call(
        body,
        out_shape=jax.ShapeDtypeStruct((order, 4 * columns), jnp.bfloat16),
        grid_spec=pltpu.PrefetchScalarGridSpec(
            num_scalar_prefetch=2,
            grid=(2 * steps,),
            in_specs=[spec, spec],
            out_specs=pl.BlockSpec((block, 4 * columns), lambda i, info, rmap: (jnp.maximum(i - steps, 0), 0)),
            scratch_shapes=[
                pltpu.VMEM((block * 4, columns), jnp.float32),
                pltpu.VMEM((order * 4, columns), jnp.float32),
            ],
        ),
        compiler_params=pltpu.CompilerParams(vmem_limit_bytes=56 * 2**20),
        cost_estimate=pl.CostEstimate(flops=1_000_000, bytes_accessed=100_000, transcendentals=0),
        name="reorder",
    )(info, receiver_map, surface, sibling)


def weights_of(info, slot, own_w, sib_w):
    first = info[0] == 0
    chip = info[4 + slot]
    mine = own_w[chip].astype(jnp.float32)
    other = sib_w[chip].astype(jnp.float32)
    natural = jnp.concatenate([jnp.where(first, mine, other), jnp.where(first, other, mine)], axis=1)
    rolled = pltpu.roll(natural, 4, 0)
    low = lax.broadcasted_iota(jnp.int32, natural.shape, 0) < 4
    core0 = jnp.where(low, natural, rolled)
    core1 = jnp.where(low, rolled, natural)
    return jnp.where(first, core0, core1), jnp.where(first, core1, core0)


def all_weights(info, slot0, slots, own_w, sib_w):
    tiles = []
    for slot in range(slots):
        tiles.extend(weights_of(info, slot0 + slot, own_w, sib_w))
    return jnp.concatenate(tiles, axis=0)


def product(info, slot0, groups, surf, own_w, sib_w, earlier):
    order, width = surf.shape
    half = width // 2
    block = 2048
    steps = order // block
    flat = []
    for group in groups:
        flat.extend(group if isinstance(group, tuple) else (group,))
    count = len(flat)
    total_rows = 64 * len(groups)
    slots = total_rows // 16

    def join(refs):
        refs = list(refs)
        parts = []
        for group in groups:
            if isinstance(group, tuple):
                parts.extend((refs.pop(0)[...], refs.pop(0)[...]))
            else:
                parts.append(refs.pop(0)[...])
        return jnp.concatenate(parts, axis=0)

    def body(info, *refs):
        rows = refs[:count]
        data = refs[count : 2 * count]
        surf_ref, own_ref, sib_ref, before, mult, sums, total = refs[2 * count :]
        step = pl.program_id(0)

        @pl.when(step == 0)
        def _():
            total[...] = jnp.zeros_like(total)

        total[...] += jnp.dot(join(rows), surf_ref[...], preferred_element_type=jnp.float32)

        @pl.when(step == steps - 1)
        def _():
            sign = signs(total_rows, half)
            value = total[:, :half] + sign * flip4(total[:, half:])
            mult[...] = value
            seen = join(data).astype(jnp.float32)
            weight = all_weights(info, slot0, slots, own_ref, sib_ref)
            scaled = weight * value

            def add(terms):
                return jnp.sum(terms, axis=0, keepdims=True)

            numer_real = add(scaled * seen)
            numer_imag = add(scaled * (-sign * flip4(seen)))
            energy = add(scaled * value)
            row = lax.broadcasted_iota(jnp.int32, (8, half), 0)
            packed = jnp.where(row == 0, numer_real, jnp.where(row == 1, numer_imag, jnp.where(row == 2, energy, 0.0)))
            sums[...] = packed + before[...]

    row_specs = [pl.BlockSpec((a.shape[0], block), lambda i, info: (0, i)) for a in flat]
    data_specs = [pl.BlockSpec((a.shape[0], half), lambda i, info: (0, info[1])) for a in flat]
    whole = lambda a: pl.BlockSpec(a.shape, lambda i, info: (0,) * a.ndim)
    return pl.pallas_call(
        body,
        out_shape=[
            jax.ShapeDtypeStruct((total_rows, half), jnp.float32),
            jax.ShapeDtypeStruct((8, half), jnp.float32),
        ],
        grid_spec=pltpu.PrefetchScalarGridSpec(
            num_scalar_prefetch=1,
            grid=(steps,),
            in_specs=row_specs + data_specs + [
                pl.BlockSpec((block, width), lambda i, info: (i, 0)), whole(own_w), whole(sib_w), whole(earlier),
            ],
            out_specs=[
                pl.BlockSpec((total_rows, half), lambda i, info: (0, 0)),
                pl.BlockSpec((8, half), lambda i, info: (0, 0)),
            ],
            scratch_shapes=[pltpu.VMEM((total_rows, width), jnp.float32)],
        ),
        compiler_params=pltpu.CompilerParams(vmem_limit_bytes=40 * 2**20),
        cost_estimate=pl.CostEstimate(flops=1_000_000, bytes_accessed=100_000, transcendentals=0),
        name="product",
    )(info, *flat, *flat, surf, own_w, sib_w, earlier)


def subtract(info, groups, mults, own_w, sib_w, shares, total_shots):
    half = mults[0].shape[1]
    flat = []
    for group in groups:
        flat.extend(group if isinstance(group, tuple) else (group,))
    count = len(flat)

    def body(info, *refs):
        data = list(refs[:count])
        mult_refs = list(refs[count : count + len(mults)])
        own_ref, sib_ref = refs[count + len(mults) : count + len(mults) + 2]
        share_refs = refs[count + len(mults) + 2 : -3]
        out, gains, kept = refs[-3:]
        for k, share in enumerate(share_refs):
            kept[k] = share[...]
        here = info[2]
        sums = kept[here]
        for place in range(1, 4):
            sums = sums + kept[(here + 4 - place) % 4]
        denom = sums[2:3] + ridge_share * total_shots
        gain_real = sums[0:1] / denom
        gain_imag = sums[1:2] / denom
        row = lax.broadcasted_iota(jnp.int32, (8, half), 0)
        gains[...] = jnp.where(row == 0, gain_real, jnp.where(row == 1, gain_imag, 0.0))
        sign = signs(64, half)
        lines = []
        for ref in mult_refs:
            lines.extend((ref, start) for start in range(0, ref.shape[0], 64))
        for index, group in enumerate(groups):
            if isinstance(group, tuple):
                seen = jnp.concatenate([data.pop(0)[...], data.pop(0)[...]], axis=0)
            else:
                seen = data.pop(0)[...]
            ref, start = lines[index]
            value = ref[start : start + 64, :]
            weight = all_weights(info, index * 4, 4, own_ref, sib_ref)
            term = weight * (gain_real * value + sign * gain_imag * flip4(value))
            term = term.astype(jnp.bfloat16).astype(jnp.float32)
            left = (seen.astype(jnp.float32) - term).astype(jnp.bfloat16)
            for slot in range(4):
                out[info[4 + index * 4 + slot]] = left[slot * 16 : (slot + 1) * 16, :]

    whole = lambda a: pl.BlockSpec(a.shape, lambda i, info: (0,) * a.ndim)
    return pl.pallas_call(
        body,
        out_shape=[
            jax.ShapeDtypeStruct((CHIPS, 16, half), jnp.bfloat16),
            jax.ShapeDtypeStruct((8, half), jnp.float32),
        ],
        grid_spec=pltpu.PrefetchScalarGridSpec(
            num_scalar_prefetch=1,
            grid=(1,),
            in_specs=[pl.BlockSpec((a.shape[0], half), lambda i, info: (0, info[1])) for a in flat]
            + [whole(a) for a in (*mults, own_w, sib_w, *shares)],
            out_specs=[
                pl.BlockSpec((CHIPS, 16, half), lambda i, info: (0, 0, 0)),
                pl.BlockSpec((8, half), lambda i, info: (0, 0)),
            ],
            scratch_shapes=[pltpu.VMEM((4, 8, half), jnp.float32)],
        ),
        compiler_params=pltpu.CompilerParams(vmem_limit_bytes=24 * 2**20),
        cost_estimate=pl.CostEstimate(flops=4_000_000, bytes_accessed=2_000_000, transcendentals=0),
        name="subtract",
    )(info, *flat, *mults, own_w, sib_w, *shares)


def per_device(recorded, surface, receiver_map, live_traces):
    x, y, z, core = (lax.axis_index(a) for a in ("grp", "y", "z", "core"))
    nrec = recorded.shape[3]
    columns = surface.shape[3]
    table = jnp.where(core == 0, jnp.asarray(np.array(SLOTS[0], np.int32)), jnp.asarray(np.array(SLOTS[1], np.int32)))
    chips = (y + table[:, 0] + NY) % NY * NZ + (z + table[:, 1] + NZ) % NZ
    zero = jnp.zeros((), jnp.int32)
    info = jnp.concatenate([jnp.stack([core, y * NZ + z, x, zero]), chips]).astype(jnp.int32)

    by_freq = jnp.transpose(recorded, (1, 0, 2, 3)).reshape(2, 8, nrec)
    mine = lax.dynamic_index_in_dim(by_freq, core, 0, keepdims=False)
    other = lax.dynamic_index_in_dim(by_freq, 1 - core, 0, keepdims=False)
    block = jnp.concatenate([mine, swap(other)], axis=0)
    block, surface, live_traces = lax.optimization_barrier((block, surface, live_traces))
    sib_surface = swap(surface)
    sib_live = swap(live_traces)

    up, down, right, left = (0, 1), (0, -1), (1, 0), (-1, 0)
    p1 = send(block, up, right)
    m1 = send(block, down, left)
    m2 = send(block, (0, -2), (-2, 0))
    low = jnp.concatenate([block, p1, m1, m2], axis=0)
    low, sib_live, p1, m2, rmap4 = lax.optimization_barrier((low, sib_live, p1, m2, receiver_map * 4))

    p5 = send(low, right, up)
    m5 = send(low, left, down)
    p2 = send(p1, up, None)
    m3 = send(m2, down, None)
    surf = reorder(info, rmap4, surface, sib_surface)
    p5, m5, p2, m3, surf = lax.optimization_barrier((p5, m5, p2, m3, surf))

    p6 = send(p5, right, up)
    m6 = send(m5, left, down)
    p3 = send(p2, up, None)
    m4 = send(m3, down, None)
    high = jnp.concatenate([p2, p3, m3, m4], axis=0)
    m6 = jnp.where(core == 0, high, m6)
    p7 = send(jnp.where(core == 0, high, p6), right, up)
    m7 = send(m6, left, down)

    shots = live_traces.shape[0]
    own_w = live_traces.reshape(CHIPS, shots // CHIPS, columns)
    sib_w = sib_live.reshape(CHIPS, shots // CHIPS, columns)
    early = [low, p5, m5, p6, m6]
    none = jnp.zeros((8, 2 * columns), jnp.float32)
    mult1, sums1 = product(info, 0, early, surf, own_w, sib_w, none)
    p7, m7, sums1 = lax.optimization_barrier((p7, m7, sums1))
    p8 = send(p7[:32], right, up)
    m8 = send(m7[32:], left, down)
    late = [p7, m7, (p8, m8)]
    mult2, sums = product(info, 4 * len(early), late, surf, own_w, sib_w, sums1)
    shares = [sums] + [lax.ppermute(sums, "grp", [(i, (i + k) % 4) for i in range(4)]) for k in (1, 2, 3)]
    total_shots = shots * lax.axis_size("grp")
    out, gains = subtract(info, early + late, [mult1, mult2], own_w, sib_w, shares, total_shots)

    back = lax.all_to_all(out, ("y", "z"), split_axis=0, concat_axis=0, tiled=True)
    back, gains = lax.optimization_barrier((back, gains))
    mine = back[:, :8]
    other = swap(back[:, 8:])
    both = jnp.where(core == 0, jnp.stack([mine, other]), jnp.stack([other, mine]))
    both = both.reshape(2, CHIPS, 2, 4, 2 * columns)
    primaries = jnp.transpose(both, (2, 0, 3, 1, 4)).reshape(2, 2, 4, nrec)

    halves = jnp.transpose(gains[:2].reshape(2, 2, columns), (1, 0, 2))
    kept = lax.dynamic_index_in_dim(halves, core, 0, keepdims=False)
    given = swap(lax.dynamic_index_in_dim(halves, 1 - core, 0, keepdims=False))
    gains = jnp.where(core == 0, jnp.stack([kept, given], 1), jnp.stack([given, kept], 1))
    return (primaries, gains)


def solution(mesh):
    fine = Mesh(mesh.devices.reshape(4, NY, NZ, 2), ("grp", "y", "z", "core"))
    every = ("grp", "y", "z", "core")
    return jax.shard_map(
        per_device,
        mesh=fine,
        in_specs=(P(None, None, every, None), P(None, None, None, RCV), P(), P("grp", RCV)),
        out_specs=(P(None, None, every, None), P(None, None, RCV)),
        check_vma=False,
    )
```

```python
import jax
import jax.numpy as jnp
import numpy as np
from jax import lax
from jax.experimental import pallas as pl
from jax.experimental.pallas import tpu as pltpu
from jax.sharding import Mesh, PartitionSpec as P

ridge_share = 0.05
NY, NZ = 4, 8
CHIPS = NY * NZ
RCV = ("y", "z", "core")

LOW_Z = [(0, 0), (0, -1), (0, 1), (0, 2)]
HIGH_Z = [(0, -2), (0, -3), (0, 3), (0, 4)]
LOW_Y = [(0, 0), (-1, 0), (1, 0), (2, 0)]


def shift(blocks, dy, dz):
    return [(a + dy, b + dz) for a, b in blocks]


SLOTS = (
    LOW_Z + shift(LOW_Z, -1, 0) + shift(LOW_Z, 1, 0) + shift(LOW_Z, -2, 0) + HIGH_Z
    + shift(HIGH_Z, -1, 0) + shift(HIGH_Z, 1, 0) + shift(HIGH_Z[:2], -2, 0) + shift(HIGH_Z[2:], 2, 0),
    LOW_Y + shift(LOW_Y, 0, -1) + shift(LOW_Y, 0, 1) + shift(LOW_Y, 0, -2) + shift(LOW_Y, 0, 2)
    + shift(LOW_Y, 0, -3) + shift(LOW_Y, 0, 3) + shift(LOW_Y[:2], 0, -4) + shift(LOW_Y[2:], 0, 4),
)


def send(value, move0, move1):
    pairs = []
    for y in range(NY):
        for z in range(NZ):
            for core, move in enumerate((move0, move1)):
                if move is None:
                    continue
                to = ((y + move[0]) % NY * NZ + (z + move[1]) % NZ) * 2 + core
                pairs.append(((y * NZ + z) * 2 + core, to))
    return lax.ppermute(value, RCV, pairs)


def swap(value):
    return lax.ppermute(value, "core", [(0, 1), (1, 0)])


def flip4(value):
    rows, cols = value.shape
    return pltpu.roll(value.reshape(rows // 8, 8, cols), 4, 1).reshape(rows, cols)


def signs(rows, cols):
    row = lax.broadcasted_iota(jnp.int32, (rows, cols), 0)
    return jnp.where(row % 8 < 4, -1.0, 1.0).astype(jnp.float32)


def reorder_body(block, steps, info, rmap, own, sib, out, stage, held):
    step = pl.program_id(0)
    first = info[0] == 0

    @pl.when(step < steps)
    def _():
        for part in range(2):
            mine = own[part, 0].astype(jnp.float32)
            other = sib[part, 0].astype(jnp.float32)
            stage[pl.ds(part * 2, block, stride=4), :] = jnp.where(first, mine, other)
            stage[pl.ds(part * 2 + 1, block, stride=4), :] = jnp.where(first, other, mine)
        unroll = 128

        def rows(g, carry):
            start = g * unroll
            to = [rmap[step * block + start + u] for u in range(unroll)]
            for some in range(0, unroll, 32):
                lines = [stage[pl.ds(pl.multiple_of((start + some + u) * 4, 4), 4), :] for u in range(32)]
                for u in range(32):
                    held[pl.ds(pl.multiple_of(to[some + u], 4), 4), :] = lines[u]
            return carry

        lax.fori_loop(0, block // unroll, rows, 0)

    @pl.when(step >= steps)
    def _():
        base = (step - steps) * block * 4
        for plane in range(4):
            got = held[pl.ds(base + plane, block, stride=4), :]
            out[:, plane * 128 : (plane + 1) * 128] = got.astype(jnp.bfloat16)


def reorder(info, receiver_map, surface, sibling):
    order, columns = surface.shape[2:]
    block = 2048
    steps = order // block
    spec = pl.BlockSpec((2, 1, block, columns), lambda i, info, rmap: (0, info[0], jnp.minimum(i, steps - 1), 0))

    def body(info, rmap, own, sib, out, stage, held):
        reorder_body(block, steps, info, rmap, own, sib, out, stage, held)

    return pl.pallas_call(
        body,
        out_shape=jax.ShapeDtypeStruct((order, 4 * columns), jnp.bfloat16),
        grid_spec=pltpu.PrefetchScalarGridSpec(
            num_scalar_prefetch=2,
            grid=(2 * steps,),
            in_specs=[spec, spec],
            out_specs=pl.BlockSpec((block, 4 * columns), lambda i, info, rmap: (jnp.maximum(i - steps, 0), 0)),
            scratch_shapes=[
                pltpu.VMEM((block * 4, columns), jnp.float32),
                pltpu.VMEM((order * 4, columns), jnp.float32),
            ],
        ),
        compiler_params=pltpu.CompilerParams(vmem_limit_bytes=56 * 2**20),
        cost_estimate=pl.CostEstimate(flops=1_000_000, bytes_accessed=100_000, transcendentals=0),
        name="reorder",
    )(info, receiver_map, surface, sibling)


def weights_of(info, slot, own_w, sib_w):
    first = info[0] == 0
    chip = info[4 + slot]
    mine = own_w[chip].astype(jnp.float32)
    other = sib_w[chip].astype(jnp.float32)
    natural = jnp.concatenate([jnp.where(first, mine, other), jnp.where(first, other, mine)], axis=1)
    rolled = pltpu.roll(natural, 4, 0)
    low = lax.broadcasted_iota(jnp.int32, natural.shape, 0) < 4
    core0 = jnp.where(low, natural, rolled)
    core1 = jnp.where(low, rolled, natural)
    return jnp.where(first, core0, core1), jnp.where(first, core1, core0)


def all_weights(info, slot0, slots, own_w, sib_w):
    tiles = []
    for slot in range(slots):
        tiles.extend(weights_of(info, slot0 + slot, own_w, sib_w))
    return jnp.concatenate(tiles, axis=0)


def product(info, slot0, groups, surf, own_w, sib_w, earlier):
    order, width = surf.shape
    half = width // 2
    block = 2048
    steps = order // block
    flat = []
    for group in groups:
        flat.extend(group if isinstance(group, tuple) else (group,))
    count = len(flat)
    total_rows = 64 * len(groups)
    slots = total_rows // 16

    def join(refs):
        refs = list(refs)
        parts = []
        for group in groups:
            if isinstance(group, tuple):
                parts.extend((refs.pop(0)[...], refs.pop(0)[...]))
            else:
                parts.append(refs.pop(0)[...])
        return jnp.concatenate(parts, axis=0)

    def body(info, *refs):
        rows = refs[:count]
        data = refs[count : 2 * count]
        surf_ref, own_ref, sib_ref, before, mult, sums, total = refs[2 * count :]
        step = pl.program_id(0)

        @pl.when(step == 0)
        def _():
            total[...] = jnp.zeros_like(total)

        total[...] += jnp.dot(join(rows), surf_ref[...], preferred_element_type=jnp.float32)

        @pl.when(step == steps - 1)
        def _():
            sign = signs(total_rows, half)
            value = total[:, :half] + sign * flip4(total[:, half:])
            mult[...] = value
            seen = join(data).astype(jnp.float32)
            weight = all_weights(info, slot0, slots, own_ref, sib_ref)
            scaled = weight * value

            def add(terms):
                return jnp.sum(terms, axis=0, keepdims=True)

            numer_real = add(scaled * seen)
            numer_imag = add(scaled * (-sign * flip4(seen)))
            energy = add(scaled * value)
            row = lax.broadcasted_iota(jnp.int32, (8, half), 0)
            packed = jnp.where(row == 0, numer_real, jnp.where(row == 1, numer_imag, jnp.where(row == 2, energy, 0.0)))
            sums[...] = packed + before[...]

    row_specs = [pl.BlockSpec((a.shape[0], block), lambda i, info: (0, i)) for a in flat]
    data_specs = [pl.BlockSpec((a.shape[0], half), lambda i, info: (0, info[1])) for a in flat]
    whole = lambda a: pl.BlockSpec(a.shape, lambda i, info: (0,) * a.ndim)
    return pl.pallas_call(
        body,
        out_shape=[
            jax.ShapeDtypeStruct((total_rows, half), jnp.float32),
            jax.ShapeDtypeStruct((8, half), jnp.float32),
        ],
        grid_spec=pltpu.PrefetchScalarGridSpec(
            num_scalar_prefetch=1,
            grid=(steps,),
            in_specs=row_specs + data_specs + [
                pl.BlockSpec((block, width), lambda i, info: (i, 0)), whole(own_w), whole(sib_w), whole(earlier),
            ],
            out_specs=[
                pl.BlockSpec((total_rows, half), lambda i, info: (0, 0)),
                pl.BlockSpec((8, half), lambda i, info: (0, 0)),
            ],
            scratch_shapes=[pltpu.VMEM((total_rows, width), jnp.float32)],
        ),
        compiler_params=pltpu.CompilerParams(vmem_limit_bytes=40 * 2**20),
        cost_estimate=pl.CostEstimate(flops=1_000_000, bytes_accessed=100_000, transcendentals=0),
        name="product",
    )(info, *flat, *flat, surf, own_w, sib_w, earlier)


def subtract(info, groups, mults, own_w, sib_w, shares, total_shots):
    half = mults[0].shape[1]
    flat = []
    for group in groups:
        flat.extend(group if isinstance(group, tuple) else (group,))
    count = len(flat)

    def body(info, *refs):
        data = list(refs[:count])
        mult_refs = list(refs[count : count + len(mults)])
        own_ref, sib_ref = refs[count + len(mults) : count + len(mults) + 2]
        share_refs = refs[count + len(mults) + 2 : -3]
        out, gains, kept = refs[-3:]
        for k, share in enumerate(share_refs):
            kept[k] = share[...]
        here = info[2]
        sums = kept[here]
        for place in range(1, 4):
            sums = sums + kept[(here + 4 - place) % 4]
        denom = sums[2:3] + ridge_share * total_shots
        gain_real = sums[0:1] / denom
        gain_imag = sums[1:2] / denom
        row = lax.broadcasted_iota(jnp.int32, (8, half), 0)
        gains[...] = jnp.where(row == 0, gain_real, jnp.where(row == 1, gain_imag, 0.0))
        sign = signs(64, half)
        lines = []
        for ref in mult_refs:
            lines.extend((ref, start) for start in range(0, ref.shape[0], 64))
        for index, group in enumerate(groups):
            if isinstance(group, tuple):
                seen = jnp.concatenate([data.pop(0)[...], data.pop(0)[...]], axis=0)
            else:
                seen = data.pop(0)[...]
            ref, start = lines[index]
            value = ref[start : start + 64, :]
            weight = all_weights(info, index * 4, 4, own_ref, sib_ref)
            term = weight * (gain_real * value + sign * gain_imag * flip4(value))
            term = term.astype(jnp.bfloat16).astype(jnp.float32)
            left = (seen.astype(jnp.float32) - term).astype(jnp.bfloat16)
            for slot in range(4):
                out[info[4 + index * 4 + slot]] = left[slot * 16 : (slot + 1) * 16, :]

    whole = lambda a: pl.BlockSpec(a.shape, lambda i, info: (0,) * a.ndim)
    return pl.pallas_call(
        body,
        out_shape=[
            jax.ShapeDtypeStruct((CHIPS, 16, half), jnp.bfloat16),
            jax.ShapeDtypeStruct((8, half), jnp.float32),
        ],
        grid_spec=pltpu.PrefetchScalarGridSpec(
            num_scalar_prefetch=1,
            grid=(1,),
            in_specs=[pl.BlockSpec((a.shape[0], half), lambda i, info: (0, info[1])) for a in flat]
            + [whole(a) for a in (*mults, own_w, sib_w, *shares)],
            out_specs=[
                pl.BlockSpec((CHIPS, 16, half), lambda i, info: (0, 0, 0)),
                pl.BlockSpec((8, half), lambda i, info: (0, 0)),
            ],
            scratch_shapes=[pltpu.VMEM((4, 8, half), jnp.float32)],
        ),
        compiler_params=pltpu.CompilerParams(vmem_limit_bytes=24 * 2**20),
        cost_estimate=pl.CostEstimate(flops=4_000_000, bytes_accessed=2_000_000, transcendentals=0),
        name="subtract",
    )(info, *flat, *mults, own_w, sib_w, *shares)


def per_device(recorded, surface, receiver_map, live_traces):
    x, y, z, core = (lax.axis_index(a) for a in ("grp", "y", "z", "core"))
    nrec = recorded.shape[3]
    columns = surface.shape[3]
    table = jnp.where(core == 0, jnp.asarray(np.array(SLOTS[0], np.int32)), jnp.asarray(np.array(SLOTS[1], np.int32)))
    chips = (y + table[:, 0] + NY) % NY * NZ + (z + table[:, 1] + NZ) % NZ
    zero = jnp.zeros((), jnp.int32)
    info = jnp.concatenate([jnp.stack([core, y * NZ + z, x, zero]), chips]).astype(jnp.int32)

    by_freq = jnp.transpose(recorded, (1, 0, 2, 3)).reshape(2, 8, nrec)
    mine = lax.dynamic_index_in_dim(by_freq, core, 0, keepdims=False)
    other = lax.dynamic_index_in_dim(by_freq, 1 - core, 0, keepdims=False)
    block = jnp.concatenate([mine, swap(other)], axis=0)
    block, surface, live_traces = lax.optimization_barrier((block, surface, live_traces))
    sib_surface = swap(surface)
    sib_live = swap(live_traces)

    up, down, right, left = (0, 1), (0, -1), (1, 0), (-1, 0)
    p1 = send(block, up, right)
    m1 = send(block, down, left)
    m2 = send(block, (0, -2), (-2, 0))
    low = jnp.concatenate([block, p1, m1, m2], axis=0)
    low, info, rmap4 = lax.optimization_barrier((low, info, receiver_map * 4))

    p5 = send(low, right, up)
    m5 = send(low, left, down)
    high = jnp.concatenate([send(low[:32], (0, 2), None), send(low[32:], (0, -2), None)], axis=0)
    surf = reorder(info, rmap4, surface, sib_surface)
    p5, m5, high, surf, sib_live = lax.optimization_barrier((p5, m5, high, surf, sib_live))

    p6 = send(p5, right, up)
    m6 = send(m5, left, down)
    m6 = jnp.where(core == 0, high, m6)
    p7 = send(jnp.where(core == 0, high, p6), right, up)
    m7 = send(m6, left, down)

    shots = live_traces.shape[0]
    own_w = live_traces.reshape(CHIPS, shots // CHIPS, columns)
    sib_w = sib_live.reshape(CHIPS, shots // CHIPS, columns)
    early = [low, p5, m5, p6, m6]
    none = jnp.zeros((8, 2 * columns), jnp.float32)
    mult1, sums1 = product(info, 0, early, surf, own_w, sib_w, none)
    p7, m7, sums1 = lax.optimization_barrier((p7, m7, sums1))
    p8 = send(p7[:32], right, up)
    m8 = send(m7[32:], left, down)
    late = [p7, m7, (p8, m8)]
    mult2, sums = product(info, 4 * len(early), late, surf, own_w, sib_w, sums1)
    shares = [sums] + [lax.ppermute(sums, "grp", [(i, (i + k) % 4) for i in range(4)]) for k in (1, 2, 3)]
    total_shots = shots * lax.axis_size("grp")
    out, gains = subtract(info, early + late, [mult1, mult2], own_w, sib_w, shares, total_shots)

    back = lax.all_to_all(out, ("y", "z"), split_axis=0, concat_axis=0, tiled=True)
    back, gains = lax.optimization_barrier((back, gains))
    mine = back[:, :8]
    other = swap(back[:, 8:])
    both = jnp.where(core == 0, jnp.stack([mine, other]), jnp.stack([other, mine]))
    both = both.reshape(2, CHIPS, 2, 4, 2 * columns)
    primaries = jnp.transpose(both, (2, 0, 3, 1, 4)).reshape(2, 2, 4, nrec)

    halves = jnp.transpose(gains[:2].reshape(2, 2, columns), (1, 0, 2))
    kept = lax.dynamic_index_in_dim(halves, core, 0, keepdims=False)
    given = swap(lax.dynamic_index_in_dim(halves, 1 - core, 0, keepdims=False))
    gains = jnp.where(core == 0, jnp.stack([kept, given], 1), jnp.stack([given, kept], 1))
    return (primaries, gains)


def solution(mesh):
    fine = Mesh(mesh.devices.reshape(4, NY, NZ, 2), ("grp", "y", "z", "core"))
    every = ("grp", "y", "z", "core")
    return jax.shard_map(
        per_device,
        mesh=fine,
        in_specs=(P(None, None, every, None), P(None, None, None, RCV), P(), P("grp", RCV)),
        out_specs=(P(None, None, every, None), P(None, None, RCV)),
        check_vma=False,
    )
```

```python
import jax
import jax.numpy as jnp
import numpy as np
from jax import lax
from jax.experimental import pallas as pl
from jax.experimental.pallas import tpu as pltpu
from jax.sharding import Mesh, PartitionSpec as P

ridge_share = 0.05
NY, NZ = 4, 8
CHIPS = NY * NZ
RCV = ("y", "z", "core")

LOW_Z = [(0, 0), (0, -1), (0, 1), (0, 2)]
HIGH_Z = [(0, -2), (0, -3), (0, 3), (0, 4)]
LOW_Y = [(0, 0), (-1, 0), (1, 0), (2, 0)]


def shift(blocks, dy, dz):
    return [(a + dy, b + dz) for a, b in blocks]


SLOTS = (
    LOW_Z + shift(LOW_Z, -1, 0) + shift(LOW_Z, 1, 0) + shift(LOW_Z, -2, 0) + HIGH_Z
    + shift(HIGH_Z, -1, 0) + shift(HIGH_Z, 1, 0) + shift(HIGH_Z[:2], -2, 0) + shift(HIGH_Z[2:], 2, 0),
    LOW_Y + shift(LOW_Y, 0, -1) + shift(LOW_Y, 0, 1) + shift(LOW_Y, 0, -2) + shift(LOW_Y, 0, 2)
    + shift(LOW_Y, 0, -3) + shift(LOW_Y, 0, 3) + shift(LOW_Y[:2], 0, -4) + shift(LOW_Y[2:], 0, 4),
)


def send(value, move0, move1):
    pairs = []
    for y in range(NY):
        for z in range(NZ):
            for core, move in enumerate((move0, move1)):
                if move is None:
                    continue
                to = ((y + move[0]) % NY * NZ + (z + move[1]) % NZ) * 2 + core
                pairs.append(((y * NZ + z) * 2 + core, to))
    return lax.ppermute(value, RCV, pairs)


def swap(value):
    return lax.ppermute(value, "core", [(0, 1), (1, 0)])


def flip4(value):
    rows, cols = value.shape
    return pltpu.roll(value.reshape(rows // 8, 8, cols), 4, 1).reshape(rows, cols)


def signs(rows, cols):
    row = lax.broadcasted_iota(jnp.int32, (rows, cols), 0)
    return jnp.where(row % 8 < 4, -1.0, 1.0).astype(jnp.float32)


def reorder_body(block, steps, info, rmap, own, sib, out, stage, held):
    step = pl.program_id(0)
    first = info[0] == 0

    @pl.when(step < steps)
    def _():
        for part in range(2):
            mine = own[part, 0].astype(jnp.float32)
            other = sib[part, 0].astype(jnp.float32)
            stage[pl.ds(part * 2, block, stride=4), :] = jnp.where(first, mine, other)
            stage[pl.ds(part * 2 + 1, block, stride=4), :] = jnp.where(first, other, mine)
        unroll = 128

        def rows(g, carry):
            start = g * unroll
            to = [rmap[step * block + start + u] for u in range(unroll)]
            for some in range(0, unroll, 32):
                lines = [stage[pl.ds(pl.multiple_of((start + some + u) * 4, 4), 4), :] for u in range(32)]
                for u in range(32):
                    held[pl.ds(pl.multiple_of(to[some + u], 4), 4), :] = lines[u]
            return carry

        lax.fori_loop(0, block // unroll, rows, 0)

    @pl.when(step >= steps)
    def _():
        base = (step - steps) * block * 4
        for plane in range(4):
            got = held[pl.ds(base + plane, block, stride=4), :]
            out[:, plane * 128 : (plane + 1) * 128] = got.astype(jnp.bfloat16)


def reorder(info, receiver_map, surface, sibling):
    order, columns = surface.shape[2:]
    block = 2048
    steps = order // block
    spec = pl.BlockSpec((2, 1, block, columns), lambda i, info, rmap: (0, info[0], jnp.minimum(i, steps - 1), 0))

    def body(info, rmap, own, sib, out, stage, held):
        reorder_body(block, steps, info, rmap, own, sib, out, stage, held)

    return pl.pallas_call(
        body,
        out_shape=jax.ShapeDtypeStruct((order, 4 * columns), jnp.bfloat16),
        grid_spec=pltpu.PrefetchScalarGridSpec(
            num_scalar_prefetch=2,
            grid=(2 * steps,),
            in_specs=[spec, spec],
            out_specs=pl.BlockSpec((block, 4 * columns), lambda i, info, rmap: (jnp.maximum(i - steps, 0), 0)),
            scratch_shapes=[
                pltpu.VMEM((block * 4, columns), jnp.float32),
                pltpu.VMEM((order * 4, columns), jnp.float32),
            ],
        ),
        compiler_params=pltpu.CompilerParams(vmem_limit_bytes=56 * 2**20),
        cost_estimate=pl.CostEstimate(flops=1_000_000, bytes_accessed=100_000, transcendentals=0),
        name="reorder",
    )(info, receiver_map, surface, sibling)


def weights_of(info, slot, own_w, sib_w):
    first = info[0] == 0
    chip = info[4 + slot]
    mine = own_w[chip].astype(jnp.float32)
    other = sib_w[chip].astype(jnp.float32)
    natural = jnp.concatenate([jnp.where(first, mine, other), jnp.where(first, other, mine)], axis=1)
    rolled = pltpu.roll(natural, 4, 0)
    low = lax.broadcasted_iota(jnp.int32, natural.shape, 0) < 4
    core0 = jnp.where(low, natural, rolled)
    core1 = jnp.where(low, rolled, natural)
    return jnp.where(first, core0, core1), jnp.where(first, core1, core0)


def all_weights(info, slot0, slots, own_w, sib_w):
    tiles = []
    for slot in range(slots):
        tiles.extend(weights_of(info, slot0 + slot, own_w, sib_w))
    return jnp.concatenate(tiles, axis=0)


def product(info, slot0, groups, surf, own_w, sib_w, earlier):
    order, width = surf.shape
    half = width // 2
    block = 2048
    steps = order // block
    flat = []
    for group in groups:
        flat.extend(group if isinstance(group, tuple) else (group,))
    count = len(flat)
    total_rows = 64 * len(groups)
    slots = total_rows // 16

    def join(refs):
        refs = list(refs)
        parts = []
        for group in groups:
            if isinstance(group, tuple):
                parts.extend((refs.pop(0)[...], refs.pop(0)[...]))
            else:
                parts.append(refs.pop(0)[...])
        return jnp.concatenate(parts, axis=0)

    def body(info, *refs):
        rows = refs[:count]
        data = refs[count : 2 * count]
        surf_ref, own_ref, sib_ref, before, mult, sums, total = refs[2 * count :]
        step = pl.program_id(0)

        @pl.when(step == 0)
        def _():
            total[...] = jnp.zeros_like(total)

        total[...] += jnp.dot(join(rows), surf_ref[...], preferred_element_type=jnp.float32)

        @pl.when(step == steps - 1)
        def _():
            sign = signs(total_rows, half)
            value = total[:, :half] + sign * flip4(total[:, half:])
            mult[...] = value
            seen = join(data).astype(jnp.float32)
            weight = all_weights(info, slot0, slots, own_ref, sib_ref)
            scaled = weight * value

            def add(terms):
                return jnp.sum(terms, axis=0, keepdims=True)

            numer_real = add(scaled * seen)
            numer_imag = add(scaled * (-sign * flip4(seen)))
            energy = add(scaled * value)
            row = lax.broadcasted_iota(jnp.int32, (8, half), 0)
            packed = jnp.where(row == 0, numer_real, jnp.where(row == 1, numer_imag, jnp.where(row == 2, energy, 0.0)))
            sums[...] = packed + before[...]

    row_specs = [pl.BlockSpec((a.shape[0], block), lambda i, info: (0, i)) for a in flat]
    data_specs = [pl.BlockSpec((a.shape[0], half), lambda i, info: (0, info[1])) for a in flat]
    whole = lambda a: pl.BlockSpec(a.shape, lambda i, info: (0,) * a.ndim)
    return pl.pallas_call(
        body,
        out_shape=[
            jax.ShapeDtypeStruct((total_rows, half), jnp.float32),
            jax.ShapeDtypeStruct((8, half), jnp.float32),
        ],
        grid_spec=pltpu.PrefetchScalarGridSpec(
            num_scalar_prefetch=1,
            grid=(steps,),
            in_specs=row_specs + data_specs + [
                pl.BlockSpec((block, width), lambda i, info: (i, 0)), whole(own_w), whole(sib_w), whole(earlier),
            ],
            out_specs=[
                pl.BlockSpec((total_rows, half), lambda i, info: (0, 0)),
                pl.BlockSpec((8, half), lambda i, info: (0, 0)),
            ],
            scratch_shapes=[pltpu.VMEM((total_rows, width), jnp.float32)],
        ),
        compiler_params=pltpu.CompilerParams(vmem_limit_bytes=40 * 2**20),
        cost_estimate=pl.CostEstimate(flops=1_000_000, bytes_accessed=100_000, transcendentals=0),
        name="product",
    )(info, *flat, *flat, surf, own_w, sib_w, earlier)


def subtract(info, groups, mults, own_w, sib_w, shares, total_shots):
    half = mults[0].shape[1]
    flat = []
    for group in groups:
        flat.extend(group if isinstance(group, tuple) else (group,))
    count = len(flat)

    def body(info, *refs):
        data = list(refs[:count])
        mult_refs = list(refs[count : count + len(mults)])
        own_ref, sib_ref = refs[count + len(mults) : count + len(mults) + 2]
        share_refs = refs[count + len(mults) + 2 : -3]
        out, gains, kept = refs[-3:]
        for k, share in enumerate(share_refs):
            kept[k] = share[...]
        here = info[2]
        sums = kept[here]
        for place in range(1, 4):
            sums = sums + kept[(here + 4 - place) % 4]
        denom = sums[2:3] + ridge_share * total_shots
        gain_real = sums[0:1] / denom
        gain_imag = sums[1:2] / denom
        row = lax.broadcasted_iota(jnp.int32, (8, half), 0)
        gains[...] = jnp.where(row == 0, gain_real, jnp.where(row == 1, gain_imag, 0.0))
        sign = signs(64, half)
        lines = []
        for ref in mult_refs:
            lines.extend((ref, start) for start in range(0, ref.shape[0], 64))
        for index, group in enumerate(groups):
            if isinstance(group, tuple):
                seen = jnp.concatenate([data.pop(0)[...], data.pop(0)[...]], axis=0)
            else:
                seen = data.pop(0)[...]
            ref, start = lines[index]
            value = ref[start : start + 64, :]
            weight = all_weights(info, index * 4, 4, own_ref, sib_ref)
            term = weight * (gain_real * value + sign * gain_imag * flip4(value))
            term = term.astype(jnp.bfloat16).astype(jnp.float32)
            left = (seen.astype(jnp.float32) - term).astype(jnp.bfloat16)
            for slot in range(4):
                out[info[4 + index * 4 + slot]] = left[slot * 16 : (slot + 1) * 16, :]

    whole = lambda a: pl.BlockSpec(a.shape, lambda i, info: (0,) * a.ndim)
    return pl.pallas_call(
        body,
        out_shape=[
            jax.ShapeDtypeStruct((CHIPS, 16, half), jnp.bfloat16),
            jax.ShapeDtypeStruct((8, half), jnp.float32),
        ],
        grid_spec=pltpu.PrefetchScalarGridSpec(
            num_scalar_prefetch=1,
            grid=(1,),
            in_specs=[pl.BlockSpec((a.shape[0], half), lambda i, info: (0, info[1])) for a in flat]
            + [whole(a) for a in (*mults, own_w, sib_w, *shares)],
            out_specs=[
                pl.BlockSpec((CHIPS, 16, half), lambda i, info: (0, 0, 0)),
                pl.BlockSpec((8, half), lambda i, info: (0, 0)),
            ],
            scratch_shapes=[pltpu.VMEM((4, 8, half), jnp.float32)],
        ),
        compiler_params=pltpu.CompilerParams(vmem_limit_bytes=24 * 2**20),
        cost_estimate=pl.CostEstimate(flops=4_000_000, bytes_accessed=2_000_000, transcendentals=0),
        name="subtract",
    )(info, *flat, *mults, own_w, sib_w, *shares)


def per_device(recorded, surface, receiver_map, live_traces):
    x, y, z, core = (lax.axis_index(a) for a in ("grp", "y", "z", "core"))
    nrec = recorded.shape[3]
    columns = surface.shape[3]
    table = jnp.where(core == 0, jnp.asarray(np.array(SLOTS[0], np.int32)), jnp.asarray(np.array(SLOTS[1], np.int32)))
    chips = (y + table[:, 0] + NY) % NY * NZ + (z + table[:, 1] + NZ) % NZ
    zero = jnp.zeros((), jnp.int32)
    info = jnp.concatenate([jnp.stack([core, y * NZ + z, x, zero]), chips]).astype(jnp.int32)

    by_freq = jnp.transpose(recorded, (1, 0, 2, 3)).reshape(2, 8, nrec)
    mine = lax.dynamic_index_in_dim(by_freq, core, 0, keepdims=False)
    other = lax.dynamic_index_in_dim(by_freq, 1 - core, 0, keepdims=False)
    block = jnp.concatenate([mine, swap(other)], axis=0)
    block, surface, live_traces = lax.optimization_barrier((block, surface, live_traces))
    sib_surface = swap(surface)
    sib_live = swap(live_traces)

    up, down, right, left = (0, 1), (0, -1), (1, 0), (-1, 0)
    p1 = send(block, up, right)
    m1 = send(block, down, left)
    m2 = send(block, (0, -2), (-2, 0))
    low = jnp.concatenate([block, p1, m1, m2], axis=0)
    low, info, rmap4, sib_live = lax.optimization_barrier((low, info, receiver_map * 4, sib_live))

    p5 = send(low, right, up)
    m5 = send(low, left, down)
    hp = send(low[:32], (0, 2), None)
    hm = send(low[32:], (0, -2), None)
    surf = reorder(info, rmap4, surface, sib_surface)
    p5, m5, hp, hm, surf = lax.optimization_barrier((p5, m5, hp, hm, surf))
    high = jnp.concatenate([hp, hm], axis=0)

    p6 = send(p5, right, up)
    m6 = send(m5, left, down)
    m6 = jnp.where(core == 0, high, m6)
    p7 = send(jnp.where(core == 0, high, p6), right, up)
    m7 = send(m6, left, down)

    shots = live_traces.shape[0]
    own_w = live_traces.reshape(CHIPS, shots // CHIPS, columns)
    sib_w = sib_live.reshape(CHIPS, shots // CHIPS, columns)
    early = [low, p5, m5, p6, m6]
    none = jnp.zeros((8, 2 * columns), jnp.float32)
    mult1, sums1 = product(info, 0, early, surf, own_w, sib_w, none)
    p7, m7, sums1 = lax.optimization_barrier((p7, m7, sums1))
    p8 = send(p7[:32], right, up)
    m8 = send(m7[32:], left, down)
    late = [p7, m7, (p8, m8)]
    mult2, sums = product(info, 4 * len(early), late, surf, own_w, sib_w, sums1)
    shares = [sums] + [lax.ppermute(sums, "grp", [(i, (i + k) % 4) for i in range(4)]) for k in (1, 2, 3)]
    total_shots = shots * lax.axis_size("grp")
    out, gains = subtract(info, early + late, [mult1, mult2], own_w, sib_w, shares, total_shots)

    back = lax.all_to_all(out, ("y", "z"), split_axis=0, concat_axis=0, tiled=True)
    back, gains = lax.optimization_barrier((back, gains))
    mine = back[:, :8]
    other = swap(back[:, 8:])
    both = jnp.where(core == 0, jnp.stack([mine, other]), jnp.stack([other, mine]))
    both = both.reshape(2, CHIPS, 2, 4, 2 * columns)
    primaries = jnp.transpose(both, (2, 0, 3, 1, 4)).reshape(2, 2, 4, nrec)

    halves = jnp.transpose(gains[:2].reshape(2, 2, columns), (1, 0, 2))
    kept = lax.dynamic_index_in_dim(halves, core, 0, keepdims=False)
    given = swap(lax.dynamic_index_in_dim(halves, 1 - core, 0, keepdims=False))
    gains = jnp.where(core == 0, jnp.stack([kept, given], 1), jnp.stack([given, kept], 1))
    return (primaries, gains)


def solution(mesh):
    fine = Mesh(mesh.devices.reshape(4, NY, NZ, 2), ("grp", "y", "z", "core"))
    every = ("grp", "y", "z", "core")
    return jax.shard_map(
        per_device,
        mesh=fine,
        in_specs=(P(None, None, every, None), P(None, None, None, RCV), P(), P("grp", RCV)),
        out_specs=(P(None, None, every, None), P(None, None, RCV)),
        check_vma=False,
    )
```

```python
import jax
import jax.numpy as jnp
import numpy as np
from jax import lax
from jax.experimental import pallas as pl
from jax.experimental.pallas import tpu as pltpu
from jax.sharding import Mesh, PartitionSpec as P

ridge_share = 0.05
NY, NZ = 4, 8
CHIPS = NY * NZ
RCV = ("y", "z", "core")

LOW_Z = [(0, 0), (0, -1), (0, 1), (0, 2)]
HIGH_Z = [(0, -2), (0, -3), (0, 3), (0, 4)]
LOW_Y = [(0, 0), (-1, 0), (1, 0), (2, 0)]


def shift(blocks, dy, dz):
    return [(a + dy, b + dz) for a, b in blocks]


SLOTS = (
    LOW_Z + shift(LOW_Z, -1, 0) + shift(LOW_Z, 1, 0) + shift(LOW_Z, -2, 0) + HIGH_Z
    + shift(HIGH_Z, -1, 0) + shift(HIGH_Z, 1, 0) + shift(HIGH_Z[:2], -2, 0) + shift(HIGH_Z[2:], 2, 0),
    LOW_Y + shift(LOW_Y, 0, -1) + shift(LOW_Y, 0, 1) + shift(LOW_Y, 0, -2) + shift(LOW_Y, 0, 2)
    + shift(LOW_Y, 0, -3) + shift(LOW_Y, 0, 3) + shift(LOW_Y[:2], 0, -4) + shift(LOW_Y[2:], 0, 4),
)


def send(value, move0, move1):
    pairs = []
    for y in range(NY):
        for z in range(NZ):
            for core, move in enumerate((move0, move1)):
                if move is None:
                    continue
                to = ((y + move[0]) % NY * NZ + (z + move[1]) % NZ) * 2 + core
                pairs.append(((y * NZ + z) * 2 + core, to))
    return lax.ppermute(value, RCV, pairs)


def swap(value):
    return lax.ppermute(value, "core", [(0, 1), (1, 0)])


def flip4(value):
    rows, cols = value.shape
    return pltpu.roll(value.reshape(rows // 8, 8, cols), 4, 1).reshape(rows, cols)


def signs(rows, cols):
    row = lax.broadcasted_iota(jnp.int32, (rows, cols), 0)
    return jnp.where(row % 8 < 4, -1.0, 1.0).astype(jnp.float32)


def split_freqs(recorded):
    parts, freqs, shots, nrec = recorded.shape

    def body(rec, mine, other):
        first = lax.axis_index("core") == 0
        rows = [
            jnp.concatenate([rec[part, freq].astype(jnp.float32) for part in range(parts)], axis=0)
            for freq in range(freqs)
        ]
        mine[...] = jnp.where(first, rows[0], rows[1]).astype(jnp.bfloat16)
        other[...] = jnp.where(first, rows[1], rows[0]).astype(jnp.bfloat16)

    return pl.pallas_call(
        body,
        out_shape=[jax.ShapeDtypeStruct((parts * shots, nrec), jnp.bfloat16)] * 2,
        in_specs=[pl.BlockSpec(memory_space=pltpu.VMEM)],
        out_specs=[pl.BlockSpec(memory_space=pltpu.VMEM)] * 2,
        compiler_params=pltpu.CompilerParams(vmem_limit_bytes=16 * 2**20),
        name="split_freqs",
    )(recorded)


def assemble(back, got, gains, got_gains):
    chips, _, width = back.shape
    half = width // 2

    def body(back, got, gains, got_gains, out, out_gains):
        core = lax.axis_index("core")
        first = core == 0
        for chip in range(chips):
            mine = back[chip].astype(jnp.float32)[:8]
            other = got[chip].astype(jnp.float32)[8:]
            for freq, rows in enumerate((jnp.where(first, mine, other), jnp.where(first, other, mine))):
                for part in range(2):
                    out[part, freq, :, chip * width : (chip + 1) * width] = rows[part * 4 : part * 4 + 4].astype(
                        jnp.bfloat16
                    )
        mine = jnp.where(first, gains[:, :half], gains[:, half:])
        other = jnp.where(first, got_gains[:, :half], got_gains[:, half:])
        for freq, rows in enumerate((jnp.where(first, mine, other), jnp.where(first, other, mine))):
            for part in range(2):
                out_gains[part, freq : freq + 1, :] = rows[part : part + 1]

    return pl.pallas_call(
        body,
        out_shape=[
            jax.ShapeDtypeStruct((2, 2, 4, chips * width), jnp.bfloat16),
            jax.ShapeDtypeStruct((2, 2, half), jnp.float32),
        ],
        in_specs=[pl.BlockSpec(memory_space=pltpu.VMEM)] * 4,
        out_specs=[pl.BlockSpec(memory_space=pltpu.VMEM)] * 2,
        compiler_params=pltpu.CompilerParams(vmem_limit_bytes=16 * 2**20),
        name="assemble",
    )(back, got, gains, got_gains)


def reorder_body(block, steps, info, rmap, own, sib, out, stage, held):
    step = pl.program_id(0)
    first = info[0] == 0

    @pl.when(step < steps)
    def _():
        for part in range(2):
            mine = own[part, 0].astype(jnp.float32)
            other = sib[part, 0].astype(jnp.float32)
            stage[pl.ds(part * 2, block, stride=4), :] = jnp.where(first, mine, other)
            stage[pl.ds(part * 2 + 1, block, stride=4), :] = jnp.where(first, other, mine)
        unroll = 128

        def rows(g, carry):
            start = g * unroll
            to = [rmap[step * block + start + u] for u in range(unroll)]
            for some in range(0, unroll, 32):
                lines = [stage[pl.ds(pl.multiple_of((start + some + u) * 4, 4), 4), :] for u in range(32)]
                for u in range(32):
                    held[pl.ds(pl.multiple_of(to[some + u], 4), 4), :] = lines[u]
            return carry

        lax.fori_loop(0, block // unroll, rows, 0)

    @pl.when(step >= steps)
    def _():
        base = (step - steps) * block * 4
        for plane in range(4):
            got = held[pl.ds(base + plane, block, stride=4), :]
            out[:, plane * 128 : (plane + 1) * 128] = got.astype(jnp.bfloat16)


def reorder(info, receiver_map, surface, sibling):
    order, columns = surface.shape[2:]
    block = 2048
    steps = order // block
    spec = pl.BlockSpec((2, 1, block, columns), lambda i, info, rmap: (0, info[0], jnp.minimum(i, steps - 1), 0))

    def body(info, rmap, own, sib, out, stage, held):
        reorder_body(block, steps, info, rmap, own, sib, out, stage, held)

    return pl.pallas_call(
        body,
        out_shape=jax.ShapeDtypeStruct((order, 4 * columns), jnp.bfloat16),
        grid_spec=pltpu.PrefetchScalarGridSpec(
            num_scalar_prefetch=2,
            grid=(2 * steps,),
            in_specs=[spec, spec],
            out_specs=pl.BlockSpec((block, 4 * columns), lambda i, info, rmap: (jnp.maximum(i - steps, 0), 0)),
            scratch_shapes=[
                pltpu.VMEM((block * 4, columns), jnp.float32),
                pltpu.VMEM((order * 4, columns), jnp.float32),
            ],
        ),
        compiler_params=pltpu.CompilerParams(vmem_limit_bytes=56 * 2**20),
        cost_estimate=pl.CostEstimate(flops=1_000_000, bytes_accessed=100_000, transcendentals=0),
        name="reorder",
    )(info, receiver_map, surface, sibling)


def weights_of(info, slot, own_w, sib_w):
    first = info[0] == 0
    chip = info[4 + slot]
    mine = own_w[chip].astype(jnp.float32)
    other = sib_w[chip].astype(jnp.float32)
    natural = jnp.concatenate([jnp.where(first, mine, other), jnp.where(first, other, mine)], axis=1)
    rolled = pltpu.roll(natural, 4, 0)
    low = lax.broadcasted_iota(jnp.int32, natural.shape, 0) < 4
    core0 = jnp.where(low, natural, rolled)
    core1 = jnp.where(low, rolled, natural)
    return jnp.where(first, core0, core1), jnp.where(first, core1, core0)


def all_weights(info, slot0, slots, own_w, sib_w):
    tiles = []
    for slot in range(slots):
        tiles.extend(weights_of(info, slot0 + slot, own_w, sib_w))
    return jnp.concatenate(tiles, axis=0)


def product(info, slot0, groups, surf, own_w, sib_w, earlier):
    order, width = surf.shape
    half = width // 2
    block = 2048
    steps = order // block
    flat = []
    for group in groups:
        flat.extend(group if isinstance(group, tuple) else (group,))
    count = len(flat)
    total_rows = 64 * len(groups)
    slots = total_rows // 16

    def join(refs):
        refs = list(refs)
        parts = []
        for group in groups:
            if isinstance(group, tuple):
                parts.extend((refs.pop(0)[...], refs.pop(0)[...]))
            else:
                parts.append(refs.pop(0)[...])
        return jnp.concatenate(parts, axis=0)

    def body(info, *refs):
        rows = refs[:count]
        data = refs[count : 2 * count]
        surf_ref, own_ref, sib_ref, before, mult, sums, total = refs[2 * count :]
        step = pl.program_id(0)

        @pl.when(step == 0)
        def _():
            total[...] = jnp.zeros_like(total)

        total[...] += jnp.dot(join(rows), surf_ref[...], preferred_element_type=jnp.float32)

        @pl.when(step == steps - 1)
        def _():
            sign = signs(total_rows, half)
            value = total[:, :half] + sign * flip4(total[:, half:])
            mult[...] = value
            seen = join(data).astype(jnp.float32)
            weight = all_weights(info, slot0, slots, own_ref, sib_ref)
            scaled = weight * value

            def add(terms):
                return jnp.sum(terms, axis=0, keepdims=True)

            numer_real = add(scaled * seen)
            numer_imag = add(scaled * (-sign * flip4(seen)))
            energy = add(scaled * value)
            row = lax.broadcasted_iota(jnp.int32, (8, half), 0)
            packed = jnp.where(row == 0, numer_real, jnp.where(row == 1, numer_imag, jnp.where(row == 2, energy, 0.0)))
            sums[...] = packed + before[...]

    row_specs = [pl.BlockSpec((a.shape[0], block), lambda i, info: (0, i)) for a in flat]
    data_specs = [pl.BlockSpec((a.shape[0], half), lambda i, info: (0, info[1])) for a in flat]
    whole = lambda a: pl.BlockSpec(a.shape, lambda i, info: (0,) * a.ndim)
    return pl.pallas_call(
        body,
        out_shape=[
            jax.ShapeDtypeStruct((total_rows, half), jnp.float32),
            jax.ShapeDtypeStruct((8, half), jnp.float32),
        ],
        grid_spec=pltpu.PrefetchScalarGridSpec(
            num_scalar_prefetch=1,
            grid=(steps,),
            in_specs=row_specs + data_specs + [
                pl.BlockSpec((block, width), lambda i, info: (i, 0)), whole(own_w), whole(sib_w), whole(earlier),
            ],
            out_specs=[
                pl.BlockSpec((total_rows, half), lambda i, info: (0, 0)),
                pl.BlockSpec((8, half), lambda i, info: (0, 0)),
            ],
            scratch_shapes=[pltpu.VMEM((total_rows, width), jnp.float32)],
        ),
        compiler_params=pltpu.CompilerParams(vmem_limit_bytes=40 * 2**20),
        cost_estimate=pl.CostEstimate(flops=1_000_000, bytes_accessed=100_000, transcendentals=0),
        name="product",
    )(info, *flat, *flat, surf, own_w, sib_w, earlier)


def subtract(info, groups, mults, own_w, sib_w, shares, total_shots):
    half = mults[0].shape[1]
    flat = []
    for group in groups:
        flat.extend(group if isinstance(group, tuple) else (group,))
    count = len(flat)

    def body(info, *refs):
        data = list(refs[:count])
        mult_refs = list(refs[count : count + len(mults)])
        own_ref, sib_ref = refs[count + len(mults) : count + len(mults) + 2]
        share_refs = refs[count + len(mults) + 2 : -2]
        out, gains = refs[-2:]
        sums = share_refs[0][...] + share_refs[1][...]
        denom = sums[2:3] + ridge_share * total_shots
        gain_real = sums[0:1] / denom
        gain_imag = sums[1:2] / denom
        row = lax.broadcasted_iota(jnp.int32, (8, half), 0)
        gains[...] = jnp.where(row == 0, gain_real, jnp.where(row == 1, gain_imag, 0.0))
        sign = signs(64, half)
        lines = []
        for ref in mult_refs:
            lines.extend((ref, start) for start in range(0, ref.shape[0], 64))
        for index, group in enumerate(groups):
            if isinstance(group, tuple):
                seen = jnp.concatenate([data.pop(0)[...], data.pop(0)[...]], axis=0)
            else:
                seen = data.pop(0)[...]
            ref, start = lines[index]
            value = ref[start : start + 64, :]
            weight = all_weights(info, index * 4, 4, own_ref, sib_ref)
            term = weight * (gain_real * value + sign * gain_imag * flip4(value))
            term = term.astype(jnp.bfloat16).astype(jnp.float32)
            left = (seen.astype(jnp.float32) - term).astype(jnp.bfloat16)
            for slot in range(4):
                out[info[4 + index * 4 + slot]] = left[slot * 16 : (slot + 1) * 16, :]

    whole = lambda a: pl.BlockSpec(a.shape, lambda i, info: (0,) * a.ndim)
    return pl.pallas_call(
        body,
        out_shape=[
            jax.ShapeDtypeStruct((CHIPS, 16, half), jnp.bfloat16),
            jax.ShapeDtypeStruct((8, half), jnp.float32),
        ],
        grid_spec=pltpu.PrefetchScalarGridSpec(
            num_scalar_prefetch=1,
            grid=(1,),
            in_specs=[pl.BlockSpec((a.shape[0], half), lambda i, info: (0, info[1])) for a in flat]
            + [whole(a) for a in (*mults, own_w, sib_w, *shares)],
            out_specs=[
                pl.BlockSpec((CHIPS, 16, half), lambda i, info: (0, 0, 0)),
                pl.BlockSpec((8, half), lambda i, info: (0, 0)),
            ],
        ),
        compiler_params=pltpu.CompilerParams(vmem_limit_bytes=24 * 2**20),
        cost_estimate=pl.CostEstimate(flops=4_000_000, bytes_accessed=2_000_000, transcendentals=0),
        name="subtract",
    )(info, *flat, *mults, own_w, sib_w, *shares)


def per_device(recorded, surface, receiver_map, live_traces):
    x, y, z, core = (lax.axis_index(a) for a in ("grp", "y", "z", "core"))
    nrec = recorded.shape[3]
    columns = surface.shape[3]
    table = jnp.where(core == 0, jnp.asarray(np.array(SLOTS[0], np.int32)), jnp.asarray(np.array(SLOTS[1], np.int32)))
    chips = (y + table[:, 0] + NY) % NY * NZ + (z + table[:, 1] + NZ) % NZ
    zero = jnp.zeros((), jnp.int32)
    info = jnp.concatenate([jnp.stack([core, y * NZ + z, x, zero]), chips]).astype(jnp.int32)

    mine, other = split_freqs(recorded)
    sib_live = swap(live_traces)
    block = jnp.concatenate([mine, swap(other)], axis=0)
    block, surface, sib_live = lax.optimization_barrier((block, surface, sib_live))
    sib_surface = swap(surface)

    up, down, right, left = (0, 1), (0, -1), (1, 0), (-1, 0)
    p1 = send(block, up, right)
    m1 = send(block, down, left)
    m2 = send(block, (0, -2), (-2, 0))
    low = jnp.concatenate([block, p1, m1, m2], axis=0)
    low, info, rmap4 = lax.optimization_barrier((low, info, receiver_map * 4))

    p5 = send(low, right, up)
    m5 = send(low, left, down)
    hp = send(low[:32], (0, 2), right)
    hm = send(low[32:], (0, -2), left)
    surf = reorder(info, rmap4, surface, sib_surface)
    p5, m5, hp, hm, surf = lax.optimization_barrier((p5, m5, hp, hm, surf))
    high = jnp.concatenate([hp, hm], axis=0)

    p6 = send(p5, right, up)
    m6 = send(m5, left, down)
    m6 = jnp.where(core == 0, high, m6)
    p7 = send(jnp.where(core == 0, high, p6), right, up)
    m7 = send(m6, left, down)

    shots = live_traces.shape[0]
    own_w = live_traces.reshape(CHIPS, shots // CHIPS, columns)
    sib_w = sib_live.reshape(CHIPS, shots // CHIPS, columns)
    early = [low, p5, m5, p6, m6]
    none = jnp.zeros((8, 2 * columns), jnp.float32)
    mult1, sums1 = product(info, 0, early, surf, own_w, sib_w, none)
    p7, m7, sums1 = lax.optimization_barrier((p7, m7, sums1))
    p8 = send(p7[:32], right, up)
    m8 = send(m7[32:], left, down)
    middle, late = [p7, m7], [(p8, m8)]
    mult2, sums2 = product(info, 4 * len(early), middle, surf, own_w, sib_w, sums1)
    mult3, sums = product(info, 4 * len(early + middle), late, surf, own_w, sib_w, sums2)
    sums = sums + lax.ppermute(sums, "grp", [(0, 1), (1, 0), (2, 3), (3, 2)])
    shares = [sums, lax.ppermute(sums, "grp", [(0, 2), (2, 0), (1, 3), (3, 1)])]
    total_shots = shots * lax.axis_size("grp")
    groups = early + middle + late
    out, gains = subtract(info, groups, [mult1, mult2, mult3], own_w, sib_w, shares, total_shots)

    back = lax.all_to_all(out, ("y", "z"), split_axis=0, concat_axis=0, tiled=True)
    back, gains = lax.optimization_barrier((back, gains))
    primaries, gains = assemble(back, swap(back), gains, swap(gains))
    return (primaries, gains)


def solution(mesh):
    fine = Mesh(mesh.devices.reshape(4, NY, NZ, 2), ("grp", "y", "z", "core"))
    every = ("grp", "y", "z", "core")
    return jax.shard_map(
        per_device,
        mesh=fine,
        in_specs=(P(None, None, every, None), P(None, None, None, RCV), P(), P("grp", RCV)),
        out_specs=(P(None, None, every, None), P(None, None, RCV)),
        check_vma=False,
    )
```

```python
import jax
import jax.numpy as jnp
from jax import lax
from jax.experimental import pallas as pl
from jax.experimental.pallas import tpu as pltpu
from jax.sharding import Mesh, PartitionSpec as P

ridge_share = 0.05
NY, NZ = 4, 8
CHIPS = NY * NZ
RCV = ("y", "z", "core")

LOW_Z = [(0, 0), (0, -1), (0, 1), (0, 2)]
HIGH_Z = [(0, -2), (0, -3), (0, 3), (0, 4)]
LOW_Y = [(0, 0), (-1, 0), (1, 0), (2, 0)]


def shift(blocks, dy, dz):
    return [(a + dy, b + dz) for a, b in blocks]


SLOTS = (
    LOW_Z + shift(LOW_Z, -1, 0) + shift(LOW_Z, 1, 0) + shift(LOW_Z, -2, 0) + HIGH_Z
    + shift(HIGH_Z, -1, 0) + shift(HIGH_Z, 1, 0) + shift(HIGH_Z[:2], -2, 0) + shift(HIGH_Z[2:], 2, 0),
    LOW_Y + shift(LOW_Y, 0, -1) + shift(LOW_Y, 0, 1) + shift(LOW_Y, 0, -2) + shift(LOW_Y, 0, 2)
    + shift(LOW_Y, 0, -3) + shift(LOW_Y, 0, 3) + shift(LOW_Y[:2], 0, -4) + shift(LOW_Y[2:], 0, 4),
)


def send(value, move0, move1):
    pairs = []
    for y in range(NY):
        for z in range(NZ):
            for core, move in enumerate((move0, move1)):
                if move is None:
                    continue
                to = ((y + move[0]) % NY * NZ + (z + move[1]) % NZ) * 2 + core
                pairs.append(((y * NZ + z) * 2 + core, to))
    return lax.ppermute(value, RCV, pairs)


def swap(value):
    return lax.ppermute(value, "core", [(0, 1), (1, 0)])


def flip4(value):
    rows, cols = value.shape
    return pltpu.roll(value.reshape(rows // 8, 8, cols), 4, 1).reshape(rows, cols)


def signs(rows, cols):
    row = lax.broadcasted_iota(jnp.int32, (rows, cols), 0)
    return jnp.where(row % 8 < 4, -1.0, 1.0).astype(jnp.float32)


def split_freqs(recorded):
    parts, freqs, shots, nrec = recorded.shape

    def body(rec, mine, other):
        first = lax.axis_index("core") == 0
        rows = [
            jnp.concatenate([rec[part, freq].astype(jnp.float32) for part in range(parts)], axis=0)
            for freq in range(freqs)
        ]
        mine[...] = jnp.where(first, rows[0], rows[1]).astype(jnp.bfloat16)
        other[...] = jnp.where(first, rows[1], rows[0]).astype(jnp.bfloat16)

    return pl.pallas_call(
        body,
        out_shape=[jax.ShapeDtypeStruct((parts * shots, nrec), jnp.bfloat16)] * 2,
        in_specs=[pl.BlockSpec(memory_space=pltpu.VMEM)],
        out_specs=[pl.BlockSpec(memory_space=pltpu.VMEM)] * 2,
        compiler_params=pltpu.CompilerParams(vmem_limit_bytes=16 * 2**20),
        name="split_freqs",
    )(recorded)


def assemble(back, got, gains, got_gains):
    chips, _, width = back.shape
    half = width // 2

    def body(back, got, gains, got_gains, out, out_gains):
        core = lax.axis_index("core")
        first = core == 0
        for chip in range(chips):
            mine = back[chip].astype(jnp.float32)[:8]
            other = got[chip].astype(jnp.float32)[8:]
            for freq, rows in enumerate((jnp.where(first, mine, other), jnp.where(first, other, mine))):
                for part in range(2):
                    out[part, freq, :, chip * width : (chip + 1) * width] = rows[part * 4 : part * 4 + 4].astype(
                        jnp.bfloat16
                    )
        mine = jnp.where(first, gains[:, :half], gains[:, half:])
        other = jnp.where(first, got_gains[:, :half], got_gains[:, half:])
        for freq, rows in enumerate((jnp.where(first, mine, other), jnp.where(first, other, mine))):
            for part in range(2):
                out_gains[part, freq : freq + 1, :] = rows[part : part + 1]

    return pl.pallas_call(
        body,
        out_shape=[
            jax.ShapeDtypeStruct((2, 2, 4, chips * width), jnp.bfloat16),
            jax.ShapeDtypeStruct((2, 2, half), jnp.float32),
        ],
        in_specs=[pl.BlockSpec(memory_space=pltpu.VMEM)] * 4,
        out_specs=[pl.BlockSpec(memory_space=pltpu.VMEM)] * 2,
        compiler_params=pltpu.CompilerParams(vmem_limit_bytes=16 * 2**20),
        name="assemble",
    )(back, got, gains, got_gains)


def reorder_body(block, steps, info, rmap, own, sib, out, stage, held):
    step = pl.program_id(0)
    first = info[0] == 0

    @pl.when(step < steps)
    def _():
        for part in range(2):
            mine = own[part, 0].astype(jnp.float32)
            other = sib[part, 0].astype(jnp.float32)
            stage[pl.ds(part * 2, block, stride=4), :] = jnp.where(first, mine, other)
            stage[pl.ds(part * 2 + 1, block, stride=4), :] = jnp.where(first, other, mine)
        unroll = 128

        def rows(g, carry):
            start = g * unroll
            to = [rmap[step * block + start + u] for u in range(unroll)]
            for some in range(0, unroll, 32):
                lines = [stage[pl.ds(pl.multiple_of((start + some + u) * 4, 4), 4), :] for u in range(32)]
                for u in range(32):
                    held[pl.ds(pl.multiple_of(to[some + u], 4), 4), :] = lines[u]
            return carry

        lax.fori_loop(0, block // unroll, rows, 0)

    @pl.when(step >= steps)
    def _():
        top = pl.multiple_of((step - steps) * block, block)
        for plane in range(4):
            got = held[pl.ds(top * 4 + plane, block, stride=4), :]
            out[pl.ds(top, block), plane * 128 : (plane + 1) * 128] = got.astype(jnp.bfloat16)


def reorder(info, receiver_map, surface, sibling):
    order, columns = surface.shape[2:]
    block = 2048
    steps = order // block
    spec = pl.BlockSpec((2, 1, block, columns), lambda i, info, rmap: (0, info[0], jnp.minimum(i, steps - 1), 0))

    def body(info, rmap, own, sib, out, stage, held):
        reorder_body(block, steps, info, rmap, own, sib, out, stage, held)

    return pl.pallas_call(
        body,
        out_shape=pltpu.VMEM((order, 4 * columns), jnp.bfloat16),
        grid_spec=pltpu.PrefetchScalarGridSpec(
            num_scalar_prefetch=2,
            grid=(2 * steps,),
            in_specs=[spec, spec],
            out_specs=pl.BlockSpec(memory_space=pltpu.VMEM),
            scratch_shapes=[
                pltpu.VMEM((block * 4, columns), jnp.float32),
                pltpu.VMEM((order * 4, columns), jnp.float32),
            ],
        ),
        compiler_params=pltpu.CompilerParams(vmem_limit_bytes=44 * 2**20),
        cost_estimate=pl.CostEstimate(flops=1_000_000, bytes_accessed=100_000, transcendentals=0),
        name="reorder",
    )(info, receiver_map, surface, sibling)


def slot_chip(slot):
    core, y, z = (lax.axis_index(a) for a in ("core", "y", "z"))
    dy, dz = (jnp.where(core == 0, a, b) for a, b in zip(SLOTS[0][slot], SLOTS[1][slot]))
    return ((y + dy + NY) & (NY - 1)) * NZ + ((z + dz + NZ) & (NZ - 1))


def weights_of(info, slot, own_w, sib_w):
    first = info[0] == 0
    chip = slot_chip(slot)
    mine = own_w[chip].astype(jnp.float32)
    other = sib_w[chip].astype(jnp.float32)
    natural = jnp.concatenate([jnp.where(first, mine, other), jnp.where(first, other, mine)], axis=1)
    rolled = pltpu.roll(natural, 4, 0)
    low = lax.broadcasted_iota(jnp.int32, natural.shape, 0) < 4
    core0 = jnp.where(low, natural, rolled)
    core1 = jnp.where(low, rolled, natural)
    return jnp.where(first, core0, core1), jnp.where(first, core1, core0)


def all_weights(info, slot0, slots, own_w, sib_w):
    tiles = []
    for slot in range(slots):
        tiles.extend(weights_of(info, slot0 + slot, own_w, sib_w))
    return jnp.concatenate(tiles, axis=0)


def product(info, slot0, groups, surf, own_w, sib_w, earlier):
    order, width = surf.shape
    half = width // 2
    block = 2048
    steps = order // block
    flat = []
    for group in groups:
        flat.extend(group if isinstance(group, tuple) else (group,))
    count = len(flat)
    total_rows = 64 * len(groups)
    slots = total_rows // 16

    def join(refs):
        refs = list(refs)
        parts = []
        for group in groups:
            if isinstance(group, tuple):
                parts.extend((refs.pop(0)[...], refs.pop(0)[...]))
            else:
                parts.append(refs.pop(0)[...])
        return jnp.concatenate(parts, axis=0)

    def body(info, *refs):
        rows = refs[:count]
        data = refs[count : 2 * count]
        surf_ref, own_ref, sib_ref, before, mult, sums, total = refs[2 * count :]
        step = pl.program_id(0)

        @pl.when(step == 0)
        def _():
            total[...] = jnp.zeros_like(total)

        surf = surf_ref[pl.ds(pl.multiple_of(step * block, block), block), :]
        total[...] += jnp.dot(join(rows), surf, preferred_element_type=jnp.float32)

        @pl.when(step == steps - 1)
        def _():
            sign = signs(total_rows, half)
            value = total[:, :half] + sign * flip4(total[:, half:])
            mult[...] = value
            seen = join(data).astype(jnp.float32)
            weight = all_weights(info, slot0, slots, own_ref, sib_ref)
            scaled = weight * value

            def add(terms):
                return jnp.sum(terms, axis=0, keepdims=True)

            numer_real = add(scaled * seen)
            numer_imag = add(scaled * (-sign * flip4(seen)))
            energy = add(scaled * value)
            row = lax.broadcasted_iota(jnp.int32, (8, half), 0)
            packed = jnp.where(row == 0, numer_real, jnp.where(row == 1, numer_imag, jnp.where(row == 2, energy, 0.0)))
            sums[...] = packed + before[...]

    row_specs = [pl.BlockSpec((a.shape[0], block), lambda i, info: (0, i)) for a in flat]
    data_specs = [pl.BlockSpec((a.shape[0], half), lambda i, info: (0, info[1])) for a in flat]
    whole = lambda a: pl.BlockSpec(a.shape, lambda i, info: (0,) * a.ndim)
    return pl.pallas_call(
        body,
        out_shape=[
            jax.ShapeDtypeStruct((total_rows, half), jnp.float32),
            jax.ShapeDtypeStruct((8, half), jnp.float32),
        ],
        grid_spec=pltpu.PrefetchScalarGridSpec(
            num_scalar_prefetch=1,
            grid=(steps,),
            in_specs=row_specs + data_specs + [
                pl.BlockSpec(memory_space=pltpu.VMEM), whole(own_w), whole(sib_w), whole(earlier),
            ],
            out_specs=[
                pl.BlockSpec((total_rows, half), lambda i, info: (0, 0)),
                pl.BlockSpec((8, half), lambda i, info: (0, 0)),
            ],
            scratch_shapes=[pltpu.VMEM((total_rows, width), jnp.float32)],
        ),
        compiler_params=pltpu.CompilerParams(vmem_limit_bytes=32 * 2**20),
        cost_estimate=pl.CostEstimate(flops=1_000_000, bytes_accessed=100_000, transcendentals=0),
        name="product",
    )(info, *flat, *flat, surf, own_w, sib_w, earlier)


def subtract(info, groups, mults, own_w, sib_w, shares, total_shots):
    half = mults[0].shape[1]
    flat = []
    for group in groups:
        flat.extend(group if isinstance(group, tuple) else (group,))
    count = len(flat)

    def body(info, *refs):
        data = list(refs[:count])
        mult_refs = list(refs[count : count + len(mults)])
        own_ref, sib_ref = refs[count + len(mults) : count + len(mults) + 2]
        share_refs = refs[count + len(mults) + 2 : -3]
        out, gains, kept = refs[-3:]
        for k, share in enumerate(share_refs):
            kept[k] = share[...]
        here = lax.axis_index("grp")
        sums = kept[here]
        for place in range(1, 4):
            sums = sums + kept[(here + 4 - place) & 3]
        denom = sums[2:3] + ridge_share * total_shots
        gain_real = sums[0:1] / denom
        gain_imag = sums[1:2] / denom
        row = lax.broadcasted_iota(jnp.int32, (8, half), 0)
        gains[...] = jnp.where(row == 0, gain_real, jnp.where(row == 1, gain_imag, 0.0))
        sign = signs(64, half)
        lines = []
        for ref in mult_refs:
            lines.extend((ref, start) for start in range(0, ref.shape[0], 64))
        for index, group in enumerate(groups):
            if isinstance(group, tuple):
                seen = jnp.concatenate([data.pop(0)[...], data.pop(0)[...]], axis=0)
            else:
                seen = data.pop(0)[...]
            ref, start = lines[index]
            value = ref[start : start + 64, :]
            weight = all_weights(info, index * 4, 4, own_ref, sib_ref)
            term = weight * (gain_real * value + sign * gain_imag * flip4(value))
            term = term.astype(jnp.bfloat16).astype(jnp.float32)
            left = (seen.astype(jnp.float32) - term).astype(jnp.bfloat16)
            for slot in range(4):
                out[slot_chip(index * 4 + slot)] = left[slot * 16 : (slot + 1) * 16, :]

    whole = lambda a: pl.BlockSpec(a.shape, lambda i, info: (0,) * a.ndim)
    return pl.pallas_call(
        body,
        out_shape=[
            jax.ShapeDtypeStruct((CHIPS, 16, half), jnp.bfloat16),
            jax.ShapeDtypeStruct((8, half), jnp.float32),
        ],
        grid_spec=pltpu.PrefetchScalarGridSpec(
            num_scalar_prefetch=1,
            grid=(1,),
            in_specs=[pl.BlockSpec((a.shape[0], half), lambda i, info: (0, info[1])) for a in flat]
            + [whole(a) for a in (*mults, own_w, sib_w, *shares)],
            out_specs=[
                pl.BlockSpec((CHIPS, 16, half), lambda i, info: (0, 0, 0)),
                pl.BlockSpec((8, half), lambda i, info: (0, 0)),
            ],
            scratch_shapes=[pltpu.VMEM((4, 8, half), jnp.float32)],
        ),
        compiler_params=pltpu.CompilerParams(vmem_limit_bytes=24 * 2**20),
        cost_estimate=pl.CostEstimate(flops=4_000_000, bytes_accessed=2_000_000, transcendentals=0),
        name="subtract",
    )(info, *flat, *mults, own_w, sib_w, *shares)


def per_device(recorded, surface, receiver_map, live_traces):
    y, z, core = (lax.axis_index(a) for a in ("y", "z", "core"))
    nrec = recorded.shape[3]
    columns = surface.shape[3]
    info = jnp.stack([core, y * NZ + z]).astype(jnp.int32)

    mine, other = split_freqs(recorded)
    sib_live = swap(live_traces)
    block = jnp.concatenate([mine, swap(other)], axis=0)
    block, surface, sib_live = lax.optimization_barrier((block, surface, sib_live))
    sib_surface = swap(surface)

    up, down, right, left = (0, 1), (0, -1), (1, 0), (-1, 0)
    m2 = send(block, (0, -2), (-2, 0))
    m1 = send(block, down, left)
    p1 = send(block, up, right)
    low = jnp.concatenate([block, p1, m1, m2], axis=0)
    low, info, rmap4 = lax.optimization_barrier((low, info, receiver_map * 4))

    p5 = send(low, right, up)
    m5 = send(low, left, down)
    hp = send(low[:32], (0, 2), right)
    hm = send(low[32:], (0, -2), left)
    surf = reorder(info, rmap4, surface, sib_surface)
    p5, m5, hp, hm, surf = lax.optimization_barrier((p5, m5, hp, hm, surf))
    high = jnp.concatenate([hp, hm], axis=0)

    p6 = send(p5, right, up)
    m6 = send(m5, left, down)
    m6 = jnp.where(core == 0, high, m6)
    p7 = send(jnp.where(core == 0, high, p6), right, up)
    m7 = send(m6, left, down)

    shots = live_traces.shape[0]
    own_w = live_traces.reshape(CHIPS, shots // CHIPS, columns)
    sib_w = sib_live.reshape(CHIPS, shots // CHIPS, columns)
    early = [low, p5, m5, p6, m6]
    none = jnp.zeros((8, 2 * columns), jnp.float32)
    mult1, sums1 = product(info, 0, early, surf, own_w, sib_w, none)
    p7, m7, sums1 = lax.optimization_barrier((p7, m7, sums1))
    p8 = send(p7[:32], right, up)
    m8 = send(m7[32:], left, down)
    middle, late = [p7, m7], [(p8, m8)]
    mult2, sums2 = product(info, 4 * len(early), middle, surf, own_w, sib_w, sums1)
    mult3, sums = product(info, 4 * len(early + middle), late, surf, own_w, sib_w, sums2)
    shares = [sums] + [lax.ppermute(sums, "grp", [(i, (i + k) % 4) for i in range(4)]) for k in (1, 2, 3)]
    total_shots = shots * lax.axis_size("grp")
    groups = early + middle + late
    out, gains = subtract(info, groups, [mult1, mult2, mult3], own_w, sib_w, shares, total_shots)

    back = lax.all_to_all(out, ("y", "z"), split_axis=0, concat_axis=0, tiled=True)
    back, gains = lax.optimization_barrier((back, gains))
    primaries, gains = assemble(back, swap(back), gains, swap(gains))
    return (primaries, gains)


def solution(mesh):
    fine = Mesh(mesh.devices.reshape(4, NY, NZ, 2), ("grp", "y", "z", "core"))
    every = ("grp", "y", "z", "core")
    return jax.shard_map(
        per_device,
        mesh=fine,
        in_specs=(P(None, None, every, None), P(None, None, None, RCV), P(), P("grp", RCV)),
        out_specs=(P(None, None, every, None), P(None, None, RCV)),
        check_vma=False,
    )
```

```python
import jax
import jax.numpy as jnp
from jax import lax
from jax.experimental import pallas as pl
from jax.experimental.pallas import tpu as pltpu
from jax.sharding import Mesh, PartitionSpec as P

ridge_share = 0.05
NY, NZ = 4, 8
CHIPS = NY * NZ
RCV = ("y", "z", "core")

LOW_Z = [(0, 0), (0, -1), (0, 1), (0, 2)]
HIGH_Z = [(0, -2), (0, -3), (0, 3), (0, 4)]
LOW_Y = [(0, 0), (-1, 0), (1, 0), (2, 0)]


def shift(blocks, dy, dz):
    return [(a + dy, b + dz) for a, b in blocks]


SLOTS = (
    LOW_Y + shift(LOW_Y, 0, -1) + shift(LOW_Y, 0, 1) + shift(LOW_Y, 0, -2) + shift(LOW_Y, 0, 2)
    + shift(LOW_Y, 0, -3) + shift(LOW_Y, 0, 3) + shift(LOW_Y[:2], 0, -4) + shift(LOW_Y[2:], 0, 4),
    LOW_Z + shift(LOW_Z, -1, 0) + shift(LOW_Z, 1, 0) + shift(LOW_Z, -2, 0) + HIGH_Z
    + shift(HIGH_Z, -1, 0) + shift(HIGH_Z, 1, 0) + shift(HIGH_Z[:2], -2, 0) + shift(HIGH_Z[2:], 2, 0),
)


def send(value, move1, move0):
    pairs = []
    for y in range(NY):
        for z in range(NZ):
            for core, move in enumerate((move0, move1)):
                if move is None:
                    continue
                to = ((y + move[0]) % NY * NZ + (z + move[1]) % NZ) * 2 + core
                pairs.append(((y * NZ + z) * 2 + core, to))
    return lax.ppermute(value, RCV, pairs)


def swap(value):
    return lax.ppermute(value, "core", [(0, 1), (1, 0)])


def flip4(value):
    rows, cols = value.shape
    return pltpu.roll(value.reshape(rows // 8, 8, cols), 4, 1).reshape(rows, cols)


def signs(rows, cols):
    row = lax.broadcasted_iota(jnp.int32, (rows, cols), 0)
    return jnp.where(row % 8 < 4, -1.0, 1.0).astype(jnp.float32)


def split_freqs(recorded):
    parts, freqs, shots, nrec = recorded.shape

    def body(rec, mine, other):
        first = lax.axis_index("core") == 0
        rows = [
            jnp.concatenate([rec[part, freq].astype(jnp.float32) for part in range(parts)], axis=0)
            for freq in range(freqs)
        ]
        mine[...] = jnp.where(first, rows[0], rows[1]).astype(jnp.bfloat16)
        other[...] = jnp.where(first, rows[1], rows[0]).astype(jnp.bfloat16)

    return pl.pallas_call(
        body,
        out_shape=[jax.ShapeDtypeStruct((parts * shots, nrec), jnp.bfloat16)] * 2,
        in_specs=[pl.BlockSpec(memory_space=pltpu.VMEM)],
        out_specs=[pl.BlockSpec(memory_space=pltpu.VMEM)] * 2,
        compiler_params=pltpu.CompilerParams(vmem_limit_bytes=16 * 2**20),
        name="split_freqs",
    )(recorded)


def assemble(back, got, gains, got_gains):
    chips, _, width = back.shape
    half = width // 2

    def body(back, got, gains, got_gains, out, out_gains):
        core = lax.axis_index("core")
        first = core == 0
        for chip in range(chips):
            mine = back[chip].astype(jnp.float32)[:8]
            other = got[chip].astype(jnp.float32)[8:]
            for freq, rows in enumerate((jnp.where(first, mine, other), jnp.where(first, other, mine))):
                for part in range(2):
                    out[part, freq, :, chip * width : (chip + 1) * width] = rows[part * 4 : part * 4 + 4].astype(
                        jnp.bfloat16
                    )
        mine = jnp.where(first, gains[:, :half], gains[:, half:])
        other = jnp.where(first, got_gains[:, :half], got_gains[:, half:])
        for freq, rows in enumerate((jnp.where(first, mine, other), jnp.where(first, other, mine))):
            for part in range(2):
                out_gains[part, freq : freq + 1, :] = rows[part : part + 1]

    return pl.pallas_call(
        body,
        out_shape=[
            jax.ShapeDtypeStruct((2, 2, 4, chips * width), jnp.bfloat16),
            jax.ShapeDtypeStruct((2, 2, half), jnp.float32),
        ],
        in_specs=[pl.BlockSpec(memory_space=pltpu.VMEM)] * 4,
        out_specs=[pl.BlockSpec(memory_space=pltpu.VMEM)] * 2,
        compiler_params=pltpu.CompilerParams(vmem_limit_bytes=16 * 2**20),
        name="assemble",
    )(back, got, gains, got_gains)


def scatter_rows(info, rmap4, surface, sibling):
    order, columns = surface.shape[2:]
    block = 2048
    unroll = 128
    steps = order // block

    def body(info, rmap, own, sib, held, stage):
        step = pl.program_id(0)
        first = info[0] == 0
        for part in range(2):
            mine = own[part, 0].astype(jnp.float32)
            other = sib[part, 0].astype(jnp.float32)
            stage[pl.ds(part * 2, block, stride=4), :] = jnp.where(first, mine, other)
            stage[pl.ds(part * 2 + 1, block, stride=4), :] = jnp.where(first, other, mine)

        def rows(g, carry):
            start = g * unroll
            to = [rmap[step * block + start + u] for u in range(unroll)]
            for some in range(0, unroll, 32):
                lines = [stage[pl.ds(pl.multiple_of((start + some + u) * 4, 4), 4), :] for u in range(32)]
                for u in range(32):
                    held[pl.ds(pl.multiple_of(to[some + u], 4), 4), :] = lines[u]
            return carry

        lax.fori_loop(0, block // unroll, rows, 0)

    spec = pl.BlockSpec((2, 1, block, columns), lambda i, info, rmap: (0, info[0], i, 0))
    return pl.pallas_call(
        body,
        out_shape=pltpu.VMEM((order * 4, columns), jnp.float32),
        grid_spec=pltpu.PrefetchScalarGridSpec(
            num_scalar_prefetch=2,
            grid=(steps,),
            in_specs=[spec, spec],
            out_specs=pl.BlockSpec(memory_space=pltpu.VMEM),
            scratch_shapes=[pltpu.VMEM((block * 4, columns), jnp.float32)],
        ),
        compiler_params=pltpu.CompilerParams(vmem_limit_bytes=36 * 2**20),
        cost_estimate=pl.CostEstimate(flops=1_000_000, bytes_accessed=100_000, transcendentals=0),
        name="scatter_rows",
    )(info, rmap4, surface, sibling)


def pack_rows(held):
    rows, columns = held.shape
    order = rows // 4
    block = 1024

    def body(held, out):
        def some(step, carry):
            top = pl.multiple_of(step * block, block)
            for plane in range(4):
                got = held[pl.ds(top * 4 + plane, block, stride=4), :]
                out[pl.ds(top, block), plane * columns : (plane + 1) * columns] = got.astype(jnp.bfloat16)
            return carry

        lax.fori_loop(0, order // block, some, 0)

    return pl.pallas_call(
        body,
        out_shape=pltpu.VMEM((order, 4 * columns), jnp.bfloat16),
        in_specs=[pl.BlockSpec(memory_space=pltpu.VMEM)],
        out_specs=pl.BlockSpec(memory_space=pltpu.VMEM),
        compiler_params=pltpu.CompilerParams(vmem_limit_bytes=6 * 2**20),
        cost_estimate=pl.CostEstimate(flops=1_000_000, bytes_accessed=100_000, transcendentals=0),
        name="pack_rows",
    )(held)


def slot_chip(slot):
    core, y, z = (lax.axis_index(a) for a in ("core", "y", "z"))
    dy, dz = (jnp.where(core == 0, a, b) for a, b in zip(SLOTS[0][slot], SLOTS[1][slot]))
    return ((y + dy + NY) & (NY - 1)) * NZ + ((z + dz + NZ) & (NZ - 1))


def weights_of(info, slot, own_w, sib_w):
    first = info[0] == 0
    chip = slot_chip(slot)
    mine = own_w[chip].astype(jnp.float32)
    other = sib_w[chip].astype(jnp.float32)
    natural = jnp.concatenate([jnp.where(first, mine, other), jnp.where(first, other, mine)], axis=1)
    rolled = pltpu.roll(natural, 4, 0)
    low = lax.broadcasted_iota(jnp.int32, natural.shape, 0) < 4
    core0 = jnp.where(low, natural, rolled)
    core1 = jnp.where(low, rolled, natural)
    return jnp.where(first, core0, core1), jnp.where(first, core1, core0)


def all_weights(info, slot0, slots, own_w, sib_w):
    tiles = []
    for slot in range(slots):
        tiles.extend(weights_of(info, slot0 + slot, own_w, sib_w))
    return jnp.concatenate(tiles, axis=0)


def product(info, slot0, groups, surf, own_w, sib_w, earlier):
    order, width = surf.shape
    half = width // 2
    block = 2048
    steps = order // block
    flat = []
    for group in groups:
        flat.extend(group if isinstance(group, tuple) else (group,))
    count = len(flat)
    total_rows = 64 * len(groups)
    slots = total_rows // 16

    def join(refs):
        refs = list(refs)
        parts = []
        for group in groups:
            if isinstance(group, tuple):
                parts.extend((refs.pop(0)[...], refs.pop(0)[...]))
            else:
                parts.append(refs.pop(0)[...])
        return jnp.concatenate(parts, axis=0)

    def body(info, *refs):
        rows = refs[:count]
        data = refs[count : 2 * count]
        surf_ref, own_ref, sib_ref, before, mult, sums, total = refs[2 * count :]
        step = pl.program_id(0)

        @pl.when(step == 0)
        def _():
            total[...] = jnp.zeros_like(total)

        surf = surf_ref[pl.ds(pl.multiple_of(step * block, block), block), :]
        total[...] += jnp.dot(join(rows), surf, preferred_element_type=jnp.float32)

        @pl.when(step == steps - 1)
        def _():
            sign = signs(total_rows, half)
            value = total[:, :half] + sign * flip4(total[:, half:])
            mult[...] = value
            seen = join(data).astype(jnp.float32)
            weight = all_weights(info, slot0, slots, own_ref, sib_ref)
            scaled = weight * value

            def add(terms):
                return jnp.sum(terms, axis=0, keepdims=True)

            numer_real = add(scaled * seen)
            numer_imag = add(scaled * (-sign * flip4(seen)))
            energy = add(scaled * value)
            row = lax.broadcasted_iota(jnp.int32, (8, half), 0)
            packed = jnp.where(row == 0, numer_real, jnp.where(row == 1, numer_imag, jnp.where(row == 2, energy, 0.0)))
            sums[...] = packed + before[...]

    row_specs = [pl.BlockSpec((a.shape[0], block), lambda i, info: (0, i)) for a in flat]
    data_specs = [pl.BlockSpec((a.shape[0], half), lambda i, info: (0, info[1])) for a in flat]
    whole = lambda a: pl.BlockSpec(a.shape, lambda i, info: (0,) * a.ndim)
    return pl.pallas_call(
        body,
        out_shape=[
            jax.ShapeDtypeStruct((total_rows, half), jnp.float32),
            jax.ShapeDtypeStruct((8, half), jnp.float32),
        ],
        grid_spec=pltpu.PrefetchScalarGridSpec(
            num_scalar_prefetch=1,
            grid=(steps,),
            in_specs=row_specs + data_specs + [
                pl.BlockSpec(memory_space=pltpu.VMEM), whole(own_w), whole(sib_w), whole(earlier),
            ],
            out_specs=[
                pl.BlockSpec((total_rows, half), lambda i, info: (0, 0)),
                pl.BlockSpec((8, half), lambda i, info: (0, 0)),
            ],
            scratch_shapes=[pltpu.VMEM((total_rows, width), jnp.float32)],
        ),
        compiler_params=pltpu.CompilerParams(vmem_limit_bytes=20 * 2**20),
        cost_estimate=pl.CostEstimate(flops=1_000_000, bytes_accessed=100_000, transcendentals=0),
        name="product",
    )(info, *flat, *flat, surf, own_w, sib_w, earlier)


def subtract(info, groups, mults, own_w, sib_w, shares, total_shots):
    half = mults[0].shape[1]
    flat = []
    for group in groups:
        flat.extend(group if isinstance(group, tuple) else (group,))
    count = len(flat)

    def body(info, *refs):
        data = list(refs[:count])
        mult_refs = list(refs[count : count + len(mults)])
        own_ref, sib_ref = refs[count + len(mults) : count + len(mults) + 2]
        share_refs = refs[count + len(mults) + 2 : -3]
        out, gains, kept = refs[-3:]
        for k, share in enumerate(share_refs):
            kept[k] = share[...]
        here = lax.axis_index("grp")
        sums = kept[here]
        for place in range(1, 4):
            sums = sums + kept[(here + 4 - place) & 3]
        denom = sums[2:3] + ridge_share * total_shots
        gain_real = sums[0:1] / denom
        gain_imag = sums[1:2] / denom
        row = lax.broadcasted_iota(jnp.int32, (8, half), 0)
        gains[...] = jnp.where(row == 0, gain_real, jnp.where(row == 1, gain_imag, 0.0))
        sign = signs(64, half)
        lines = []
        for ref in mult_refs:
            lines.extend((ref, start) for start in range(0, ref.shape[0], 64))
        for index, group in enumerate(groups):
            if isinstance(group, tuple):
                seen = jnp.concatenate([data.pop(0)[...], data.pop(0)[...]], axis=0)
            else:
                seen = data.pop(0)[...]
            ref, start = lines[index]
            value = ref[start : start + 64, :]
            weight = all_weights(info, index * 4, 4, own_ref, sib_ref)
            term = weight * (gain_real * value + sign * gain_imag * flip4(value))
            term = term.astype(jnp.bfloat16).astype(jnp.float32)
            left = (seen.astype(jnp.float32) - term).astype(jnp.bfloat16)
            for slot in range(4):
                out[slot_chip(index * 4 + slot)] = left[slot * 16 : (slot + 1) * 16, :]

    whole = lambda a: pl.BlockSpec(a.shape, lambda i, info: (0,) * a.ndim)
    return pl.pallas_call(
        body,
        out_shape=[
            jax.ShapeDtypeStruct((CHIPS, 16, half), jnp.bfloat16),
            jax.ShapeDtypeStruct((8, half), jnp.float32),
        ],
        grid_spec=pltpu.PrefetchScalarGridSpec(
            num_scalar_prefetch=1,
            grid=(1,),
            in_specs=[pl.BlockSpec((a.shape[0], half), lambda i, info: (0, info[1])) for a in flat]
            + [whole(a) for a in (*mults, own_w, sib_w, *shares)],
            out_specs=[
                pl.BlockSpec((CHIPS, 16, half), lambda i, info: (0, 0, 0)),
                pl.BlockSpec((8, half), lambda i, info: (0, 0)),
            ],
            scratch_shapes=[pltpu.VMEM((4, 8, half), jnp.float32)],
        ),
        compiler_params=pltpu.CompilerParams(vmem_limit_bytes=24 * 2**20),
        cost_estimate=pl.CostEstimate(flops=4_000_000, bytes_accessed=2_000_000, transcendentals=0),
        name="subtract",
    )(info, *flat, *mults, own_w, sib_w, *shares)


def per_device(recorded, surface, receiver_map, live_traces):
    y, z, core = (lax.axis_index(a) for a in ("y", "z", "core"))
    nrec = recorded.shape[3]
    columns = surface.shape[3]
    info = jnp.stack([core, y * NZ + z]).astype(jnp.int32)

    mine, other = split_freqs(recorded)
    sib_live = swap(live_traces)
    block = jnp.concatenate([mine, swap(other)], axis=0)
    block, surface, sib_live = lax.optimization_barrier((block, surface, sib_live))
    sib_surface = swap(surface)

    up, down, right, left = (0, 1), (0, -1), (1, 0), (-1, 0)
    m2 = send(block, (0, -2), (-2, 0))
    m1 = send(block, down, left)
    p1 = send(block, up, right)
    low = jnp.concatenate([block, p1, m1, m2], axis=0)
    low, info, rmap4 = lax.optimization_barrier((low, info, receiver_map * 4))

    p5 = send(low, right, up)
    m5 = send(low, left, down)
    hp = send(low[:32], (0, 2), right)
    hm = send(low[32:], (0, -2), left)
    held = scatter_rows(info, rmap4, surface, sib_surface)
    p5, m5, held = lax.optimization_barrier((p5, m5, held))

    p6 = send(p5, right, up)
    m6 = send(m5, left, down)
    high = jnp.concatenate([hp, hm], axis=0)
    surf = pack_rows(held)
    p6, m6, surf = lax.optimization_barrier((p6, m6, surf))
    m6 = jnp.where(core == 1, high, m6)
    p7 = send(jnp.where(core == 1, high, p6), right, up)
    m7 = send(m6, left, down)

    shots = live_traces.shape[0]
    own_w = live_traces.reshape(CHIPS, shots // CHIPS, columns)
    sib_w = sib_live.reshape(CHIPS, shots // CHIPS, columns)
    early = [low, p5, m5, p6, m6]
    none = jnp.zeros((8, 2 * columns), jnp.float32)
    mult1, sums1 = product(info, 0, early, surf, own_w, sib_w, none)
    p7, m7, sums1 = lax.optimization_barrier((p7, m7, sums1))
    p8 = send(p7[:32], right, up)
    m8 = send(m7[32:], left, down)
    middle, late = [p7, m7], [(p8, m8)]
    mult2, sums2 = product(info, 4 * len(early), middle, surf, own_w, sib_w, sums1)
    mult3, sums = product(info, 4 * len(early + middle), late, surf, own_w, sib_w, sums2)
    shares = [sums] + [lax.ppermute(sums, "grp", [(i, (i + k) % 4) for i in range(4)]) for k in (1, 2, 3)]
    total_shots = shots * lax.axis_size("grp")
    groups = early + middle + late
    out, gains = subtract(info, groups, [mult1, mult2, mult3], own_w, sib_w, shares, total_shots)

    back = lax.all_to_all(out, ("y", "z"), split_axis=0, concat_axis=0, tiled=True)
    back, gains = lax.optimization_barrier((back, gains))
    primaries, gains = assemble(back, swap(back), gains, swap(gains))
    return (primaries, gains)


def solution(mesh):
    fine = Mesh(mesh.devices.reshape(4, NY, NZ, 2), ("grp", "y", "z", "core"))
    every = ("grp", "y", "z", "core")
    return jax.shard_map(
        per_device,
        mesh=fine,
        in_specs=(P(None, None, every, None), P(None, None, None, RCV), P(), P("grp", RCV)),
        out_specs=(P(None, None, every, None), P(None, None, RCV)),
        check_vma=False,
    )
```

```python
import jax
import jax.numpy as jnp
from jax import lax
from jax.experimental import pallas as pl
from jax.experimental.pallas import tpu as pltpu
from jax.sharding import Mesh, PartitionSpec as P

ridge_share = 0.05
NY, NZ = 4, 8
CHIPS = NY * NZ
RCV = ("y", "z", "core")

LOW_Z = [(0, 0), (0, -1), (0, 1), (0, 2)]
HIGH_Z = [(0, -2), (0, -3), (0, 3), (0, 4)]
LOW_Y = [(0, 0), (-1, 0), (1, 0), (2, 0)]


def shift(blocks, dy, dz):
    return [(a + dy, b + dz) for a, b in blocks]


SLOTS = (
    LOW_Y + shift(LOW_Y, 0, -1) + shift(LOW_Y, 0, 1) + shift(LOW_Y, 0, -2) + shift(LOW_Y, 0, 2)
    + shift(LOW_Y, 0, -3) + shift(LOW_Y, 0, 3) + shift(LOW_Y[:2], 0, -4) + shift(LOW_Y[2:], 0, 4),
    LOW_Z + shift(LOW_Z, -1, 0) + shift(LOW_Z, 1, 0) + shift(LOW_Z, -2, 0) + HIGH_Z
    + shift(HIGH_Z, -1, 0) + shift(HIGH_Z, 1, 0) + shift(HIGH_Z[:2], -2, 0) + shift(HIGH_Z[2:], 2, 0),
)


def send(value, move1, move0):
    pairs = []
    for y in range(NY):
        for z in range(NZ):
            for core, move in enumerate((move0, move1)):
                if move is None:
                    continue
                to = ((y + move[0]) % NY * NZ + (z + move[1]) % NZ) * 2 + core
                pairs.append(((y * NZ + z) * 2 + core, to))
    return lax.ppermute(value, RCV, pairs)


def swap(value):
    return lax.ppermute(value, "core", [(0, 1), (1, 0)])


def flip4(value):
    rows, cols = value.shape
    return pltpu.roll(value.reshape(rows // 8, 8, cols), 4, 1).reshape(rows, cols)


def signs(rows, cols):
    row = lax.broadcasted_iota(jnp.int32, (rows, cols), 0)
    return jnp.where(row % 8 < 4, -1.0, 1.0).astype(jnp.float32)


def split_freqs(recorded):
    parts, freqs, shots, nrec = recorded.shape

    def body(rec, mine, other):
        first = lax.axis_index("core") == 0
        rows = [
            jnp.concatenate([rec[part, freq].astype(jnp.float32) for part in range(parts)], axis=0)
            for freq in range(freqs)
        ]
        mine[...] = jnp.where(first, rows[0], rows[1]).astype(jnp.bfloat16)
        other[...] = jnp.where(first, rows[1], rows[0]).astype(jnp.bfloat16)

    return pl.pallas_call(
        body,
        out_shape=[jax.ShapeDtypeStruct((parts * shots, nrec), jnp.bfloat16)] * 2,
        in_specs=[pl.BlockSpec(memory_space=pltpu.VMEM)],
        out_specs=[pl.BlockSpec(memory_space=pltpu.VMEM)] * 2,
        compiler_params=pltpu.CompilerParams(vmem_limit_bytes=16 * 2**20),
        name="split_freqs",
    )(recorded)


def assemble(back, got, gains, got_gains):
    chips, _, width = back.shape
    half = width // 2

    def body(back, got, gains, got_gains, out, out_gains):
        core = lax.axis_index("core")
        first = core == 0
        for chip in range(chips):
            mine = back[chip].astype(jnp.float32)[:8]
            other = got[chip].astype(jnp.float32)[8:]
            for freq, rows in enumerate((jnp.where(first, mine, other), jnp.where(first, other, mine))):
                for part in range(2):
                    out[part, freq, :, chip * width : (chip + 1) * width] = rows[part * 4 : part * 4 + 4].astype(
                        jnp.bfloat16
                    )
        mine = jnp.where(first, gains[:, :half], gains[:, half:])
        other = jnp.where(first, got_gains[:, :half], got_gains[:, half:])
        for freq, rows in enumerate((jnp.where(first, mine, other), jnp.where(first, other, mine))):
            for part in range(2):
                out_gains[part, freq : freq + 1, :] = rows[part : part + 1]

    return pl.pallas_call(
        body,
        out_shape=[
            jax.ShapeDtypeStruct((2, 2, 4, chips * width), jnp.bfloat16),
            jax.ShapeDtypeStruct((2, 2, half), jnp.float32),
        ],
        in_specs=[pl.BlockSpec(memory_space=pltpu.VMEM)] * 4,
        out_specs=[pl.BlockSpec(memory_space=pltpu.VMEM)] * 2,
        compiler_params=pltpu.CompilerParams(vmem_limit_bytes=16 * 2**20),
        name="assemble",
    )(back, got, gains, got_gains)


def scatter_rows(info, rmap4, surface, sibling):
    order, columns = surface.shape[2:]
    block = 2048
    unroll = 128
    steps = order // block

    def body(info, rmap, own, sib, held, stage):
        step = pl.program_id(0)
        first = info[0] == 0
        for part in range(2):
            mine = own[part, 0].astype(jnp.float32)
            other = sib[part, 0].astype(jnp.float32)
            stage[pl.ds(part * 2, block, stride=4), :] = jnp.where(first, mine, other)
            stage[pl.ds(part * 2 + 1, block, stride=4), :] = jnp.where(first, other, mine)

        def rows(g, carry):
            start = g * unroll
            to = [rmap[step * block + start + u] for u in range(unroll)]
            for some in range(0, unroll, 32):
                lines = [stage[pl.ds(pl.multiple_of((start + some + u) * 4, 4), 4), :] for u in range(32)]
                for u in range(32):
                    held[pl.ds(pl.multiple_of(to[some + u], 4), 4), :] = lines[u]
            return carry

        lax.fori_loop(0, block // unroll, rows, 0)

    spec = pl.BlockSpec((2, 1, block, columns), lambda i, info, rmap: (0, info[0], i, 0))
    return pl.pallas_call(
        body,
        out_shape=pltpu.VMEM((order * 4, columns), jnp.float32),
        grid_spec=pltpu.PrefetchScalarGridSpec(
            num_scalar_prefetch=2,
            grid=(steps,),
            in_specs=[spec, spec],
            out_specs=pl.BlockSpec(memory_space=pltpu.VMEM),
            scratch_shapes=[pltpu.VMEM((block * 4, columns), jnp.float32)],
        ),
        compiler_params=pltpu.CompilerParams(vmem_limit_bytes=36 * 2**20),
        cost_estimate=pl.CostEstimate(flops=1_000_000, bytes_accessed=100_000, transcendentals=0),
        name="scatter_rows",
    )(info, rmap4, surface, sibling)


def pack_rows(held):
    rows, columns = held.shape
    order = rows // 4
    block = 1024

    def body(held, out):
        def some(step, carry):
            top = pl.multiple_of(step * block, block)
            for plane in range(4):
                got = held[pl.ds(top * 4 + plane, block, stride=4), :]
                out[pl.ds(top, block), plane * columns : (plane + 1) * columns] = got.astype(jnp.bfloat16)
            return carry

        lax.fori_loop(0, order // block, some, 0)

    return pl.pallas_call(
        body,
        out_shape=pltpu.VMEM((order, 4 * columns), jnp.bfloat16),
        in_specs=[pl.BlockSpec(memory_space=pltpu.VMEM)],
        out_specs=pl.BlockSpec(memory_space=pltpu.VMEM),
        compiler_params=pltpu.CompilerParams(vmem_limit_bytes=6 * 2**20),
        cost_estimate=pl.CostEstimate(flops=1_000_000, bytes_accessed=100_000, transcendentals=0),
        name="pack_rows",
    )(held)


def slot_chip(slot):
    core, y, z = (lax.axis_index(a) for a in ("core", "y", "z"))
    dy, dz = (jnp.where(core == 0, a, b) for a, b in zip(SLOTS[0][slot], SLOTS[1][slot]))
    return ((y + dy + NY) & (NY - 1)) * NZ + ((z + dz + NZ) & (NZ - 1))


def weights_of(info, slot, own_w, sib_w):
    first = info[0] == 0
    chip = slot_chip(slot)
    mine = own_w[chip].astype(jnp.float32)
    other = sib_w[chip].astype(jnp.float32)
    natural = jnp.concatenate([jnp.where(first, mine, other), jnp.where(first, other, mine)], axis=1)
    rolled = pltpu.roll(natural, 4, 0)
    low = lax.broadcasted_iota(jnp.int32, natural.shape, 0) < 4
    core0 = jnp.where(low, natural, rolled)
    core1 = jnp.where(low, rolled, natural)
    return jnp.where(first, core0, core1), jnp.where(first, core1, core0)


def all_weights(info, slot0, slots, own_w, sib_w):
    tiles = []
    for slot in range(slots):
        tiles.extend(weights_of(info, slot0 + slot, own_w, sib_w))
    return jnp.concatenate(tiles, axis=0)


def product(info, slot0, groups, surf, own_w, sib_w, earlier):
    order, width = surf.shape
    half = width // 2
    block = 2048
    steps = order // block
    flat = []
    for group in groups:
        flat.extend(group if isinstance(group, tuple) else (group,))
    count = len(flat)
    total_rows = 64 * len(groups)
    slots = total_rows // 16

    def join(refs):
        refs = list(refs)
        parts = []
        for group in groups:
            if isinstance(group, tuple):
                parts.extend((refs.pop(0)[...], refs.pop(0)[...]))
            else:
                parts.append(refs.pop(0)[...])
        return jnp.concatenate(parts, axis=0)

    def body(info, *refs):
        rows = refs[:count]
        data = refs[count : 2 * count]
        surf_ref, own_ref, sib_ref, before, mult, sums, total = refs[2 * count :]
        step = pl.program_id(0)

        @pl.when(step == 0)
        def _():
            total[...] = jnp.zeros_like(total)

        surf = surf_ref[pl.ds(pl.multiple_of(step * block, block), block), :]
        total[...] += jnp.dot(join(rows), surf, preferred_element_type=jnp.float32)

        @pl.when(step == steps - 1)
        def _():
            sign = signs(total_rows, half)
            value = total[:, :half] + sign * flip4(total[:, half:])
            mult[...] = value
            seen = join(data).astype(jnp.float32)
            weight = all_weights(info, slot0, slots, own_ref, sib_ref)
            scaled = weight * value

            def add(terms):
                return jnp.sum(terms, axis=0, keepdims=True)

            numer_real = add(scaled * seen)
            numer_imag = add(scaled * (-sign * flip4(seen)))
            energy = add(scaled * value)
            row = lax.broadcasted_iota(jnp.int32, (8, half), 0)
            packed = jnp.where(row == 0, numer_real, jnp.where(row == 1, numer_imag, jnp.where(row == 2, energy, 0.0)))
            sums[...] = packed + before[...]

    row_specs = [pl.BlockSpec((a.shape[0], block), lambda i, info: (0, i)) for a in flat]
    data_specs = [pl.BlockSpec((a.shape[0], half), lambda i, info: (0, info[1])) for a in flat]
    whole = lambda a: pl.BlockSpec(a.shape, lambda i, info: (0,) * a.ndim)
    return pl.pallas_call(
        body,
        out_shape=[
            jax.ShapeDtypeStruct((total_rows, half), jnp.float32),
            jax.ShapeDtypeStruct((8, half), jnp.float32),
        ],
        grid_spec=pltpu.PrefetchScalarGridSpec(
            num_scalar_prefetch=1,
            grid=(steps,),
            in_specs=row_specs + data_specs + [
                pl.BlockSpec(memory_space=pltpu.VMEM), whole(own_w), whole(sib_w), whole(earlier),
            ],
            out_specs=[
                pl.BlockSpec((total_rows, half), lambda i, info: (0, 0)),
                pl.BlockSpec((8, half), lambda i, info: (0, 0)),
            ],
            scratch_shapes=[pltpu.VMEM((total_rows, width), jnp.float32)],
        ),
        compiler_params=pltpu.CompilerParams(vmem_limit_bytes=20 * 2**20),
        cost_estimate=pl.CostEstimate(flops=1_000_000, bytes_accessed=100_000, transcendentals=0),
        name="product",
    )(info, *flat, *flat, surf, own_w, sib_w, earlier)


def subtract(info, groups, mults, own_w, sib_w, shares, total_shots):
    half = mults[0].shape[1]
    flat = []
    for group in groups:
        flat.extend(group if isinstance(group, tuple) else (group,))
    count = len(flat)

    def body(info, *refs):
        data = list(refs[:count])
        mult_refs = list(refs[count : count + len(mults)])
        own_ref, sib_ref = refs[count + len(mults) : count + len(mults) + 2]
        share_refs = refs[count + len(mults) + 2 : -3]
        out, gains, kept = refs[-3:]
        for k, share in enumerate(share_refs):
            kept[k] = share[...]
        here = lax.axis_index("grp")
        sums = kept[here]
        for place in range(1, 4):
            sums = sums + kept[(here + 4 - place) & 3]
        denom = sums[2:3] + ridge_share * total_shots
        gain_real = sums[0:1] / denom
        gain_imag = sums[1:2] / denom
        row = lax.broadcasted_iota(jnp.int32, (8, half), 0)
        gains[...] = jnp.where(row == 0, gain_real, jnp.where(row == 1, gain_imag, 0.0))
        sign = signs(64, half)
        lines = []
        for ref in mult_refs:
            lines.extend((ref, start) for start in range(0, ref.shape[0], 64))
        for index, group in enumerate(groups):
            if isinstance(group, tuple):
                seen = jnp.concatenate([data.pop(0)[...], data.pop(0)[...]], axis=0)
            else:
                seen = data.pop(0)[...]
            ref, start = lines[index]
            value = ref[start : start + 64, :]
            weight = all_weights(info, index * 4, 4, own_ref, sib_ref)
            term = weight * (gain_real * value + sign * gain_imag * flip4(value))
            term = term.astype(jnp.bfloat16).astype(jnp.float32)
            left = (seen.astype(jnp.float32) - term).astype(jnp.bfloat16)
            for slot in range(4):
                out[slot_chip(index * 4 + slot)] = left[slot * 16 : (slot + 1) * 16, :]

    whole = lambda a: pl.BlockSpec(a.shape, lambda i, info: (0,) * a.ndim)
    return pl.pallas_call(
        body,
        out_shape=[
            jax.ShapeDtypeStruct((CHIPS, 16, half), jnp.bfloat16),
            jax.ShapeDtypeStruct((8, half), jnp.float32),
        ],
        grid_spec=pltpu.PrefetchScalarGridSpec(
            num_scalar_prefetch=1,
            grid=(1,),
            in_specs=[pl.BlockSpec((a.shape[0], half), lambda i, info: (0, info[1])) for a in flat]
            + [whole(a) for a in (*mults, own_w, sib_w, *shares)],
            out_specs=[
                pl.BlockSpec((CHIPS, 16, half), lambda i, info: (0, 0, 0)),
                pl.BlockSpec((8, half), lambda i, info: (0, 0)),
            ],
            scratch_shapes=[pltpu.VMEM((4, 8, half), jnp.float32)],
        ),
        compiler_params=pltpu.CompilerParams(vmem_limit_bytes=24 * 2**20),
        cost_estimate=pl.CostEstimate(flops=4_000_000, bytes_accessed=2_000_000, transcendentals=0),
        name="subtract",
    )(info, *flat, *mults, own_w, sib_w, *shares)


def per_device(recorded, surface, receiver_map, live_traces):
    y, z, core = (lax.axis_index(a) for a in ("y", "z", "core"))
    nrec = recorded.shape[3]
    columns = surface.shape[3]
    info = jnp.stack([core, y * NZ + z]).astype(jnp.int32)

    mine, other = split_freqs(recorded)
    sib_live = swap(live_traces)
    block = jnp.concatenate([mine, swap(other)], axis=0)
    block, surface, sib_live = lax.optimization_barrier((block, surface, sib_live))
    sib_surface = swap(surface)

    up, down, right, left = (0, 1), (0, -1), (1, 0), (-1, 0)
    m2 = send(block, (0, -2), (-2, 0))
    m1 = send(block, down, left)
    p1 = send(block, up, right)
    low = jnp.concatenate([block, p1, m1, m2], axis=0)
    low, p1, m2, info, rmap4 = lax.optimization_barrier((low, p1, m2, info, receiver_map * 4))

    p5 = send(low, right, up)
    m5 = send(low, left, down)
    p2 = send(p1, up, right)
    m3 = send(m2, down, left)
    held = scatter_rows(info, rmap4, surface, sib_surface)
    p5, m5, p2, m3, held = lax.optimization_barrier((p5, m5, p2, m3, held))

    p6 = send(p5, right, up)
    m6 = send(m5, left, down)
    p3 = send(p2, up, right)
    m4 = send(m3, down, left)
    high = jnp.concatenate([p2, p3, m3, m4], axis=0)
    surf = pack_rows(held)
    p6, m6, surf = lax.optimization_barrier((p6, m6, surf))
    m6 = jnp.where(core == 1, high, m6)
    p7 = send(jnp.where(core == 1, high, p6), right, up)
    m7 = send(m6, left, down)

    shots = live_traces.shape[0]
    own_w = live_traces.reshape(CHIPS, shots // CHIPS, columns)
    sib_w = sib_live.reshape(CHIPS, shots // CHIPS, columns)
    early = [low, p5, m5, p6, m6]
    none = jnp.zeros((8, 2 * columns), jnp.float32)
    mult1, sums1 = product(info, 0, early, surf, own_w, sib_w, none)
    p7, m7, sums1 = lax.optimization_barrier((p7, m7, sums1))
    p8 = send(p7[:32], right, up)
    m8 = send(m7[32:], left, down)
    middle, late = [p7, m7], [(p8, m8)]
    mult2, sums2 = product(info, 4 * len(early), middle, surf, own_w, sib_w, sums1)
    mult3, sums = product(info, 4 * len(early + middle), late, surf, own_w, sib_w, sums2)
    shares = [sums] + [lax.ppermute(sums, "grp", [(i, (i + k) % 4) for i in range(4)]) for k in (1, 2, 3)]
    total_shots = shots * lax.axis_size("grp")
    groups = early + middle + late
    out, gains = subtract(info, groups, [mult1, mult2, mult3], own_w, sib_w, shares, total_shots)

    back = lax.all_to_all(out, ("y", "z"), split_axis=0, concat_axis=0, tiled=True)
    back, gains = lax.optimization_barrier((back, gains))
    primaries, gains = assemble(back, swap(back), gains, swap(gains))
    return (primaries, gains)


def solution(mesh):
    fine = Mesh(mesh.devices.reshape(4, NY, NZ, 2), ("grp", "y", "z", "core"))
    every = ("grp", "y", "z", "core")
    return jax.shard_map(
        per_device,
        mesh=fine,
        in_specs=(P(None, None, every, None), P(None, None, None, RCV), P(), P("grp", RCV)),
        out_specs=(P(None, None, every, None), P(None, None, RCV)),
        check_vma=False,
    )
```

```python
import jax
import jax.numpy as jnp
from jax import lax
from jax.experimental import pallas as pl
from jax.experimental.pallas import tpu as pltpu
from jax.sharding import Mesh, PartitionSpec as P

ridge_share = 0.05
NY, NZ = 4, 8
CHIPS = NY * NZ
RCV = ("y", "z", "core")

LOW_Z = [(0, 0), (0, -1), (0, 1), (0, 2)]
HIGH_Z = [(0, -2), (0, -3), (0, 3), (0, 4)]
LOW_Y = [(0, 0), (-1, 0), (1, 0), (2, 0)]


def shift(blocks, dy, dz):
    return [(a + dy, b + dz) for a, b in blocks]


SLOTS = (
    LOW_Y + shift(LOW_Y, 0, -1) + shift(LOW_Y, 0, 1) + shift(LOW_Y, 0, -2) + shift(LOW_Y, 0, 2)
    + shift(LOW_Y, 0, -3) + shift(LOW_Y, 0, 3) + shift(LOW_Y[:2], 0, -4) + shift(LOW_Y[2:], 0, 4),
    LOW_Z + shift(LOW_Z, -1, 0) + shift(LOW_Z, 1, 0) + shift(LOW_Z, -2, 0) + HIGH_Z
    + shift(HIGH_Z, -1, 0) + shift(HIGH_Z, 1, 0) + shift(HIGH_Z[:2], -2, 0) + shift(HIGH_Z[2:], 2, 0),
)


def send(value, move1, move0):
    pairs = []
    for y in range(NY):
        for z in range(NZ):
            for core, move in enumerate((move0, move1)):
                if move is None:
                    continue
                to = ((y + move[0]) % NY * NZ + (z + move[1]) % NZ) * 2 + core
                pairs.append(((y * NZ + z) * 2 + core, to))
    return lax.ppermute(value, RCV, pairs)


def swap(value):
    return lax.ppermute(value, "core", [(0, 1), (1, 0)])


def flip4(value):
    rows, cols = value.shape
    return pltpu.roll(value.reshape(rows // 8, 8, cols), 4, 1).reshape(rows, cols)


def signs(rows, cols):
    row = lax.broadcasted_iota(jnp.int32, (rows, cols), 0)
    return jnp.where(row % 8 < 4, -1.0, 1.0).astype(jnp.float32)


def split_freqs(recorded):
    parts, freqs, shots, nrec = recorded.shape

    def body(rec, mine, other):
        first = lax.axis_index("core") == 0
        rows = [
            jnp.concatenate([rec[part, freq].astype(jnp.float32) for part in range(parts)], axis=0)
            for freq in range(freqs)
        ]
        mine[...] = jnp.where(first, rows[0], rows[1]).astype(jnp.bfloat16)
        other[...] = jnp.where(first, rows[1], rows[0]).astype(jnp.bfloat16)

    return pl.pallas_call(
        body,
        out_shape=[jax.ShapeDtypeStruct((parts * shots, nrec), jnp.bfloat16)] * 2,
        in_specs=[pl.BlockSpec(memory_space=pltpu.VMEM)],
        out_specs=[pl.BlockSpec(memory_space=pltpu.VMEM)] * 2,
        compiler_params=pltpu.CompilerParams(vmem_limit_bytes=16 * 2**20),
        name="split_freqs",
    )(recorded)


def assemble(back, got, gains, got_gains):
    chips, _, width = back.shape
    half = width // 2

    def body(back, got, gains, got_gains, out, out_gains):
        core = lax.axis_index("core")
        first = core == 0
        for chip in range(chips):
            mine = back[chip].astype(jnp.float32)[:8]
            other = got[chip].astype(jnp.float32)[8:]
            for freq, rows in enumerate((jnp.where(first, mine, other), jnp.where(first, other, mine))):
                for part in range(2):
                    out[part, freq, :, chip * width : (chip + 1) * width] = rows[part * 4 : part * 4 + 4].astype(
                        jnp.bfloat16
                    )
        mine = jnp.where(first, gains[:, :half], gains[:, half:])
        other = jnp.where(first, got_gains[:, :half], got_gains[:, half:])
        for freq, rows in enumerate((jnp.where(first, mine, other), jnp.where(first, other, mine))):
            for part in range(2):
                out_gains[part, freq : freq + 1, :] = rows[part : part + 1]

    return pl.pallas_call(
        body,
        out_shape=[
            jax.ShapeDtypeStruct((2, 2, 4, chips * width), jnp.bfloat16),
            jax.ShapeDtypeStruct((2, 2, half), jnp.float32),
        ],
        in_specs=[pl.BlockSpec(memory_space=pltpu.VMEM)] * 4,
        out_specs=[pl.BlockSpec(memory_space=pltpu.VMEM)] * 2,
        compiler_params=pltpu.CompilerParams(vmem_limit_bytes=16 * 2**20),
        name="assemble",
    )(back, got, gains, got_gains)


def scatter_rows(info, rmap4, surface, sibling):
    order, columns = surface.shape[2:]
    block = 2048
    unroll = 128
    steps = order // block

    def body(info, rmap, own, sib, held, stage):
        step = pl.program_id(0)
        first = info[0] == 0
        for part in range(2):
            mine = own[part, 0].astype(jnp.float32)
            other = sib[part, 0].astype(jnp.float32)
            stage[pl.ds(part * 2, block, stride=4), :] = jnp.where(first, mine, other)
            stage[pl.ds(part * 2 + 1, block, stride=4), :] = jnp.where(first, other, mine)

        def rows(g, carry):
            start = g * unroll
            to = [rmap[step * block + start + u] for u in range(unroll)]
            for some in range(0, unroll, 32):
                lines = [stage[pl.ds(pl.multiple_of((start + some + u) * 4, 4), 4), :] for u in range(32)]
                for u in range(32):
                    held[pl.ds(pl.multiple_of(to[some + u], 4), 4), :] = lines[u]
            return carry

        lax.fori_loop(0, block // unroll, rows, 0)

    spec = pl.BlockSpec((2, 1, block, columns), lambda i, info, rmap: (0, info[0], i, 0))
    return pl.pallas_call(
        body,
        out_shape=pltpu.VMEM((order * 4, columns), jnp.float32),
        grid_spec=pltpu.PrefetchScalarGridSpec(
            num_scalar_prefetch=2,
            grid=(steps,),
            in_specs=[spec, spec],
            out_specs=pl.BlockSpec(memory_space=pltpu.VMEM),
            scratch_shapes=[pltpu.VMEM((block * 4, columns), jnp.float32)],
        ),
        compiler_params=pltpu.CompilerParams(vmem_limit_bytes=36 * 2**20),
        cost_estimate=pl.CostEstimate(flops=1_000_000, bytes_accessed=100_000, transcendentals=0),
        name="scatter_rows",
    )(info, rmap4, surface, sibling)


def pack_rows(held):
    rows, columns = held.shape
    order = rows // 4
    block = 1024

    def body(held, out):
        def some(step, carry):
            top = pl.multiple_of(step * block, block)
            for plane in range(4):
                got = held[pl.ds(top * 4 + plane, block, stride=4), :]
                out[pl.ds(top, block), plane * columns : (plane + 1) * columns] = got.astype(jnp.bfloat16)
            return carry

        lax.fori_loop(0, order // block, some, 0)

    return pl.pallas_call(
        body,
        out_shape=pltpu.VMEM((order, 4 * columns), jnp.bfloat16),
        in_specs=[pl.BlockSpec(memory_space=pltpu.VMEM)],
        out_specs=pl.BlockSpec(memory_space=pltpu.VMEM),
        compiler_params=pltpu.CompilerParams(vmem_limit_bytes=6 * 2**20),
        cost_estimate=pl.CostEstimate(flops=1_000_000, bytes_accessed=100_000, transcendentals=0),
        name="pack_rows",
    )(held)


def choose(pieces, plus, minus):
    rows, width = plus.shape
    block = 1024
    tall = rows // len(pieces)

    def body(*refs):
        piece_refs, (plus_ref, minus_ref, out_plus, out_minus) = refs[:-4], refs[-4:]
        second = lax.axis_index("core") == 1

        def some(step, carry):
            cols = pl.ds(pl.multiple_of(step * block, block), block)
            for index, piece in enumerate(piece_refs):
                line = pl.ds(index * tall, tall)
                value = piece[:, cols]
                out_plus[line, cols] = jnp.where(second, value, plus_ref[line, cols])
                out_minus[line, cols] = jnp.where(second, value, minus_ref[line, cols])
            return carry

        lax.fori_loop(0, width // block, some, 0)

    return pl.pallas_call(
        body,
        out_shape=[jax.ShapeDtypeStruct((rows, width), jnp.bfloat16)] * 2,
        in_specs=[pl.BlockSpec(memory_space=pltpu.VMEM)] * (len(pieces) + 2),
        out_specs=[pl.BlockSpec(memory_space=pltpu.VMEM)] * 2,
        compiler_params=pltpu.CompilerParams(vmem_limit_bytes=10 * 2**20),
        cost_estimate=pl.CostEstimate(flops=1_000_000, bytes_accessed=100_000, transcendentals=0),
        name="choose",
    )(*pieces, plus, minus)


def slot_chip(slot):
    core, y, z = (lax.axis_index(a) for a in ("core", "y", "z"))
    dy, dz = (jnp.where(core == 0, a, b) for a, b in zip(SLOTS[0][slot], SLOTS[1][slot]))
    return ((y + dy + NY) & (NY - 1)) * NZ + ((z + dz + NZ) & (NZ - 1))


def weights_of(info, slot, own_w, sib_w):
    first = info[0] == 0
    chip = slot_chip(slot)
    mine = own_w[chip].astype(jnp.float32)
    other = sib_w[chip].astype(jnp.float32)
    natural = jnp.concatenate([jnp.where(first, mine, other), jnp.where(first, other, mine)], axis=1)
    rolled = pltpu.roll(natural, 4, 0)
    low = lax.broadcasted_iota(jnp.int32, natural.shape, 0) < 4
    core0 = jnp.where(low, natural, rolled)
    core1 = jnp.where(low, rolled, natural)
    return jnp.where(first, core0, core1), jnp.where(first, core1, core0)


def all_weights(info, slot0, slots, own_w, sib_w):
    tiles = []
    for slot in range(slots):
        tiles.extend(weights_of(info, slot0 + slot, own_w, sib_w))
    return jnp.concatenate(tiles, axis=0)


def product(info, slot0, groups, surf, own_w, sib_w, earlier):
    order, width = surf.shape
    half = width // 2
    block = 2048
    steps = order // block
    flat = []
    for group in groups:
        flat.extend(group if isinstance(group, tuple) else (group,))
    count = len(flat)
    total_rows = 64 * len(groups)
    slots = total_rows // 16

    def join(refs):
        refs = list(refs)
        parts = []
        for group in groups:
            if isinstance(group, tuple):
                parts.extend((refs.pop(0)[...], refs.pop(0)[...]))
            else:
                parts.append(refs.pop(0)[...])
        return jnp.concatenate(parts, axis=0)

    def body(info, *refs):
        rows = refs[:count]
        data = refs[count : 2 * count]
        surf_ref, own_ref, sib_ref, before, mult, sums, total = refs[2 * count :]
        step = pl.program_id(0)

        @pl.when(step == 0)
        def _():
            total[...] = jnp.zeros_like(total)

        surf = surf_ref[pl.ds(pl.multiple_of(step * block, block), block), :]
        total[...] += jnp.dot(join(rows), surf, preferred_element_type=jnp.float32)

        @pl.when(step == steps - 1)
        def _():
            sign = signs(total_rows, half)
            value = total[:, :half] + sign * flip4(total[:, half:])
            mult[...] = value
            seen = join(data).astype(jnp.float32)
            weight = all_weights(info, slot0, slots, own_ref, sib_ref)
            scaled = weight * value

            def add(terms):
                return jnp.sum(terms, axis=0, keepdims=True)

            numer_real = add(scaled * seen)
            numer_imag = add(scaled * (-sign * flip4(seen)))
            energy = add(scaled * value)
            row = lax.broadcasted_iota(jnp.int32, (8, half), 0)
            packed = jnp.where(row == 0, numer_real, jnp.where(row == 1, numer_imag, jnp.where(row == 2, energy, 0.0)))
            sums[...] = packed + before[...]

    row_specs = [pl.BlockSpec((a.shape[0], block), lambda i, info: (0, i)) for a in flat]
    data_specs = [pl.BlockSpec((a.shape[0], half), lambda i, info: (0, info[1])) for a in flat]
    whole = lambda a: pl.BlockSpec(a.shape, lambda i, info: (0,) * a.ndim)
    return pl.pallas_call(
        body,
        out_shape=[
            jax.ShapeDtypeStruct((total_rows, half), jnp.float32),
            jax.ShapeDtypeStruct((8, half), jnp.float32),
        ],
        grid_spec=pltpu.PrefetchScalarGridSpec(
            num_scalar_prefetch=1,
            grid=(steps,),
            in_specs=row_specs + data_specs + [
                pl.BlockSpec(memory_space=pltpu.VMEM), whole(own_w), whole(sib_w), whole(earlier),
            ],
            out_specs=[
                pl.BlockSpec((total_rows, half), lambda i, info: (0, 0)),
                pl.BlockSpec((8, half), lambda i, info: (0, 0)),
            ],
            scratch_shapes=[pltpu.VMEM((total_rows, width), jnp.float32)],
        ),
        compiler_params=pltpu.CompilerParams(vmem_limit_bytes=20 * 2**20),
        cost_estimate=pl.CostEstimate(flops=1_000_000, bytes_accessed=100_000, transcendentals=0),
        name="product",
    )(info, *flat, *flat, surf, own_w, sib_w, earlier)


def subtract(info, groups, mults, own_w, sib_w, shares, total_shots):
    half = mults[0].shape[1]
    flat = []
    for group in groups:
        flat.extend(group if isinstance(group, tuple) else (group,))
    count = len(flat)

    def body(info, *refs):
        data = list(refs[:count])
        mult_refs = list(refs[count : count + len(mults)])
        own_ref, sib_ref = refs[count + len(mults) : count + len(mults) + 2]
        share_refs = refs[count + len(mults) + 2 : -3]
        out, gains, kept = refs[-3:]
        for k, share in enumerate(share_refs):
            kept[k] = share[...]
        here = lax.axis_index("grp")
        sums = kept[here]
        for place in range(1, 4):
            sums = sums + kept[(here + 4 - place) & 3]
        denom = sums[2:3] + ridge_share * total_shots
        gain_real = sums[0:1] / denom
        gain_imag = sums[1:2] / denom
        row = lax.broadcasted_iota(jnp.int32, (8, half), 0)
        gains[...] = jnp.where(row == 0, gain_real, jnp.where(row == 1, gain_imag, 0.0))
        sign = signs(64, half)
        lines = []
        for ref in mult_refs:
            lines.extend((ref, start) for start in range(0, ref.shape[0], 64))
        for index, group in enumerate(groups):
            if isinstance(group, tuple):
                seen = jnp.concatenate([data.pop(0)[...], data.pop(0)[...]], axis=0)
            else:
                seen = data.pop(0)[...]
            ref, start = lines[index]
            value = ref[start : start + 64, :]
            weight = all_weights(info, index * 4, 4, own_ref, sib_ref)
            term = weight * (gain_real * value + sign * gain_imag * flip4(value))
            term = term.astype(jnp.bfloat16).astype(jnp.float32)
            left = (seen.astype(jnp.float32) - term).astype(jnp.bfloat16)
            for slot in range(4):
                out[slot_chip(index * 4 + slot)] = left[slot * 16 : (slot + 1) * 16, :]

    whole = lambda a: pl.BlockSpec(a.shape, lambda i, info: (0,) * a.ndim)
    return pl.pallas_call(
        body,
        out_shape=[
            jax.ShapeDtypeStruct((CHIPS, 16, half), jnp.bfloat16),
            jax.ShapeDtypeStruct((8, half), jnp.float32),
        ],
        grid_spec=pltpu.PrefetchScalarGridSpec(
            num_scalar_prefetch=1,
            grid=(1,),
            in_specs=[pl.BlockSpec((a.shape[0], half), lambda i, info: (0, info[1])) for a in flat]
            + [whole(a) for a in (*mults, own_w, sib_w, *shares)],
            out_specs=[
                pl.BlockSpec((CHIPS, 16, half), lambda i, info: (0, 0, 0)),
                pl.BlockSpec((8, half), lambda i, info: (0, 0)),
            ],
            scratch_shapes=[pltpu.VMEM((4, 8, half), jnp.float32)],
        ),
        compiler_params=pltpu.CompilerParams(vmem_limit_bytes=24 * 2**20),
        cost_estimate=pl.CostEstimate(flops=4_000_000, bytes_accessed=2_000_000, transcendentals=0),
        name="subtract",
    )(info, *flat, *mults, own_w, sib_w, *shares)


def per_device(recorded, surface, receiver_map, live_traces):
    y, z, core = (lax.axis_index(a) for a in ("y", "z", "core"))
    nrec = recorded.shape[3]
    columns = surface.shape[3]
    info = jnp.stack([core, y * NZ + z]).astype(jnp.int32)

    mine, other = split_freqs(recorded)
    sib_live = swap(live_traces)
    block = jnp.concatenate([mine, swap(other)], axis=0)
    block, surface, sib_live = lax.optimization_barrier((block, surface, sib_live))
    sib_surface = swap(surface)

    up, down, right, left = (0, 1), (0, -1), (1, 0), (-1, 0)
    m2 = send(block, (0, -2), (-2, 0))
    m1 = send(block, down, left)
    p1 = send(block, up, right)
    low = jnp.concatenate([block, p1, m1, m2], axis=0)
    low, p1, m2, info, rmap4 = lax.optimization_barrier((low, p1, m2, info, receiver_map * 4))

    p5 = send(low, right, up)
    m5 = send(low, left, down)
    p2 = send(p1, up, right)
    m3 = send(m2, down, left)
    held = scatter_rows(info, rmap4, surface, sib_surface)
    p5, m5, p2, m3, held = lax.optimization_barrier((p5, m5, p2, m3, held))

    p6 = send(p5, right, up)
    m6 = send(m5, left, down)
    p3 = send(p2, up, right)
    m4 = send(m3, down, left)
    surf = pack_rows(held)
    p6, m6, p3, m4, surf = lax.optimization_barrier((p6, m6, p3, m4, surf))
    plus, m6 = choose([p2, p3, m3, m4], p6, m6)
    p7 = send(plus, right, up)
    m7 = send(m6, left, down)

    shots = live_traces.shape[0]
    own_w = live_traces.reshape(CHIPS, shots // CHIPS, columns)
    sib_w = sib_live.reshape(CHIPS, shots // CHIPS, columns)
    early = [low, p5, m5, p6, m6]
    none = jnp.zeros((8, 2 * columns), jnp.float32)
    mult1, sums1 = product(info, 0, early, surf, own_w, sib_w, none)
    p7, m7, sums1 = lax.optimization_barrier((p7, m7, sums1))
    p8 = send(p7[:32], right, up)
    m8 = send(m7[32:], left, down)
    middle, late = [p7, m7], [(p8, m8)]
    mult2, sums2 = product(info, 4 * len(early), middle, surf, own_w, sib_w, sums1)
    mult3, sums = product(info, 4 * len(early + middle), late, surf, own_w, sib_w, sums2)
    shares = [sums] + [lax.ppermute(sums, "grp", [(i, (i + k) % 4) for i in range(4)]) for k in (1, 2, 3)]
    total_shots = shots * lax.axis_size("grp")
    groups = early + middle + late
    out, gains = subtract(info, groups, [mult1, mult2, mult3], own_w, sib_w, shares, total_shots)

    back = lax.all_to_all(out, ("y", "z"), split_axis=0, concat_axis=0, tiled=True)
    back, gains = lax.optimization_barrier((back, gains))
    primaries, gains = assemble(back, swap(back), gains, swap(gains))
    return (primaries, gains)


def solution(mesh):
    fine = Mesh(mesh.devices.reshape(4, NY, NZ, 2), ("grp", "y", "z", "core"))
    every = ("grp", "y", "z", "core")
    return jax.shard_map(
        per_device,
        mesh=fine,
        in_specs=(P(None, None, every, None), P(None, None, None, RCV), P(), P("grp", RCV)),
        out_specs=(P(None, None, every, None), P(None, None, RCV)),
        check_vma=False,
    )
```

```python
import jax
import jax.numpy as jnp
from jax import lax
from jax.experimental import pallas as pl
from jax.experimental.pallas import tpu as pltpu
from jax.sharding import Mesh, PartitionSpec as P

ridge_share = 0.05
NY, NZ = 4, 8
CHIPS = NY * NZ
RCV = ("y", "z", "core")

LOW_Z = [(0, 0), (0, -1), (0, 1), (0, 2)]
HIGH_Z = [(0, -2), (0, -3), (0, 3), (0, 4)]
LOW_Y = [(0, 0), (-1, 0), (1, 0), (2, 0)]


def shift(blocks, dy, dz):
    return [(a + dy, b + dz) for a, b in blocks]


SLOTS = (
    LOW_Y + shift(LOW_Y, 0, -1) + shift(LOW_Y, 0, 1) + shift(LOW_Y, 0, -2) + shift(LOW_Y, 0, 2)
    + shift(LOW_Y, 0, -3) + shift(LOW_Y, 0, 3) + shift(LOW_Y[:2], 0, -4) + shift(LOW_Y[2:], 0, 4),
    LOW_Z + shift(LOW_Z, -1, 0) + shift(LOW_Z, 1, 0) + shift(LOW_Z, -2, 0) + HIGH_Z
    + shift(HIGH_Z, -1, 0) + shift(HIGH_Z, 1, 0) + shift(HIGH_Z[:2], -2, 0) + shift(HIGH_Z[2:], 2, 0),
)


def send(value, move1, move0):
    pairs = []
    for y in range(NY):
        for z in range(NZ):
            for core, move in enumerate((move0, move1)):
                if move is None:
                    continue
                to = ((y + move[0]) % NY * NZ + (z + move[1]) % NZ) * 2 + core
                pairs.append(((y * NZ + z) * 2 + core, to))
    return lax.ppermute(value, RCV, pairs)


def swap(value):
    return lax.ppermute(value, "core", [(0, 1), (1, 0)])


def flip4(value):
    rows, cols = value.shape
    return pltpu.roll(value.reshape(rows // 8, 8, cols), 4, 1).reshape(rows, cols)


def signs(rows, cols):
    row = lax.broadcasted_iota(jnp.int32, (rows, cols), 0)
    return jnp.where(row % 8 < 4, -1.0, 1.0).astype(jnp.float32)


def split_freqs(recorded):
    parts, freqs, shots, nrec = recorded.shape

    def body(rec, mine, other):
        first = lax.axis_index("core") == 0
        rows = [
            jnp.concatenate([rec[part, freq].astype(jnp.float32) for part in range(parts)], axis=0)
            for freq in range(freqs)
        ]
        mine[...] = jnp.where(first, rows[0], rows[1]).astype(jnp.bfloat16)
        other[...] = jnp.where(first, rows[1], rows[0]).astype(jnp.bfloat16)

    return pl.pallas_call(
        body,
        out_shape=[jax.ShapeDtypeStruct((parts * shots, nrec), jnp.bfloat16)] * 2,
        in_specs=[pl.BlockSpec(memory_space=pltpu.VMEM)],
        out_specs=[pl.BlockSpec(memory_space=pltpu.VMEM)] * 2,
        compiler_params=pltpu.CompilerParams(vmem_limit_bytes=16 * 2**20),
        name="split_freqs",
    )(recorded)


def assemble(back, got, gains, got_gains):
    chips, _, width = back.shape
    half = width // 2

    def body(back, got, gains, got_gains, out, out_gains):
        core = lax.axis_index("core")
        first = core == 0
        for chip in range(chips):
            mine = back[chip].astype(jnp.float32)[:8]
            other = got[chip].astype(jnp.float32)[8:]
            for freq, rows in enumerate((jnp.where(first, mine, other), jnp.where(first, other, mine))):
                for part in range(2):
                    out[part, freq, :, chip * width : (chip + 1) * width] = rows[part * 4 : part * 4 + 4].astype(
                        jnp.bfloat16
                    )
        mine = jnp.where(first, gains[:, :half], gains[:, half:])
        other = jnp.where(first, got_gains[:, :half], got_gains[:, half:])
        for freq, rows in enumerate((jnp.where(first, mine, other), jnp.where(first, other, mine))):
            for part in range(2):
                out_gains[part, freq : freq + 1, :] = rows[part : part + 1]

    return pl.pallas_call(
        body,
        out_shape=[
            jax.ShapeDtypeStruct((2, 2, 4, chips * width), jnp.bfloat16),
            jax.ShapeDtypeStruct((2, 2, half), jnp.float32),
        ],
        in_specs=[pl.BlockSpec(memory_space=pltpu.VMEM)] * 4,
        out_specs=[pl.BlockSpec(memory_space=pltpu.VMEM)] * 2,
        compiler_params=pltpu.CompilerParams(vmem_limit_bytes=16 * 2**20),
        name="assemble",
    )(back, got, gains, got_gains)


def scatter_rows(info, rmap4, surface, sibling):
    order, columns = surface.shape[2:]
    block = 2048
    unroll = 128
    steps = order // block

    def body(info, rmap, own, sib, held, stage):
        step = pl.program_id(0)
        first = info[0] == 0
        for part in range(2):
            mine = own[part, 0].astype(jnp.float32)
            other = sib[part, 0].astype(jnp.float32)
            stage[pl.ds(part * 2, block, stride=4), :] = jnp.where(first, mine, other)
            stage[pl.ds(part * 2 + 1, block, stride=4), :] = jnp.where(first, other, mine)

        def rows(g, carry):
            start = g * unroll
            to = [rmap[step * block + start + u] for u in range(unroll)]
            for some in range(0, unroll, 32):
                lines = [stage[pl.ds(pl.multiple_of((start + some + u) * 4, 4), 4), :] for u in range(32)]
                for u in range(32):
                    held[pl.ds(pl.multiple_of(to[some + u], 4), 4), :] = lines[u]
            return carry

        lax.fori_loop(0, block // unroll, rows, 0)

    spec = pl.BlockSpec((2, 1, block, columns), lambda i, info, rmap: (0, info[0], i, 0))
    return pl.pallas_call(
        body,
        out_shape=pltpu.VMEM((order * 4, columns), jnp.float32),
        grid_spec=pltpu.PrefetchScalarGridSpec(
            num_scalar_prefetch=2,
            grid=(steps,),
            in_specs=[spec, spec],
            out_specs=pl.BlockSpec(memory_space=pltpu.VMEM),
            scratch_shapes=[pltpu.VMEM((block * 4, columns), jnp.float32)],
        ),
        compiler_params=pltpu.CompilerParams(vmem_limit_bytes=36 * 2**20),
        cost_estimate=pl.CostEstimate(flops=1_000_000, bytes_accessed=100_000, transcendentals=0),
        name="scatter_rows",
    )(info, rmap4, surface, sibling)


def pack_rows(held):
    rows, columns = held.shape
    order = rows // 4
    block = 1024

    def body(held, out):
        def some(step, carry):
            top = pl.multiple_of(step * block, block)
            for plane in range(4):
                got = held[pl.ds(top * 4 + plane, block, stride=4), :]
                out[pl.ds(top, block), plane * columns : (plane + 1) * columns] = got.astype(jnp.bfloat16)
            return carry

        lax.fori_loop(0, order // block, some, 0)

    return pl.pallas_call(
        body,
        out_shape=pltpu.VMEM((order, 4 * columns), jnp.bfloat16),
        in_specs=[pl.BlockSpec(memory_space=pltpu.VMEM)],
        out_specs=pl.BlockSpec(memory_space=pltpu.VMEM),
        compiler_params=pltpu.CompilerParams(vmem_limit_bytes=6 * 2**20),
        cost_estimate=pl.CostEstimate(flops=1_000_000, bytes_accessed=100_000, transcendentals=0),
        name="pack_rows",
    )(held)


def stack_rows(pieces):
    tall, width = pieces[0].shape

    def body(*refs):
        for index, piece in enumerate(refs[:-1]):
            refs[-1][index * tall : (index + 1) * tall, :] = piece[...]

    return pl.pallas_call(
        body,
        out_shape=jax.ShapeDtypeStruct((tall * len(pieces), width), jnp.bfloat16),
        in_specs=[pl.BlockSpec(memory_space=pltpu.VMEM)] * len(pieces),
        out_specs=pl.BlockSpec(memory_space=pltpu.VMEM),
        compiler_params=pltpu.CompilerParams(vmem_limit_bytes=10 * 2**20),
        cost_estimate=pl.CostEstimate(flops=1_000_000, bytes_accessed=100_000, transcendentals=0),
        name="stack_rows",
    )(*pieces)


def choose(pieces, plus, minus):
    rows, width = plus.shape
    block = 1024
    tall = rows // len(pieces)

    def body(*refs):
        piece_refs, (plus_ref, minus_ref, out_plus, out_minus) = refs[:-4], refs[-4:]
        second = lax.axis_index("core") == 1

        def some(step, carry):
            cols = pl.ds(pl.multiple_of(step * block, block), block)
            for index, piece in enumerate(piece_refs):
                line = pl.ds(index * tall, tall)
                value = piece[:, cols]
                out_plus[line, cols] = jnp.where(second, value, plus_ref[line, cols])
                out_minus[line, cols] = jnp.where(second, value, minus_ref[line, cols])
            return carry

        lax.fori_loop(0, width // block, some, 0)

    return pl.pallas_call(
        body,
        out_shape=[jax.ShapeDtypeStruct((rows, width), jnp.bfloat16)] * 2,
        in_specs=[pl.BlockSpec(memory_space=pltpu.VMEM)] * (len(pieces) + 2),
        out_specs=[pl.BlockSpec(memory_space=pltpu.VMEM)] * 2,
        compiler_params=pltpu.CompilerParams(vmem_limit_bytes=10 * 2**20),
        cost_estimate=pl.CostEstimate(flops=1_000_000, bytes_accessed=100_000, transcendentals=0),
        name="choose",
    )(*pieces, plus, minus)


def slot_chip(slot):
    core, y, z = (lax.axis_index(a) for a in ("core", "y", "z"))
    dy, dz = (jnp.where(core == 0, a, b) for a, b in zip(SLOTS[0][slot], SLOTS[1][slot]))
    return ((y + dy + NY) & (NY - 1)) * NZ + ((z + dz + NZ) & (NZ - 1))


def weights_of(info, slot, own_w, sib_w):
    first = info[0] == 0
    chip = slot_chip(slot)
    mine = own_w[chip].astype(jnp.float32)
    other = sib_w[chip].astype(jnp.float32)
    natural = jnp.concatenate([jnp.where(first, mine, other), jnp.where(first, other, mine)], axis=1)
    rolled = pltpu.roll(natural, 4, 0)
    low = lax.broadcasted_iota(jnp.int32, natural.shape, 0) < 4
    core0 = jnp.where(low, natural, rolled)
    core1 = jnp.where(low, rolled, natural)
    return jnp.where(first, core0, core1), jnp.where(first, core1, core0)


def all_weights(info, slot0, slots, own_w, sib_w):
    tiles = []
    for slot in range(slots):
        tiles.extend(weights_of(info, slot0 + slot, own_w, sib_w))
    return jnp.concatenate(tiles, axis=0)


def product(info, slot0, groups, surf, own_w, sib_w, earlier):
    order, width = surf.shape
    half = width // 2
    block = 2048 if len(groups) > 2 else 4096
    steps = order // block
    flat = []
    for group in groups:
        flat.extend(group if isinstance(group, tuple) else (group,))
    count = len(flat)
    total_rows = 64 * len(groups)
    slots = total_rows // 16

    def join(refs):
        refs = list(refs)
        parts = []
        for group in groups:
            if isinstance(group, tuple):
                parts.extend((refs.pop(0)[...], refs.pop(0)[...]))
            else:
                parts.append(refs.pop(0)[...])
        return jnp.concatenate(parts, axis=0)

    def body(info, *refs):
        rows = refs[:count]
        data = refs[count : 2 * count]
        surf_ref, own_ref, sib_ref, before, mult, sums, total = refs[2 * count :]
        step = pl.program_id(0)

        @pl.when(step == 0)
        def _():
            total[...] = jnp.zeros_like(total)

        surf = surf_ref[pl.ds(pl.multiple_of(step * block, block), block), :]
        total[...] += jnp.dot(join(rows), surf, preferred_element_type=jnp.float32)

        @pl.when(step == steps - 1)
        def _():
            sign = signs(total_rows, half)
            value = total[:, :half] + sign * flip4(total[:, half:])
            mult[...] = value
            seen = join(data).astype(jnp.float32)
            weight = all_weights(info, slot0, slots, own_ref, sib_ref)
            scaled = weight * value

            def add(terms):
                return jnp.sum(terms, axis=0, keepdims=True)

            numer_real = add(scaled * seen)
            numer_imag = add(scaled * (-sign * flip4(seen)))
            energy = add(scaled * value)
            row = lax.broadcasted_iota(jnp.int32, (8, half), 0)
            packed = jnp.where(row == 0, numer_real, jnp.where(row == 1, numer_imag, jnp.where(row == 2, energy, 0.0)))
            sums[...] = packed + before[...]

    row_specs = [pl.BlockSpec((a.shape[0], block), lambda i, info: (0, i)) for a in flat]
    data_specs = [pl.BlockSpec((a.shape[0], half), lambda i, info: (0, info[1])) for a in flat]
    whole = lambda a: pl.BlockSpec(a.shape, lambda i, info: (0,) * a.ndim)
    return pl.pallas_call(
        body,
        out_shape=[
            jax.ShapeDtypeStruct((total_rows, half), jnp.float32),
            jax.ShapeDtypeStruct((8, half), jnp.float32),
        ],
        grid_spec=pltpu.PrefetchScalarGridSpec(
            num_scalar_prefetch=1,
            grid=(steps,),
            in_specs=row_specs + data_specs + [
                pl.BlockSpec(memory_space=pltpu.VMEM), whole(own_w), whole(sib_w), whole(earlier),
            ],
            out_specs=[
                pl.BlockSpec((total_rows, half), lambda i, info: (0, 0)),
                pl.BlockSpec((8, half), lambda i, info: (0, 0)),
            ],
            scratch_shapes=[pltpu.VMEM((total_rows, width), jnp.float32)],
        ),
        compiler_params=pltpu.CompilerParams(vmem_limit_bytes=20 * 2**20),
        cost_estimate=pl.CostEstimate(flops=1_000_000, bytes_accessed=100_000, transcendentals=0),
        name="product",
    )(info, *flat, *flat, surf, own_w, sib_w, earlier)


def subtract(info, groups, mults, own_w, sib_w, shares, total_shots):
    half = mults[0].shape[1]
    flat = []
    for group in groups:
        flat.extend(group if isinstance(group, tuple) else (group,))
    count = len(flat)

    def body(info, *refs):
        data = list(refs[:count])
        mult_refs = list(refs[count : count + len(mults)])
        own_ref, sib_ref = refs[count + len(mults) : count + len(mults) + 2]
        share_refs = refs[count + len(mults) + 2 : -3]
        out, gains, kept = refs[-3:]
        for k, share in enumerate(share_refs):
            kept[k] = share[...]
        here = lax.axis_index("grp")
        sums = kept[here]
        for place in range(1, 4):
            sums = sums + kept[(here + 4 - place) & 3]
        denom = sums[2:3] + ridge_share * total_shots
        gain_real = sums[0:1] / denom
        gain_imag = sums[1:2] / denom
        row = lax.broadcasted_iota(jnp.int32, (8, half), 0)
        gains[...] = jnp.where(row == 0, gain_real, jnp.where(row == 1, gain_imag, 0.0))
        sign = signs(64, half)
        lines = []
        for ref in mult_refs:
            lines.extend((ref, start) for start in range(0, ref.shape[0], 64))
        for index, group in enumerate(groups):
            if isinstance(group, tuple):
                seen = jnp.concatenate([data.pop(0)[...], data.pop(0)[...]], axis=0)
            else:
                seen = data.pop(0)[...]
            ref, start = lines[index]
            value = ref[start : start + 64, :]
            weight = all_weights(info, index * 4, 4, own_ref, sib_ref)
            term = weight * (gain_real * value + sign * gain_imag * flip4(value))
            term = term.astype(jnp.bfloat16).astype(jnp.float32)
            left = (seen.astype(jnp.float32) - term).astype(jnp.bfloat16)
            for slot in range(4):
                out[slot_chip(index * 4 + slot)] = left[slot * 16 : (slot + 1) * 16, :]

    whole = lambda a: pl.BlockSpec(a.shape, lambda i, info: (0,) * a.ndim)
    return pl.pallas_call(
        body,
        out_shape=[
            jax.ShapeDtypeStruct((CHIPS, 16, half), jnp.bfloat16),
            jax.ShapeDtypeStruct((8, half), jnp.float32),
        ],
        grid_spec=pltpu.PrefetchScalarGridSpec(
            num_scalar_prefetch=1,
            grid=(1,),
            in_specs=[pl.BlockSpec((a.shape[0], half), lambda i, info: (0, info[1])) for a in flat]
            + [whole(a) for a in (*mults, own_w, sib_w, *shares)],
            out_specs=[
                pl.BlockSpec((CHIPS, 16, half), lambda i, info: (0, 0, 0)),
                pl.BlockSpec((8, half), lambda i, info: (0, 0)),
            ],
            scratch_shapes=[pltpu.VMEM((4, 8, half), jnp.float32)],
        ),
        compiler_params=pltpu.CompilerParams(vmem_limit_bytes=24 * 2**20),
        cost_estimate=pl.CostEstimate(flops=4_000_000, bytes_accessed=2_000_000, transcendentals=0),
        name="subtract",
    )(info, *flat, *mults, own_w, sib_w, *shares)


def per_device(recorded, surface, receiver_map, live_traces):
    y, z, core = (lax.axis_index(a) for a in ("y", "z", "core"))
    nrec = recorded.shape[3]
    columns = surface.shape[3]
    info = jnp.stack([core, y * NZ + z]).astype(jnp.int32)

    mine, other = split_freqs(recorded)
    sib_live = swap(live_traces)
    block = jnp.concatenate([mine, swap(other)], axis=0)
    block, surface, sib_live = lax.optimization_barrier((block, surface, sib_live))
    sib_surface = swap(surface)

    up, down, right, left = (0, 1), (0, -1), (1, 0), (-1, 0)
    m2 = send(block, (0, -2), (-2, 0))
    m1 = send(block, down, left)
    p1 = send(block, up, right)
    low = stack_rows([block, p1, m1, m2])
    low, p1, m2, info, rmap4 = lax.optimization_barrier((low, p1, m2, info, receiver_map * 4))

    p5 = send(low, right, up)
    m5 = send(low, left, down)
    p2 = send(p1, up, right)
    m3 = send(m2, down, left)
    held = scatter_rows(info, rmap4, surface, sib_surface)
    p5, m5, p2, m3, held = lax.optimization_barrier((p5, m5, p2, m3, held))

    p6 = send(p5, right, up)
    m6 = send(m5, left, down)
    p3 = send(p2, up, right)
    m4 = send(m3, down, left)
    surf = pack_rows(held)
    p6, m6, p3, m4, surf = lax.optimization_barrier((p6, m6, p3, m4, surf))
    plus, m6 = choose([p2, p3, m3, m4], p6, m6)
    p7 = send(plus, right, up)
    m7 = send(m6, left, down)

    shots = live_traces.shape[0]
    own_w = live_traces.reshape(CHIPS, shots // CHIPS, columns)
    sib_w = sib_live.reshape(CHIPS, shots // CHIPS, columns)
    early = [low, p5, m5, p6, m6]
    none = jnp.zeros((8, 2 * columns), jnp.float32)
    mult1, sums1 = product(info, 0, early, surf, own_w, sib_w, none)
    p7, m7, sums1 = lax.optimization_barrier((p7, m7, sums1))
    p8 = send(p7[:32], right, up)
    m8 = send(m7[32:], left, down)
    middle, late = [p7, m7], [(p8, m8)]
    mult2, sums2 = product(info, 4 * len(early), middle, surf, own_w, sib_w, sums1)
    mult3, sums = product(info, 4 * len(early + middle), late, surf, own_w, sib_w, sums2)
    shares = [sums] + [lax.ppermute(sums, "grp", [(i, (i + k) % 4) for i in range(4)]) for k in (1, 2, 3)]
    total_shots = shots * lax.axis_size("grp")
    groups = early + middle + late
    out, gains = subtract(info, groups, [mult1, mult2, mult3], own_w, sib_w, shares, total_shots)

    back = lax.all_to_all(out, ("y", "z"), split_axis=0, concat_axis=0, tiled=True)
    back, gains = lax.optimization_barrier((back, gains))
    primaries, gains = assemble(back, swap(back), gains, swap(gains))
    return (primaries, gains)


def solution(mesh):
    fine = Mesh(mesh.devices.reshape(4, NY, NZ, 2), ("grp", "y", "z", "core"))
    every = ("grp", "y", "z", "core")
    return jax.shard_map(
        per_device,
        mesh=fine,
        in_specs=(P(None, None, every, None), P(None, None, None, RCV), P(), P("grp", RCV)),
        out_specs=(P(None, None, every, None), P(None, None, RCV)),
        check_vma=False,
    )
```

```python
import jax
import jax.numpy as jnp
from jax import lax
from jax.experimental import pallas as pl
from jax.experimental.pallas import tpu as pltpu
from jax.sharding import Mesh, PartitionSpec as P

ridge_share = 0.05
NY, NZ = 4, 8
CHIPS = NY * NZ
RCV = ("y", "z", "core")

LOW_Z = [(0, 0), (0, -1), (0, 1), (0, 2)]
HIGH_Z = [(0, -2), (0, -3), (0, 3), (0, 4)]
LOW_Y = [(0, 0), (-1, 0), (1, 0), (2, 0)]


def shift(blocks, dy, dz):
    return [(a + dy, b + dz) for a, b in blocks]


SLOTS = (
    LOW_Y + shift(LOW_Y, 0, -1) + shift(LOW_Y, 0, 1) + shift(LOW_Y, 0, -2) + shift(LOW_Y, 0, 2)
    + shift(LOW_Y, 0, -3) + shift(LOW_Y, 0, 3) + shift(LOW_Y[:2], 0, -4) + shift(LOW_Y[2:], 0, 4),
    LOW_Z + shift(LOW_Z, -1, 0) + shift(LOW_Z, 1, 0) + shift(LOW_Z, -2, 0) + HIGH_Z
    + shift(HIGH_Z, -1, 0) + shift(HIGH_Z, 1, 0) + shift(HIGH_Z[:2], -2, 0) + shift(HIGH_Z[2:], 2, 0),
)


def send(value, move1, move0):
    pairs = []
    for y in range(NY):
        for z in range(NZ):
            for core, move in enumerate((move0, move1)):
                if move is None:
                    continue
                to = ((y + move[0]) % NY * NZ + (z + move[1]) % NZ) * 2 + core
                pairs.append(((y * NZ + z) * 2 + core, to))
    return lax.ppermute(value, RCV, pairs)


def swap(value):
    return lax.ppermute(value, "core", [(0, 1), (1, 0)])


def flip4(value):
    rows, cols = value.shape
    return pltpu.roll(value.reshape(rows // 8, 8, cols), 4, 1).reshape(rows, cols)


def signs(rows, cols):
    row = lax.broadcasted_iota(jnp.int32, (rows, cols), 0)
    return jnp.where(row % 8 < 4, -1.0, 1.0).astype(jnp.float32)


def split_freqs(recorded):
    parts, freqs, shots, nrec = recorded.shape

    def body(rec, mine, other):
        first = lax.axis_index("core") == 0
        rows = [
            jnp.concatenate([rec[part, freq].astype(jnp.float32) for part in range(parts)], axis=0)
            for freq in range(freqs)
        ]
        mine[...] = jnp.where(first, rows[0], rows[1]).astype(jnp.bfloat16)
        other[...] = jnp.where(first, rows[1], rows[0]).astype(jnp.bfloat16)

    return pl.pallas_call(
        body,
        out_shape=[jax.ShapeDtypeStruct((parts * shots, nrec), jnp.bfloat16)] * 2,
        in_specs=[pl.BlockSpec(memory_space=pltpu.VMEM)],
        out_specs=[pl.BlockSpec(memory_space=pltpu.VMEM)] * 2,
        compiler_params=pltpu.CompilerParams(vmem_limit_bytes=16 * 2**20),
        name="split_freqs",
    )(recorded)


def assemble(back, got, gains, got_gains):
    chips, _, width = back.shape
    half = width // 2

    def body(back, got, gains, got_gains, out, out_gains):
        core = lax.axis_index("core")
        first = core == 0
        for chip in range(chips):
            mine = back[chip].astype(jnp.float32)[:8]
            other = got[chip].astype(jnp.float32)[8:]
            for freq, rows in enumerate((jnp.where(first, mine, other), jnp.where(first, other, mine))):
                for part in range(2):
                    out[part, freq, :, chip * width : (chip + 1) * width] = rows[part * 4 : part * 4 + 4].astype(
                        jnp.bfloat16
                    )
        mine = jnp.where(first, gains[:, :half], gains[:, half:])
        other = jnp.where(first, got_gains[:, :half], got_gains[:, half:])
        for freq, rows in enumerate((jnp.where(first, mine, other), jnp.where(first, other, mine))):
            for part in range(2):
                out_gains[part, freq : freq + 1, :] = rows[part : part + 1]

    return pl.pallas_call(
        body,
        out_shape=[
            jax.ShapeDtypeStruct((2, 2, 4, chips * width), jnp.bfloat16),
            jax.ShapeDtypeStruct((2, 2, half), jnp.float32),
        ],
        in_specs=[pl.BlockSpec(memory_space=pltpu.VMEM)] * 4,
        out_specs=[pl.BlockSpec(memory_space=pltpu.VMEM)] * 2,
        compiler_params=pltpu.CompilerParams(vmem_limit_bytes=16 * 2**20),
        name="assemble",
    )(back, got, gains, got_gains)


def scatter_rows(info, rmap4, surface, sibling):
    order, columns = surface.shape[2:]
    block = 2048
    unroll = 128
    steps = order // block

    def body(info, rmap, own, sib, held, stage):
        step = pl.program_id(0)
        first = info[0] == 0
        for part in range(2):
            mine = own[part, 0].astype(jnp.float32)
            other = sib[part, 0].astype(jnp.float32)
            stage[pl.ds(part * 2, block, stride=4), :] = jnp.where(first, mine, other)
            stage[pl.ds(part * 2 + 1, block, stride=4), :] = jnp.where(first, other, mine)

        def rows(g, carry):
            start = g * unroll
            to = [rmap[step * block + start + u] for u in range(unroll)]
            for some in range(0, unroll, 32):
                lines = [stage[pl.ds(pl.multiple_of((start + some + u) * 4, 4), 4), :] for u in range(32)]
                for u in range(32):
                    held[pl.ds(pl.multiple_of(to[some + u], 4), 4), :] = lines[u]
            return carry

        lax.fori_loop(0, block // unroll, rows, 0)

    spec = pl.BlockSpec((2, 1, block, columns), lambda i, info, rmap: (0, info[0], i, 0))
    return pl.pallas_call(
        body,
        out_shape=pltpu.VMEM((order * 4, columns), jnp.float32),
        grid_spec=pltpu.PrefetchScalarGridSpec(
            num_scalar_prefetch=2,
            grid=(steps,),
            in_specs=[spec, spec],
            out_specs=pl.BlockSpec(memory_space=pltpu.VMEM),
            scratch_shapes=[pltpu.VMEM((block * 4, columns), jnp.float32)],
        ),
        compiler_params=pltpu.CompilerParams(vmem_limit_bytes=36 * 2**20),
        cost_estimate=pl.CostEstimate(flops=1_000_000, bytes_accessed=100_000, transcendentals=0),
        name="scatter_rows",
    )(info, rmap4, surface, sibling)


def pack_rows(held):
    rows, columns = held.shape
    order = rows // 4
    block = 1024

    def body(held, out):
        def some(step, carry):
            top = pl.multiple_of(step * block, block)
            for plane in range(4):
                got = held[pl.ds(top * 4 + plane, block, stride=4), :]
                out[pl.ds(top, block), plane * columns : (plane + 1) * columns] = got.astype(jnp.bfloat16)
            return carry

        lax.fori_loop(0, order // block, some, 0)

    return pl.pallas_call(
        body,
        out_shape=pltpu.VMEM((order, 4 * columns), jnp.bfloat16),
        in_specs=[pl.BlockSpec(memory_space=pltpu.VMEM)],
        out_specs=pl.BlockSpec(memory_space=pltpu.VMEM),
        compiler_params=pltpu.CompilerParams(vmem_limit_bytes=6 * 2**20),
        cost_estimate=pl.CostEstimate(flops=1_000_000, bytes_accessed=100_000, transcendentals=0),
        name="pack_rows",
    )(held)


def stack_rows(pieces):
    tall, width = pieces[0].shape

    def body(*refs):
        for index, piece in enumerate(refs[:-1]):
            refs[-1][index * tall : (index + 1) * tall, :] = piece[...]

    return pl.pallas_call(
        body,
        out_shape=jax.ShapeDtypeStruct((tall * len(pieces), width), jnp.bfloat16),
        in_specs=[pl.BlockSpec(memory_space=pltpu.VMEM)] * len(pieces),
        out_specs=pl.BlockSpec(memory_space=pltpu.VMEM),
        compiler_params=pltpu.CompilerParams(vmem_limit_bytes=10 * 2**20),
        cost_estimate=pl.CostEstimate(flops=1_000_000, bytes_accessed=100_000, transcendentals=0),
        name="stack_rows",
    )(*pieces)


def choose(pieces, plus, minus):
    rows, width = plus.shape
    block = 1024
    tall = rows // len(pieces)

    def body(*refs):
        piece_refs, (plus_ref, minus_ref, out_plus, out_minus) = refs[:-4], refs[-4:]
        second = lax.axis_index("core") == 1

        def some(step, carry):
            cols = pl.ds(pl.multiple_of(step * block, block), block)
            for index, piece in enumerate(piece_refs):
                line = pl.ds(index * tall, tall)
                value = piece[:, cols]
                out_plus[line, cols] = jnp.where(second, value, plus_ref[line, cols])
                out_minus[line, cols] = jnp.where(second, value, minus_ref[line, cols])
            return carry

        lax.fori_loop(0, width // block, some, 0)

    return pl.pallas_call(
        body,
        out_shape=[jax.ShapeDtypeStruct((rows, width), jnp.bfloat16)] * 2,
        in_specs=[pl.BlockSpec(memory_space=pltpu.VMEM)] * (len(pieces) + 2),
        out_specs=[pl.BlockSpec(memory_space=pltpu.VMEM)] * 2,
        compiler_params=pltpu.CompilerParams(vmem_limit_bytes=10 * 2**20),
        cost_estimate=pl.CostEstimate(flops=1_000_000, bytes_accessed=100_000, transcendentals=0),
        name="choose",
    )(*pieces, plus, minus)


def slot_chip(slot):
    core, y, z = (lax.axis_index(a) for a in ("core", "y", "z"))
    dy, dz = (jnp.where(core == 0, a, b) for a, b in zip(SLOTS[0][slot], SLOTS[1][slot]))
    return ((y + dy + NY) & (NY - 1)) * NZ + ((z + dz + NZ) & (NZ - 1))


def weights_of(info, slot, own_w, sib_w):
    first = info[0] == 0
    chip = slot_chip(slot)
    mine = own_w[chip].astype(jnp.float32)
    other = sib_w[chip].astype(jnp.float32)
    natural = jnp.concatenate([jnp.where(first, mine, other), jnp.where(first, other, mine)], axis=1)
    rolled = pltpu.roll(natural, 4, 0)
    low = lax.broadcasted_iota(jnp.int32, natural.shape, 0) < 4
    core0 = jnp.where(low, natural, rolled)
    core1 = jnp.where(low, rolled, natural)
    return jnp.where(first, core0, core1), jnp.where(first, core1, core0)


def all_weights(info, slot0, slots, own_w, sib_w):
    tiles = []
    for slot in range(slots):
        tiles.extend(weights_of(info, slot0 + slot, own_w, sib_w))
    return jnp.concatenate(tiles, axis=0)


def product(info, slot0, groups, surf, own_w, sib_w, earlier):
    order, width = surf.shape
    half = width // 2
    block = (8192, 4096)[len(groups) - 1] if len(groups) <= 2 else 2048
    steps = order // block
    flat = []
    for group in groups:
        flat.extend(group if isinstance(group, tuple) else (group,))
    count = len(flat)
    total_rows = 64 * len(groups)
    slots = total_rows // 16

    def join(refs):
        refs = list(refs)
        parts = []
        for group in groups:
            if isinstance(group, tuple):
                parts.extend((refs.pop(0)[...], refs.pop(0)[...]))
            else:
                parts.append(refs.pop(0)[...])
        return jnp.concatenate(parts, axis=0)

    def body(info, *refs):
        rows = refs[:count]
        data = refs[count : 2 * count]
        surf_ref, own_ref, sib_ref, before, mult, sums, total = refs[2 * count :]
        step = pl.program_id(0)

        @pl.when(step == 0)
        def _():
            total[...] = jnp.zeros_like(total)

        surf = surf_ref[pl.ds(pl.multiple_of(step * block, block), block), :]
        total[...] += jnp.dot(join(rows), surf, preferred_element_type=jnp.float32)

        @pl.when(step == steps - 1)
        def _():
            sign = signs(total_rows, half)
            value = total[:, :half] + sign * flip4(total[:, half:])
            mult[...] = value
            seen = join(data).astype(jnp.float32)
            weight = all_weights(info, slot0, slots, own_ref, sib_ref)
            scaled = weight * value

            def add(terms):
                return jnp.sum(terms, axis=0, keepdims=True)

            numer_real = add(scaled * seen)
            numer_imag = add(scaled * (-sign * flip4(seen)))
            energy = add(scaled * value)
            row = lax.broadcasted_iota(jnp.int32, (8, half), 0)
            packed = jnp.where(row == 0, numer_real, jnp.where(row == 1, numer_imag, jnp.where(row == 2, energy, 0.0)))
            sums[...] = packed + before[...]

    row_specs = [pl.BlockSpec((a.shape[0], block), lambda i, info: (0, i)) for a in flat]
    data_specs = [pl.BlockSpec((a.shape[0], half), lambda i, info: (0, info[1])) for a in flat]
    whole = lambda a: pl.BlockSpec(a.shape, lambda i, info: (0,) * a.ndim)
    return pl.pallas_call(
        body,
        out_shape=[
            jax.ShapeDtypeStruct((total_rows, half), jnp.float32),
            jax.ShapeDtypeStruct((8, half), jnp.float32),
        ],
        grid_spec=pltpu.PrefetchScalarGridSpec(
            num_scalar_prefetch=1,
            grid=(steps,),
            in_specs=row_specs + data_specs + [
                pl.BlockSpec(memory_space=pltpu.VMEM), whole(own_w), whole(sib_w), whole(earlier),
            ],
            out_specs=[
                pl.BlockSpec((total_rows, half), lambda i, info: (0, 0)),
                pl.BlockSpec((8, half), lambda i, info: (0, 0)),
            ],
            scratch_shapes=[pltpu.VMEM((total_rows, width), jnp.float32)],
        ),
        compiler_params=pltpu.CompilerParams(vmem_limit_bytes=20 * 2**20),
        cost_estimate=pl.CostEstimate(flops=1_000_000, bytes_accessed=100_000, transcendentals=0),
        name="product",
    )(info, *flat, *flat, surf, own_w, sib_w, earlier)


def subtract(info, groups, mults, own_w, sib_w, shares, total_shots):
    half = mults[0].shape[1]
    flat = []
    for group in groups:
        flat.extend(group if isinstance(group, tuple) else (group,))
    count = len(flat)

    def body(info, *refs):
        data = list(refs[:count])
        mult_refs = list(refs[count : count + len(mults)])
        own_ref, sib_ref = refs[count + len(mults) : count + len(mults) + 2]
        share_refs = refs[count + len(mults) + 2 : -3]
        out, gains, kept = refs[-3:]
        for k, share in enumerate(share_refs):
            kept[k] = share[...]
        here = lax.axis_index("grp")
        sums = kept[here]
        for place in range(1, 4):
            sums = sums + kept[(here + 4 - place) & 3]
        denom = sums[2:3] + ridge_share * total_shots
        gain_real = sums[0:1] / denom
        gain_imag = sums[1:2] / denom
        row = lax.broadcasted_iota(jnp.int32, (8, half), 0)
        gains[...] = jnp.where(row == 0, gain_real, jnp.where(row == 1, gain_imag, 0.0))
        sign = signs(64, half)
        lines = []
        for ref in mult_refs:
            lines.extend((ref, start) for start in range(0, ref.shape[0], 64))
        for index, group in enumerate(groups):
            if isinstance(group, tuple):
                seen = jnp.concatenate([data.pop(0)[...], data.pop(0)[...]], axis=0)
            else:
                seen = data.pop(0)[...]
            ref, start = lines[index]
            value = ref[start : start + 64, :]
            weight = all_weights(info, index * 4, 4, own_ref, sib_ref)
            term = weight * (gain_real * value + sign * gain_imag * flip4(value))
            term = term.astype(jnp.bfloat16).astype(jnp.float32)
            left = (seen.astype(jnp.float32) - term).astype(jnp.bfloat16)
            for slot in range(4):
                out[slot_chip(index * 4 + slot)] = left[slot * 16 : (slot + 1) * 16, :]

    whole = lambda a: pl.BlockSpec(a.shape, lambda i, info: (0,) * a.ndim)
    return pl.pallas_call(
        body,
        out_shape=[
            jax.ShapeDtypeStruct((CHIPS, 16, half), jnp.bfloat16),
            jax.ShapeDtypeStruct((8, half), jnp.float32),
        ],
        grid_spec=pltpu.PrefetchScalarGridSpec(
            num_scalar_prefetch=1,
            grid=(1,),
            in_specs=[pl.BlockSpec((a.shape[0], half), lambda i, info: (0, info[1])) for a in flat]
            + [whole(a) for a in (*mults, own_w, sib_w, *shares)],
            out_specs=[
                pl.BlockSpec((CHIPS, 16, half), lambda i, info: (0, 0, 0)),
                pl.BlockSpec((8, half), lambda i, info: (0, 0)),
            ],
            scratch_shapes=[pltpu.VMEM((4, 8, half), jnp.float32)],
        ),
        compiler_params=pltpu.CompilerParams(vmem_limit_bytes=24 * 2**20),
        cost_estimate=pl.CostEstimate(flops=4_000_000, bytes_accessed=2_000_000, transcendentals=0),
        name="subtract",
    )(info, *flat, *mults, own_w, sib_w, *shares)


def per_device(recorded, surface, receiver_map, live_traces):
    y, z, core = (lax.axis_index(a) for a in ("y", "z", "core"))
    nrec = recorded.shape[3]
    columns = surface.shape[3]
    info = jnp.stack([core, y * NZ + z]).astype(jnp.int32)

    mine, other = split_freqs(recorded)
    sib_live = swap(live_traces)
    block = jnp.concatenate([mine, swap(other)], axis=0)
    block, surface, sib_live = lax.optimization_barrier((block, surface, sib_live))
    sib_surface = swap(surface)

    up, down, right, left = (0, 1), (0, -1), (1, 0), (-1, 0)
    m2 = send(block, (0, -2), (-2, 0))
    m1 = send(block, down, left)
    p1 = send(block, up, right)
    low = stack_rows([block, p1, m1, m2])
    low, p1, m2, info, rmap4 = lax.optimization_barrier((low, p1, m2, info, receiver_map * 4))

    p5 = send(low, right, up)
    m5 = send(low, left, down)
    p2 = send(p1, up, right)
    m3 = send(m2, down, left)
    held = scatter_rows(info, rmap4, surface, sib_surface)
    p5, m5, p2, m3, held = lax.optimization_barrier((p5, m5, p2, m3, held))

    p6 = send(p5, right, up)
    m6 = send(m5, left, down)
    p3 = send(p2, up, right)
    m4 = send(m3, down, left)
    surf = pack_rows(held)
    p6, m6, p3, m4, surf = lax.optimization_barrier((p6, m6, p3, m4, surf))
    plus, m6 = choose([p2, p3, m3, m4], p6, m6)
    p7 = send(plus, right, up)
    m7 = send(m6, left, down)

    shots = live_traces.shape[0]
    own_w = live_traces.reshape(CHIPS, shots // CHIPS, columns)
    sib_w = sib_live.reshape(CHIPS, shots // CHIPS, columns)
    early = [low, p5, m5, p6, m6]
    none = jnp.zeros((8, 2 * columns), jnp.float32)
    mult1, sums1 = product(info, 0, early, surf, own_w, sib_w, none)
    p7, m7, sums1 = lax.optimization_barrier((p7, m7, sums1))
    p8 = send(p7[:32], right, up)
    m8 = send(m7[32:], left, down)
    middle, late = [p7, m7], [(p8, m8)]
    mult2, sums2 = product(info, 4 * len(early), middle, surf, own_w, sib_w, sums1)
    mult3, sums = product(info, 4 * len(early + middle), late, surf, own_w, sib_w, sums2)
    shares = [sums] + [lax.ppermute(sums, "grp", [(i, (i + k) % 4) for i in range(4)]) for k in (1, 2, 3)]
    total_shots = shots * lax.axis_size("grp")
    groups = early + middle + late
    out, gains = subtract(info, groups, [mult1, mult2, mult3], own_w, sib_w, shares, total_shots)

    back = lax.all_to_all(out, ("y", "z"), split_axis=0, concat_axis=0, tiled=True)
    back, gains = lax.optimization_barrier((back, gains))
    primaries, gains = assemble(back, swap(back), gains, swap(gains))
    return (primaries, gains)


def solution(mesh):
    fine = Mesh(mesh.devices.reshape(4, NY, NZ, 2), ("grp", "y", "z", "core"))
    every = ("grp", "y", "z", "core")
    return jax.shard_map(
        per_device,
        mesh=fine,
        in_specs=(P(None, None, every, None), P(None, None, None, RCV), P(), P("grp", RCV)),
        out_specs=(P(None, None, every, None), P(None, None, RCV)),
        check_vma=False,
    )
```
